256 devices in a mesh: lat: 8 (over x, y_lo), lon: 32 (over y_hi, z, core).
Axes of the slice: x: 4, y: 4 (y_hi: 2, y_lo: 2; y = y_hi * 2 + y_lo), z: 8, core: 2. Of those that a mesh axis runs over, the one named last changes fastest.
Arguments:
- fields: bfloat16 [2, 192, 384, 192], P(None, 'lat', 'lon'), may hold values from -6 to 6
- upstream: bfloat16 [2, 192, 384, 192], P(None, 'lat', 'lon'), may hold values from -6 to 6
- bias_f: float32 [1, 32, 6, 23, 144], P(None, 'lat'), may hold values from -4 to 260
- bias_c: float32 [1, 16, 12, 23, 144], P(None, 'lat'), may hold values from -4 to 260
- w_qkv_f: bfloat16 [192, 576], replicated, may hold values from -0.4375 to 0.4375
- w_proj_f: bfloat16 [192, 192], replicated, may hold values from -0.4375 to 0.4375
- w_merge: bfloat16 [768, 384], replicated, may hold values from -0.21875 to 0.21875
- w_qkv_c: bfloat16 [384, 1152], replicated, may hold values from -0.3125 to 0.3125
- w_proj_c: bfloat16 [384, 384], replicated, may hold values from -0.3125 to 0.3125
- w_split: bfloat16 [384, 768], replicated, may hold values from -0.3125 to 0.3125
Outputs:
- result: bfloat16 [2, 192, 384, 192], P(None, 'lat', 'lon')
- grad_fields: bfloat16 [2, 192, 384, 192], P(None, 'lat', 'lon')
- grad_bias_f: float32 [1, 32, 6, 23, 144], P(None, 'lat')
- grad_bias_c: float32 [1, 16, 12, 23, 144], P(None, 'lat')
The draws below stay inside these ranges and needn't reach their ends.
All inputs are finite; a program needn't handle non-finite values.
Results may differ from the reference program's by a relative error of at most 0.04.
Values may be sent and summed in bfloat16 or wider, within the bound.
No kernel may reach another device: no remote copies, remote signals or barrier semaphores. Data moves between devices by JAX's collectives and lax.ppermute only.
A program may use at most 192 MiB of HBM per device.

```python
import math
import jax
import jax.numpy as jnp
from jax import lax

C = 192
HEADS = 6
Z = 2
WIN_Z = 2
WIN_LAT = 6
WIN_LON = 12
NLAT = 192
NLON = 384
ZWIN = 1
LATWIN_F = 32
LATWIN_C = 16
N_LAT = 8
N_LON = 32


def draw_bias_f(key, part):
    key = jax.random.fold_in(key, 11)
    shape = (ZWIN, LATWIN_F, HEADS, 2 * WIN_LON - 1, (WIN_Z * WIN_LAT) ** 2)
    return jnp.clip(jax.random.normal(jax.random.fold_in(key, 1), shape, jnp.float32), -4.0, 4.0)


def draw_bias_c(key, part):
    key = jax.random.fold_in(key, 23)
    shape = (ZWIN, LATWIN_C, 2 * HEADS, 2 * WIN_LON - 1, (WIN_Z * WIN_LAT) ** 2)
    return jnp.clip(jax.random.normal(jax.random.fold_in(key, 1), shape, jnp.float32), -4.0, 4.0)


def shard_levels(own_key, dims, shards, least, top_value):
    loudness = 1.0
    for position, shards_of in shards:
        steps = jax.random.uniform(jax.random.fold_in(jax.random.fold_in(own_key, 6), position), (shards_of,), jnp.float32, least / len(shards), top_value / len(shards))
        loudness = loudness * jnp.repeat(jnp.exp(steps), dims[position] // shards_of).reshape((-1,) + (1,) * (len(dims) - 1 - position))
    return loudness


def normal_values(key, shape, deviation, most, split=(), kind=jnp.bfloat16):
    array = deviation * jax.random.normal(key, shape, jnp.float32)
    if split:
        array = array * shard_levels(key, shape, split, -0.22, 0.18)
    return jnp.clip(array, -most, most).astype(kind)


def setup_inputs(seed: int = 0) -> dict:
    key_list = jax.random.split(jax.random.key(seed), 11)
    fields = normal_values(key_list[0], (Z, NLAT, NLON, C), 1.0, 6.0, ((1, 8), (2, 32)))
    upstream = normal_values(key_list[1], (Z, NLAT, NLON, C), 1.0, 6.0, ((1, 8), (2, 32)))
    bias_f = draw_bias_f(jax.random.fold_in(key_list[10], 71), 0)
    bias_c = draw_bias_c(jax.random.fold_in(key_list[10], 71), 0)
    w_qkv_f = normal_values(key_list[4], (C, 3 * C), C ** -0.5, 0.4375)
    w_proj_f = normal_values(key_list[5], (C, C), C ** -0.5, 0.4375)
    w_merge = normal_values(key_list[6], (4 * C, 2 * C), (4 * C) ** -0.5, 0.21875)
    w_qkv_c = normal_values(key_list[7], (2 * C, 6 * C), (2 * C) ** -0.5, 0.3125)
    w_proj_c = normal_values(key_list[8], (2 * C, 2 * C), (2 * C) ** -0.5, 0.3125)
    w_split = normal_values(key_list[9], (2 * C, 4 * C), (2 * C) ** -0.5, 0.3125)
    return {"fields": fields, "upstream": upstream, "bias_f": bias_f, "bias_c": bias_c, "w_qkv_f": w_qkv_f, "w_proj_f": w_proj_f, "w_merge": w_merge, "w_qkv_c": w_qkv_c, "w_proj_c": w_proj_c, "w_split": w_split}


EPS = 1e-05
MASKED = -1000000000.0

def layer_norm(values):
    values = values.astype(jnp.float32)
    centred = values - lax.optimization_barrier(jnp.mean(values, axis=-1, keepdims=True))
    spread = lax.optimization_barrier(jnp.mean(centred * centred, axis=-1, keepdims=True))
    return centred * lax.rsqrt(spread + EPS)

def to_windows(values):
    levels, lat_rows, lon_cols, features = values.shape
    values = values.reshape(levels // WIN_Z, WIN_Z, lat_rows // WIN_LAT, WIN_LAT, lon_cols // WIN_LON, WIN_LON, features)
    values = values.transpose(0, 2, 4, 1, 3, 5, 6)
    return values.reshape(levels // WIN_Z, lat_rows // WIN_LAT, lon_cols // WIN_LON, WIN_Z * WIN_LAT * WIN_LON, features)

def from_windows(values):
    zwin_count, lat_windows, lon_windows, tokens, features = values.shape
    values = values.reshape(zwin_count, lat_windows, lon_windows, WIN_Z, WIN_LAT, WIN_LON, features)
    values = values.transpose(0, 3, 1, 4, 2, 5, 6)
    return values.reshape(zwin_count * WIN_Z, lat_windows * WIN_LAT, lon_windows * WIN_LON, features)

def expand_bias(bias_table):
    zwin_count, lat_windows, head_count = bias_table.shape[:3]
    positions = jnp.arange(WIN_LON)
    relative = jnp.arange(2 * WIN_LON - 1)
    select = (positions[:, None] - positions[None, :] + WIN_LON - 1 == relative[:, None, None]).astype(jnp.float32)
    expanded = jnp.einsum('abhrp,rij->abhpij', bias_table, select, precision=lax.Precision.HIGHEST)
    expanded = expanded.reshape(zwin_count, lat_windows, head_count, WIN_Z, WIN_LAT, WIN_Z, WIN_LAT, WIN_LON, WIN_LON)
    expanded = expanded.transpose(0, 1, 2, 3, 4, 7, 5, 6, 8)
    tokens = WIN_Z * WIN_LAT * WIN_LON
    return expanded.reshape(zwin_count, lat_windows, head_count, tokens, tokens)

def attend(queries, keys_in, values, bias_total, head_count):
    head_size = queries.shape[-1] // head_count
    shaped_q = queries.reshape(queries.shape[:-1] + (head_count, head_size))
    shaped_k = keys_in.reshape(keys_in.shape[:-1] + (head_count, head_size))
    shaped_v = values.reshape(values.shape[:-1] + (head_count, head_size))
    scores = jnp.einsum('...qhd,...khd->...hqk', shaped_q, shaped_k) / math.sqrt(head_size) + bias_total
    highest = lax.stop_gradient(lax.optimization_barrier(jnp.max(scores, axis=-1, keepdims=True)))
    weights = jnp.exp(scores - highest)
    weights = weights / lax.optimization_barrier(jnp.sum(weights, axis=-1, keepdims=True))
    blended = jnp.einsum('...hqk,...khd->...qhd', weights, shaped_v)
    return blended.reshape(queries.shape)

def fine_piece(rolled, bias_table, w_qkv_f, w_proj_f, first_row, total_rows):
    levels, lat_rows, lon_cols, features = rolled.shape
    head_count = bias_table.shape[2]
    normed = layer_norm(rolled).astype(jnp.bfloat16)
    projected = to_windows(jnp.dot(normed, w_qkv_f, preferred_element_type=jnp.float32))
    level_wrap = (jnp.arange(levels, dtype=jnp.int32) >= levels - WIN_Z // 2).astype(jnp.int32)
    row_wrap = (first_row + jnp.arange(lat_rows, dtype=jnp.int32) >= total_rows - WIN_LAT // 2).astype(jnp.int32)
    wrap_flags = 2 * level_wrap[:, None, None] + row_wrap[None, :, None] + jnp.zeros((1, 1, lon_cols), jnp.int32)
    wrap_flags = to_windows(wrap_flags[..., None])[..., 0]
    masking = jnp.where(wrap_flags[..., :, None] == wrap_flags[..., None, :], 0.0, MASKED).astype(jnp.float32)
    bias_total = expand_bias(bias_table)[:, :, None] + masking[:, :, :, None]
    attended = attend(projected[..., :features], projected[..., features:2 * features], projected[..., 2 * features:], bias_total, head_count)
    attended = from_windows(attended).astype(jnp.bfloat16)
    return (rolled + jnp.dot(attended, w_proj_f, preferred_element_type=jnp.float32)).astype(jnp.bfloat16)

def merge_piece(fine, w_merge):
    levels, lat_rows, lon_cols, features = fine.shape
    quartets = fine.reshape(levels, lat_rows // 2, 2, lon_cols // 2, 2, features).transpose(0, 1, 3, 2, 4, 5)
    quartets = quartets.reshape(levels, lat_rows // 2, lon_cols // 2, 4 * features)
    merged = layer_norm(quartets).astype(jnp.bfloat16)
    return jnp.dot(merged, w_merge, preferred_element_type=jnp.float32).astype(jnp.bfloat16)

def coarse_attend(queries, keys_values, bias_table, offset):
    levels, lat_rows, query_cols, features = queries.shape
    head_count = bias_table.shape[2]
    zwin_count = levels // WIN_Z
    lat_windows = lat_rows // WIN_LAT
    grouped = queries.reshape(zwin_count, WIN_Z, lat_windows, WIN_LAT, query_cols, features).transpose(0, 2, 1, 3, 4, 5)
    grouped = grouped.reshape(zwin_count, lat_windows, WIN_Z * WIN_LAT * query_cols, features)
    windows = to_windows(keys_values)[:, :, 0]
    tokens = WIN_Z * WIN_LAT * WIN_LON
    expanded = expand_bias(bias_table).reshape(zwin_count, lat_windows, head_count, WIN_Z, WIN_LAT, WIN_LON, tokens)
    rows_used = lax.dynamic_slice_in_dim(expanded, offset, query_cols, 5)
    rows_used = rows_used.reshape(zwin_count, lat_windows, head_count, WIN_Z * WIN_LAT * query_cols, tokens)
    attended = attend(grouped, windows[..., :features], windows[..., features:], rows_used, head_count)
    attended = attended.reshape(zwin_count, lat_windows, WIN_Z, WIN_LAT, query_cols, features).transpose(0, 2, 1, 3, 4, 5)
    return attended.reshape(levels, lat_rows, query_cols, features)

def finish(coarse_in, attended, w_proj_c):
    return (coarse_in + jnp.dot(attended.astype(jnp.bfloat16), w_proj_c, preferred_element_type=jnp.float32)).astype(jnp.bfloat16)

def split_piece(coarse_out, fine, w_split):
    normed = layer_norm(coarse_out).astype(jnp.bfloat16)
    widened = jnp.dot(normed, w_split, preferred_element_type=jnp.float32)
    levels, lat_rows, lon_cols, columns = widened.shape
    features = columns // 4
    widened = widened.reshape(levels, lat_rows, lon_cols, 2, 2, features).transpose(0, 1, 3, 2, 4, 5)
    widened = widened.reshape(levels, 2 * lat_rows, 2 * lon_cols, features)
    return (fine + widened).astype(jnp.bfloat16)

def coarse_group(section, bias_table, w_qkv_c, w_proj_c):
    features = section.shape[-1]
    normed = layer_norm(section).astype(jnp.bfloat16)
    projected = jnp.dot(normed, w_qkv_c, preferred_element_type=jnp.float32)
    attended = coarse_attend(projected[..., :features], projected[..., features:], bias_table, 0)
    return finish(section, attended, w_proj_c)

def fine_all(rolled, bias_f, w_qkv_f, w_proj_f):
    levels, total_rows, total_cols, features = rolled.shape
    lat_rows = total_rows // N_LAT
    lon_cols = total_cols // N_LON
    per_lat = bias_f.shape[1] // N_LAT
    blocks = rolled.reshape(levels, N_LAT, lat_rows, N_LON, lon_cols, features).transpose(1, 3, 0, 2, 4, 5)
    blocks = blocks.reshape(N_LAT * N_LON, levels, lat_rows, lon_cols, features)

    def one_block(section, block_index, table_all):
        lat_index = block_index // N_LON
        bias_table = lax.dynamic_slice_in_dim(table_all, lat_index * per_lat, per_lat, 1)
        return fine_piece(section, bias_table, w_qkv_f, w_proj_f, lat_index * lat_rows, total_rows)
    mapped_step = jax.checkpoint(one_block)

    def apply_block(item_pair):
        return mapped_step(item_pair[0], item_pair[1], bias_f)
    blended = lax.map(apply_block, (blocks, jnp.arange(N_LAT * N_LON, dtype=jnp.int32)))
    blended = blended.reshape(N_LAT, N_LON, levels, lat_rows, lon_cols, features).transpose(2, 0, 3, 1, 4, 5)
    return blended.reshape(levels, total_rows, total_cols, features)

def coarse_all(coarse_in, bias_c, w_qkv_c, w_proj_c):
    levels, total_rows, total_cols, features = coarse_in.shape
    lat_rows = total_rows // N_LAT
    pair_cols = 2 * (total_cols // N_LON)
    group_count = N_LON // 2
    per_lat = bias_c.shape[1] // N_LAT
    blocks = coarse_in.reshape(levels, N_LAT, lat_rows, group_count, pair_cols, features).transpose(1, 3, 0, 2, 4, 5)
    blocks = blocks.reshape(N_LAT * group_count, levels, lat_rows, pair_cols, features)

    def one_group(section, block_index, table_all):
        lat_index = block_index // group_count
        bias_table = lax.dynamic_slice_in_dim(table_all, lat_index * per_lat, per_lat, 1)
        return coarse_group(section, bias_table, w_qkv_c, w_proj_c)
    mapped_step = jax.checkpoint(one_group)

    def apply_group(item_pair):
        return mapped_step(item_pair[0], item_pair[1], bias_c)
    blended = lax.map(apply_group, (blocks, jnp.arange(N_LAT * group_count, dtype=jnp.int32)))
    blended = blended.reshape(N_LAT, group_count, levels, lat_rows, pair_cols, features).transpose(2, 0, 3, 1, 4, 5)
    return blended.reshape(levels, total_rows, total_cols, features)

def reference(fields, upstream, bias_f, bias_c, w_qkv_f, w_proj_f, w_merge, w_qkv_c, w_proj_c, w_split):
    shifts = (WIN_Z // 2, WIN_LAT // 2, WIN_LON // 2)

    def forward(field_in, table_f, table_c):
        rolled = jnp.roll(field_in, (-shifts[0], -shifts[1], -shifts[2]), axis=(0, 1, 2))
        fine = jnp.roll(fine_all(rolled, table_f, w_qkv_f, w_proj_f), shifts, axis=(0, 1, 2))
        coarse_out = coarse_all(merge_piece(fine, w_merge), table_c, w_qkv_c, w_proj_c)
        return split_piece(coarse_out, fine, w_split)
    result, pullback = jax.vjp(forward, fields, bias_f, bias_c)
    grad_fields, grad_bias_f, grad_bias_c = pullback(upstream)
    return (result, grad_fields, grad_bias_f, grad_bias_c)
```

```python
import math

import jax
import jax.numpy as jnp
import numpy as np
from jax import lax
from jax.experimental import pallas as pl
from jax.experimental.pallas import tpu as pltpu
from jax.sharding import PartitionSpec as P

WIN_Z = 2
WIN_LAT = 6
WIN_LON = 12
ROWS = WIN_Z * WIN_LAT
TOK = ROWS * WIN_LON
HALF = TOK // 2
REL = 2 * WIN_LON - 1
WIDE = REL * ROWS
EPS = 1e-05
MASKED = -1000000000.0
HEAD = 32
SCALE = 1.0 / math.sqrt(HEAD)
LAT = 24
LON = 12
NWF = LAT // WIN_LAT
NWC = LAT // 2 // WIN_LAT
BF = jnp.bfloat16
F32 = jnp.float32
ROW_PIECE, COL_PIECE, CORNER = 48, 288, 48
VMEM = 16 * 1024 * 1024
TABLE = 24 + 3
LANES = 384
PACKED = 24 * TABLE + 8
BATCH = 4


def natural_order():
    return [(z, i, j) for z in range(2) for j in range(LON) for i in range(LAT)]


def window_order():
    return [
        (z, WIN_LAT * w + l, n)
        for w in range(NWF)
        for n in range(LON)
        for z in range(2)
        for l in range(WIN_LAT)
    ]


def quartet_order():
    return [
        (z, 2 * (WIN_LAT * w + l) + di, 2 * n + dj)
        for di in range(2)
        for dj in range(2)
        for w in range(NWC)
        for n in range(LON // 2)
        for z in range(2)
        for l in range(WIN_LAT)
    ]


def one_hot(rows, columns):
    table = np.zeros((len(rows), columns), np.float32)
    for row, column in enumerate(rows):
        if column is not None:
            table[row, column] = 1.0
    return jnp.asarray(table, BF)


def forward_pieces():
    row = [(z, i, j) for z in range(2) for i in range(3) for j in range(6, LON)]
    col = [(z, i, j) for z in range(2) for i in range(LAT) for j in range(6)]
    corner = [(z, i, j) for z in range(2) for i in range(3) for j in range(6)]
    return row, col, corner


def back_pieces():
    row = [(z, i, j) for z in range(2) for i in range(LAT - 3, LAT) for j in range(6)]
    col = [cell for cell in window_order() if cell[2] >= 6]
    corner = [(z, i, j) for z in range(2) for i in range(LAT - 3, LAT) for j in range(6, LON)]
    return row, col, corner


def padded_pieces(pieces):
    sizes = (ROW_PIECE, COL_PIECE, CORNER)
    return [cells + [None] * (size - len(cells)) for cells, size in zip(pieces, sizes)]


def send_table(own_order, pieces):
    place = {cell: index for index, cell in enumerate(own_order)}
    cells = sum(padded_pieces(pieces), [])
    return one_hot([None if cell is None else place[cell] for cell in cells], len(own_order))


def gather_table(own_order, pieces, wanted):
    tables = [{cell: index for index, cell in enumerate(own_order)}]
    starts = [0]
    for cells in pieces:
        tables.append({cell: index for index, cell in enumerate(cells)})
    starts = [0, len(own_order), len(own_order) + ROW_PIECE, len(own_order) + ROW_PIECE + COL_PIECE]
    total = len(own_order) + ROW_PIECE + COL_PIECE + CORNER
    rows = []
    for entry in wanted:
        rows.append(None if entry is None else starts[entry[0]] + tables[entry[0]][entry[1]])
    return one_hot(rows, total)


def window_start(w):
    return (WIN_LAT * w + WIN_LAT // 2) // 8 * 8 if w < NWF - 1 else LAT - 8


def window_table():
    rows = []
    for w in range(NWF):
        offset = WIN_LAT * w + WIN_LAT // 2 - window_start(w)
        for n in range(LON):
            for z in range(2):
                for l in range(WIN_LAT):
                    rows.append(((1 - z) * LON + n) * 16 + offset + l)
    return one_hot(rows, 2 * LON * 16)


def last_window_table():
    place = {cell: index for index, cell in enumerate(window_order()[-TOK:])}
    row, _, corner = padded_pieces(back_pieces())
    return one_hot([None if cell is None else place[cell] for cell in row + corner], TOK)


def rolled_from(cells):
    wanted = []
    for z, i, j in cells:
        z, i, j = 1 - z, i + 3, j + 6
        kind = (1 if i >= LAT else 0) + (2 if j >= LON else 0)
        wanted.append((kind, (z, i % LAT, j % LON)))
    return wanted


def unrolled_from(cells):
    wanted = []
    for cell in cells:
        z, i, j = cell
        z, i, j = 1 - z, i - 3, j - 6
        kind = (1 if i < 0 else 0) + (2 if j < 0 else 0)
        wanted.append((kind, (z, i % LAT, j % LON)))
    return wanted


def dot(a, b):
    return lax.dot_general(a, b, (((1,), (0,)), ((), ())), preferred_element_type=F32)


def dot_nt(a, b):
    return lax.dot_general(a, b, (((1,), (1,)), ((), ())), preferred_element_type=F32)


def dot_tn(a, b):
    return lax.dot_general(a, b, (((0,), (0,)), ((), ())), preferred_element_type=F32)


def normalise(values, count):
    mean = jnp.sum(values, axis=-1, keepdims=True) * (1.0 / count)
    centred = values - mean
    spread = jnp.sum(centred * centred, axis=-1, keepdims=True) * (1.0 / count)
    rstd = lax.rsqrt(spread + EPS)
    return centred * rstd, rstd


def normalise_back(cotangent, normed, rstd, count):
    first = jnp.sum(cotangent, axis=-1, keepdims=True) * (1.0 / count)
    second = jnp.sum(cotangent * normed, axis=-1, keepdims=True) * (1.0 / count)
    return rstd * (cotangent - first - normed * second)


def head_mask(values, head):
    lanes = lax.broadcasted_iota(jnp.int32, values.shape, 1)
    return jnp.where(lanes // HEAD == head, values, jnp.zeros_like(values))


def softmax(scores, ones):
    highest = jnp.max(scores, axis=-1, keepdims=True)
    powers = jnp.exp(scores - highest)
    rounded = powers.astype(BF)
    inverse = 1.0 / dot(rounded, ones)
    weights = powers * jnp.concatenate([inverse, inverse[:, : TOK - 128]], axis=1)
    return rounded, inverse, weights.astype(BF)


def scores_back(weights, dweights, ones):
    weights32 = weights.astype(F32)
    product = weights32 * dweights
    total = dot(product.astype(BF), ones)
    return product - weights32 * jnp.concatenate([total, total[:, : TOK - 128]], axis=1)


def rotated(value, shift, axis):
    size = value.shape[axis]
    return pltpu.roll(value, shift % size, axis)


def sheared(value, index, bits, lanes):
    for bit in range(bits):
        value = jnp.where((index >> bit) & 1 == 1, rotated(value, lanes << bit, 2), value)
    return value


def stripes_of(table, stripes_out):
    heads = table.shape[0]
    cells = lax.broadcasted_iota(jnp.int32, (1, 24, LANES), 2) // ROWS
    index = lax.broadcasted_iota(jnp.int32, (1, 24, LANES), 1)
    place = jnp.where(index < ROWS, (cells - index) & 31, -1)
    table = jnp.concatenate([table, jnp.zeros((heads, REL, LANES - TOK), F32)], axis=2)
    table = jnp.concatenate([table, jnp.zeros((heads, 1, LANES), F32)], axis=1)
    table = rotated(sheared(table, index, 5, -ROWS), 22 * ROWS, 2)
    stripes = jnp.zeros((heads, 24, LANES), F32)
    for r in range(REL):
        stripes = jnp.where(place == 22 - r, table[:, r : r + 1], stripes)
    stripes = sheared(stripes, index, 4, -ROWS)
    stripes_out[...] = stripes + rotated(rotated(stripes, ROWS, 2), ROWS, 1)


def stripes_back(stripes):
    heads = stripes.shape[0]
    cells = lax.broadcasted_iota(jnp.int32, (1, 24, LANES), 2) // ROWS
    index = lax.broadcasted_iota(jnp.int32, (1, 24, LANES), 1)
    place = (cells + index + 10) & 31
    stripes = stripes + rotated(rotated(stripes, -ROWS, 2), ROWS, 1)
    stripes = sheared(stripes, index, 4, ROWS)
    table = jnp.zeros((heads, 24, LANES), F32)
    for p in range(ROWS):
        table = jnp.where(place == p, stripes[:, p : p + 1], table)
    return rotated(sheared(table, index, 5, ROWS), -22 * ROWS, 2)


def pack_tables(totals, packed):
    packed[24 * TABLE :, :] = jnp.zeros((PACKED - 24 * TABLE, 128), F32)
    rest = jnp.zeros((24, 128), F32)
    for start in range(0, 24, BATCH):
        tables = stripes_back(totals[start : start + BATCH])
        for head in range(start, start + BATCH):
            rest = pack_table(tables[head - start], head, packed, rest)


def pack_table(table, head, packed, rest):
    packed[24 * head : 24 * head + 24, :] = table[:, :128]
    rest = rest + rotated(table[:, 128:256], 16 * (head % 8), 1)
    if head % 8 == 7:
        start = 24 * (24 + head // 8)
        packed[start : start + 24, :] = rest
        rest = jnp.zeros((24, 128), F32)
    return rest


def mask_of(last_row):
    first = lax.broadcasted_iota(jnp.int32, (24, LANES), 0) % ROWS
    second = lax.broadcasted_iota(jnp.int32, (24, LANES), 1) % ROWS
    half = WIN_Z // 2
    level = (first // WIN_LAT >= WIN_Z - half) != (second // WIN_LAT >= WIN_Z - half)
    if last_row is not None:
        half = WIN_LAT // 2
        row = (first % WIN_LAT >= WIN_LAT - half) != (second % WIN_LAT >= WIN_LAT - half)
        level = level | (row & (last_row == 1))
    return jnp.where(level, MASKED, 0.0).astype(F32)


def padded_lanes(weights):
    blocks = []
    for start in range(0, weights.shape[1], 192):
        blocks += [weights[:, start : start + 192], jnp.zeros((weights.shape[0], 64), weights.dtype)]
    return jnp.concatenate(blocks, axis=1)


def cut(fields, row_out, col_out, corner_out):
    row_out[...] = fields[:, 6:, :3]
    col_out[...] = fields[:, :6]
    corner_out[...] = fields[:, :6, :3]


def fine_forward(last, gather, send, fields, row, col, corner, table, w_qkv_in, w_proj_in, x_out, qkv_out, weights_out, mixed_out, row_out, col_out, corner_out, rolled, stripes, x_s, qkv_s, weights_s, sems):
    rolled[:, :, LAT:, :] = jnp.zeros((2, LON, 8, 192), F32)
    rolled[:, :6, :LAT, :] = fields[:, 6:].astype(F32)
    rolled[:, 6:, :LAT, :] = col[...].astype(F32)
    rolled[:, :6, LAT : LAT + 3, :] = row[...].astype(F32)
    rolled[:, 6:, LAT : LAT + 3, :] = corner[...].astype(F32)
    x = []
    for w in range(NWF):
        start = window_start(w)
        sources = rolled[:, :, start : start + 16].reshape(2 * LON * 16, 192).astype(BF)
        x.append(dot(gather[TOK * w : TOK * w + TOK, :], sources))
    x = jnp.concatenate(x, axis=0)
    x_s[...] = x.astype(BF)
    copies = [pltpu.make_async_copy(x_s, x_out, sems.at[0])]
    copies[-1].start()
    normed, _ = normalise(x, 192)
    qkv_s[...] = dot(normed.astype(BF), padded_lanes(w_qkv_in[...])).astype(BF)
    copies.append(pltpu.make_async_copy(qkv_s, qkv_out, sems.at[1]))
    copies[-1].start()
    w_proj = jnp.concatenate([w_proj_in[...], jnp.zeros((64, 192), BF)], axis=0)
    ones = jnp.ones((TOK, 128), BF)
    level_mask = mask_of(None)
    last_mask = mask_of(last[0])
    sent = []
    for w in range(NWF):
        rows = pl.ds(w * TOK, TOK)
        for start in range(0, 6, 3):
            stripes_of(table[0, w, start : start + 3], stripes.at[start : start + 3])
        blended = []
        for group, heads in ((0, 4), (1, 2)):
            queries = qkv_s[rows, 128 * group : 128 * group + 128]
            keys = qkv_s[rows, 256 + 128 * group : 256 + 128 * group + 128]
            values = qkv_s[rows, 512 + 128 * group : 512 + 128 * group + 128]
            total = jnp.zeros((TOK, 128), F32)
            for h in range(heads):
                head = 4 * group + h
                stripe = stripes[head] + (last_mask if w == NWF - 1 else level_mask)
                bias = [rotated(stripe, -(11 - 2 * m) * ROWS, 1)[:, :TOK] for m in range(6)]
                bias = jnp.concatenate(bias, axis=0)
                scores = dot_nt(head_mask(queries, h), keys) * SCALE + bias
                rounded, inverse, weights = softmax(scores, ones)
                weights_s[w, head] = weights
                total = total + head_mask(dot(rounded, values) * inverse, h)
            blended.append(total)
        blended = jnp.concatenate(blended, axis=1).astype(BF)
        mixed = x[w * TOK : (w + 1) * TOK] + dot(blended, w_proj)
        sent.append(mixed[HALF:])
        mixed_out[rows, :] = mixed.astype(BF)
        copies.append(pltpu.make_async_copy(weights_s.at[w], weights_out.at[w], sems.at[2 + w]))
        copies[-1].start()
    col_out[...] = jnp.concatenate(sent, axis=0).astype(BF)
    pieces = dot(send[...], mixed_out[TOK * (NWF - 1) :, :]).astype(BF)
    row_out[...] = pieces[:ROW_PIECE]
    corner_out[...] = pieces[ROW_PIECE:]
    for copy in copies:
        copy.wait()


def fine_backward(gather, send, own, row, col, corner, x_in, qkv_in, weights_hbm, w_qkv_in, w_proj_in, own_out, row_out, col_out, corner_out, packed_out, dqkv, packed, totals, x, qkv, weights_in, sems):
    copies = [
        pltpu.make_async_copy(qkv_in, qkv, sems.at[0]),
        pltpu.make_async_copy(weights_hbm.at[0], weights_in.at[0], sems.at[2]),
        pltpu.make_async_copy(weights_hbm.at[1], weights_in.at[1], sems.at[3]),
        pltpu.make_async_copy(weights_hbm.at[2], weights_in.at[2], sems.at[4]),
        pltpu.make_async_copy(weights_hbm.at[3], weights_in.at[3], sems.at[5]),
        pltpu.make_async_copy(x_in, x, sems.at[1]),
    ]
    for copy in copies:
        copy.start()
    sources = jnp.concatenate([own[...], row[...], col[...], corner[...]], axis=0)
    dmix = dot(gather[...], sources).astype(BF)
    w_proj = jnp.concatenate([w_proj_in[...], jnp.zeros((64, 192), BF)], axis=0)
    datt = dot_nt(dmix, w_proj).astype(BF)
    ones = jnp.ones((TOK, 128), BF)
    copies[0].wait()
    for w in range(NWF):
        copies[1 + w].wait()
        rows = pl.ds(w * TOK, TOK)
        for group, heads in ((0, 4), (1, 2)):
            lanes = slice(128 * group, 128 * group + 128)
            queries = qkv[rows, 128 * group : 128 * group + 128]
            keys = qkv[rows, 256 + 128 * group : 256 + 128 * group + 128]
            values = qkv[rows, 512 + 128 * group : 512 + 128 * group + 128]
            grad = datt[w * TOK : (w + 1) * TOK, lanes]
            dq = jnp.zeros((TOK, 128), F32)
            dk = jnp.zeros((TOK, 128), F32)
            dv = jnp.zeros((TOK, 128), F32)
            for h in range(heads):
                head = 4 * group + h
                weights = weights_in[w, head]
                grad_h = head_mask(grad, h)
                dscores = scores_back(weights, dot_nt(grad_h, values), ones)
                ds = dscores.astype(BF)
                dq = dq + head_mask(dot(ds, keys), h)
                dk = dk + dot_tn(ds, head_mask(queries, h))
                dv = dv + dot_tn(weights, grad_h)
                wide = jnp.concatenate([dscores, jnp.zeros((TOK, LANES - TOK), F32)], axis=1)
                total = jnp.zeros((24, LANES), F32)
                for m in range(6):
                    total = total + rotated(wide[24 * m : 24 * m + 24], (11 - 2 * m) * ROWS, 1)
                totals[6 * w + head] = total
            dqkv[rows, 128 * group : 128 * group + 128] = (dq * SCALE).astype(BF)
            dqkv[rows, 256 + 128 * group : 256 + 128 * group + 128] = (dk * SCALE).astype(BF)
            dqkv[rows, 512 + 128 * group : 512 + 128 * group + 128] = dv.astype(BF)
    pack_tables(totals, packed)
    packed_out[...] = packed[...].astype(BF)
    dnormed = dot_nt(dqkv[...], padded_lanes(w_qkv_in[...])).astype(BF).astype(F32)
    copies[5].wait()
    normed, rstd = normalise(x[...].astype(F32), 192)
    dx = normalise_back(dnormed, normed, rstd, 192).astype(BF).astype(F32)
    grad_rolled = dmix.astype(F32) + dx
    own_out[...] = grad_rolled.astype(BF)
    sent = [grad_rolled[TOK * w + HALF : TOK * w + TOK] for w in range(NWF)]
    col_out[...] = jnp.concatenate(sent, axis=0).astype(BF)
    pieces = dot(send[...], own_out[TOK * (NWF - 1) :, :]).astype(BF)
    row_out[...] = pieces[:ROW_PIECE]
    corner_out[...] = pieces[ROW_PIECE:]


def reordered(gather, values, out):
    out[...] = dot(gather[...], values[...]).astype(BF)


def unpack(bits, kept, kept_far, other, other_far, fine_out, coarse_out):
    even, low = bits[0] == 0, bits[1] == 0
    halves = [part[...].astype(F32) for part in (kept, kept_far, other, other_far)]
    tables = []
    for near, far in (halves[:2], halves[2:]):
        tables.append(
            jnp.concatenate([jnp.where(low, near, far), jnp.where(low, far, near)], axis=0)
        )
    coarse = jnp.where(even, tables[0], tables[1])
    fine = jnp.where(even, tables[1], tables[0])
    for packed, out, heads in ((fine, fine_out, 6), (coarse, coarse_out, 12)):
        for head in range(24):
            rest = 24 * (24 + head // 8)
            rest = rotated(packed[rest : rest + 24], -16 * (head % 8), 1)[:, : TOK - 128]
            table = jnp.concatenate([packed[24 * head : 24 * head + 24], rest], axis=1)
            out[0, head % heads, :, head // heads, :] = table[:REL]


def assemble(gather, own, row, col, corner, out):
    sources = jnp.concatenate([own[...], row[...], col[...], corner[...]], axis=0)
    out[...] = dot(gather[...], sources).astype(BF)


def merge_forward(gather, own, row, col, corner, w_merge, w_qkv, fine_out, coarse_out, queries_out, pairs_out):
    sources = jnp.concatenate([own[...], row[...], col[...], corner[...]], axis=0)
    fine = dot(gather[...], sources)
    fine_out[...] = fine.astype(BF)
    quarter = [fine[TOK * d : TOK * (d + 1)] for d in range(4)]
    mean = sum(jnp.sum(q, axis=-1, keepdims=True) for q in quarter) * (1.0 / 768)
    centred = [q - mean for q in quarter]
    spread = sum(jnp.sum(c * c, axis=-1, keepdims=True) for c in centred) * (1.0 / 768)
    rstd = lax.rsqrt(spread + EPS)
    coarse = jnp.zeros((TOK, 384), F32)
    for d in range(4):
        coarse = coarse + dot((centred[d] * rstd).astype(BF), w_merge[192 * d : 192 * d + 192, :])
    coarse = coarse.astype(BF)
    coarse_out[...] = coarse
    normed, _ = normalise(coarse.astype(F32), 384)
    projected = dot(normed.astype(BF), w_qkv[...])
    queries_out[...] = projected[:, :384].astype(BF)
    pairs_out[...] = projected[:, 384:].astype(BF)


def coarse_middle(parity, queries_in, pairs_in, far_in, coarse_in, fine, upstream, table, w_proj, w_split, result_out, input_back_out, own_back_out, far_back_out, packed_out, attended, weights_ref, dattended, packed, totals):
    pairs = pairs_in[...].astype(F32)
    far = far_in[...].astype(F32)
    queries32 = queries_in[...].astype(F32)
    joined = []
    first = parity[0] == 0
    ones = jnp.ones((TOK, 128), BF)
    lanes = lax.broadcasted_iota(jnp.int32, (24, TOK), 1)
    wide_lanes = lax.broadcasted_iota(jnp.int32, (24, LANES), 1)
    for w in range(NWC):
        joined.append(
            jnp.concatenate([pairs[HALF * w : HALF * w + HALF], far[HALF * w : HALF * w + HALF]], axis=0).astype(BF)
        )
    for w in range(NWC):
        for start in range(0, 12, BATCH):
            stripes_of(table[0, w, start : start + BATCH], totals.at[start : start + BATCH])
        for group in range(3):
            queries = queries32[HALF * w : HALF * w + HALF, 128 * group : 128 * group + 128].astype(BF)
            keys = joined[w][:, 128 * group : 128 * group + 128]
            values = joined[w][:, 384 + 128 * group : 384 + 128 * group + 128]
            total = jnp.zeros((HALF, 128), F32)
            for h in range(4):
                head = 4 * group + h
                stripe = totals[head]
                other = jnp.where(first, rotated(stripe, -84, 1), rotated(stripe, 60, 1))
                bias = []
                for m in range(3):
                    offset = 48 - 24 * m
                    bias.append(
                        jnp.where(
                            lanes < HALF,
                            rotated(stripe, -(84 + offset), 1)[:, :TOK],
                            rotated(other, -offset, 1)[:, :TOK],
                        )
                    )
                bias = jnp.concatenate(bias, axis=0)
                scores = dot_nt(head_mask(queries, h), keys) * SCALE + bias
                rounded, inverse, weights = softmax(scores, ones)
                weights_ref[w, head] = weights
                total = total + head_mask(dot(rounded, values) * inverse, h)
            attended[HALF * w : HALF * w + HALF, 128 * group : 128 * group + 128] = total
    coarse32 = coarse_in[...].astype(F32)
    coarse_out = (coarse32 + dot(attended[...].astype(BF), w_proj[...])).astype(BF)
    normed, rstd = normalise(coarse_out.astype(F32), 384)
    normed_b = normed.astype(BF)
    back = jnp.zeros((TOK, 384), F32)
    for d in range(4):
        part = w_split[:, 192 * d : 192 * d + 192]
        up = upstream[TOK * d : TOK * d + TOK, :]
        widened = dot(normed_b, part)
        result_out[TOK * d : TOK * d + TOK, :] = (fine[TOK * d : TOK * d + TOK, :].astype(F32) + widened).astype(BF)
        back = back + dot_nt(up, part)
    back = back.astype(BF).astype(F32)
    input_back = normalise_back(back, normed, rstd, 384).astype(BF)
    input_back_out[...] = input_back
    dattended[...] = dot_nt(input_back, w_proj[...]).astype(BF).astype(F32)
    for w in range(NWC):
        for group in range(3):
            queries = queries32[HALF * w : HALF * w + HALF, 128 * group : 128 * group + 128].astype(BF)
            keys = joined[w][:, 128 * group : 128 * group + 128]
            values = joined[w][:, 384 + 128 * group : 384 + 128 * group + 128]
            grad = dattended[HALF * w : HALF * w + HALF, 128 * group : 128 * group + 128].astype(BF)
            dq = jnp.zeros((HALF, 128), F32)
            dk = jnp.zeros((TOK, 128), F32)
            dv = jnp.zeros((TOK, 128), F32)
            for h in range(4):
                head = 4 * group + h
                weights = weights_ref[w, head]
                grad_h = head_mask(grad, h)
                dscores = scores_back(weights, dot_nt(grad_h, values), ones)
                ds = dscores.astype(BF)
                dq = dq + head_mask(dot(ds, keys), h)
                dk = dk + dot_tn(ds, head_mask(queries, h))
                dv = dv + dot_tn(weights, grad_h)
                wide = jnp.concatenate([dscores, jnp.zeros((HALF, LANES - TOK), F32)], axis=1)
                near = jnp.zeros((24, LANES), F32)
                other = jnp.zeros((24, LANES), F32)
                for m in range(3):
                    offset = 48 - 24 * m
                    block = wide[24 * m : 24 * m + 24]
                    part = jnp.where(wide_lanes < HALF, block, 0.0)
                    near = near + rotated(part, 84 + offset, 1)
                    other = other + rotated(block - part, offset, 1)
                other = jnp.where(first, rotated(other, 84, 1), rotated(other, -60, 1))
                totals[12 * w + head] = near + other
            part = slice(HALF * w, HALF * w + HALF)
            cols = slice(128 * group, 128 * group + 128)
            own_back_out[part, cols] = dq * SCALE
            own_back_out[part, 384 + 128 * group : 384 + 128 * group + 128] = dk[:HALF] * SCALE
            own_back_out[part, 768 + 128 * group : 768 + 128 * group + 128] = dv[:HALF]
            far_back_out[part, cols] = (dk[HALF:] * SCALE).astype(BF)
            far_back_out[part, 384 + 128 * group : 384 + 128 * group + 128] = dv[HALF:].astype(BF)
    pack_tables(totals, packed)
    packed_out[...] = packed[...].astype(BF)


def merge_backward(send, own_back, returned, coarse_in, input_back, fine, upstream, w_merge, w_qkv, own_out, row_out, col_out, corner_out):
    returned32 = returned[...].astype(F32)
    dq = own_back[:, :384].astype(BF)
    dkv = (own_back[:, 384:] + returned32).astype(BF)
    dnormed = dot_nt(dq, w_qkv[:, :384]) + dot_nt(dkv, w_qkv[:, 384:])
    dnormed = dnormed.astype(BF).astype(F32)
    normed, rstd = normalise(coarse_in[...].astype(F32), 384)
    dx = normalise_back(dnormed, normed, rstd, 384).astype(BF)
    dcoarse = (input_back[...].astype(F32) + dx.astype(F32)).astype(BF)
    quarter = [fine[TOK * d : TOK * (d + 1), :].astype(F32) for d in range(4)]
    mean = sum(jnp.sum(q, axis=-1, keepdims=True) for q in quarter) * (1.0 / 768)
    centred = [q - mean for q in quarter]
    spread = sum(jnp.sum(c * c, axis=-1, keepdims=True) for c in centred) * (1.0 / 768)
    rstd = lax.rsqrt(spread + EPS)
    normed = [c * rstd for c in centred]
    dmerged = [
        dot_nt(dcoarse, w_merge[192 * d : 192 * d + 192, :]).astype(BF).astype(F32) for d in range(4)
    ]
    first = sum(jnp.sum(g, axis=-1, keepdims=True) for g in dmerged) * (1.0 / 768)
    second = sum(jnp.sum(g * n, axis=-1, keepdims=True) for g, n in zip(dmerged, normed)) * (1.0 / 768)
    for d in range(4):
        dfine = (rstd * (dmerged[d] - first - normed[d] * second)).astype(BF).astype(F32)
        up = upstream[TOK * d : TOK * (d + 1), :].astype(F32)
        own_out[TOK * d : TOK * (d + 1), :] = (up + dfine).astype(BF)
    pieces = dot(send[...], own_out[...]).astype(BF)
    row_out[...] = pieces[:ROW_PIECE]
    col_out[...] = pieces[ROW_PIECE : ROW_PIECE + COL_PIECE]
    corner_out[...] = pieces[ROW_PIECE + COL_PIECE :]


def moved(value, lat, lon):
    lats, lons = lax.axis_size("lat"), lax.axis_size("lon")
    if lat == 0:
        pairs = [(source, (source + lon) % lons) for source in range(lons)]
        return lax.ppermute(value, "lon", pairs)
    if lon == 0:
        pairs = [(source, (source + lat) % lats) for source in range(lats)]
        return lax.ppermute(value, "lat", pairs)
    pairs = [
        (a * lons + b, (a + lat) % lats * lons + (b + lon) % lons)
        for a in range(lats)
        for b in range(lons)
    ]
    return lax.ppermute(value, ("lat", "lon"), pairs)


def exchanged(pieces, step):
    row, col, corner = pieces
    return moved(row, step, 0), moved(col, 0, step), moved(corner, step, step)


def call(kernel, out_shapes, *operands, scratch=(), scalars=0, hbm_in=(), hbm_out=()):
    shapes = [jax.ShapeDtypeStruct(shape, dtype) for shape, dtype in out_shapes]
    scalar, array = pl.BlockSpec(memory_space=pltpu.SMEM), pl.BlockSpec(memory_space=pltpu.VMEM)
    remote = pl.BlockSpec(memory_space=pltpu.HBM)
    return pl.pallas_call(
        kernel,
        out_shape=shapes,
        in_specs=[
            scalar if i < scalars else remote if i in hbm_in else array for i in range(len(operands))
        ],
        out_specs=[remote if i in hbm_out else array for i in range(len(shapes))],
        scratch_shapes=list(scratch),
        compiler_params=pltpu.CompilerParams(vmem_limit_bytes=VMEM),
        name=kernel.__name__,
    )(*operands)


def swapped(value, step):
    pairs = [(source, source ^ step) for source in range(lax.axis_size("lon"))]
    return lax.ppermute(value, "lon", pairs)


def on_device(fields, upstream, bias_f, bias_c, w_qkv_f, w_proj_f, w_merge, w_qkv_c, w_proj_c, w_split):
    windows, quartets = window_order(), quartet_order()
    last = (lax.axis_index("lat") == lax.axis_size("lat") - 1).astype(jnp.int32).reshape(1)
    odd = lax.axis_index("lon") % 2
    parity = odd.astype(jnp.int32).reshape(1)

    fields = fields.transpose(0, 2, 1, 3)
    upstream = upstream.transpose(0, 2, 1, 3).reshape(576, 192)
    natural = natural_order()
    place = {cell: index for index, cell in enumerate(natural)}
    pieces = call(cut, [((2, 6, 3, 192), BF), ((2, 6, LAT, 192), BF), ((2, 6, 3, 192), BF)], fields)
    row, col, corner = exchanged(pieces, -1)
    (up,) = call(
        reordered, [((576, 192), BF)], one_hot([place[cell] for cell in quartets], 576), upstream
    )
    piece_shapes = [((size, 192), BF) for size in (ROW_PIECE, COL_PIECE, CORNER)]
    x, qkv, weights, mixed, *pieces = call(
        fine_forward,
        [((576, 192), BF), ((576, 768), BF), ((NWF, 6, TOK, TOK), BF), ((576, 192), BF)] + piece_shapes,
        last, window_table(), last_window_table(), fields, row, col, corner, bias_f, w_qkv_f, w_proj_f,
        scratch=[
            pltpu.VMEM((2, LON, LAT + 8, 192), F32),
            pltpu.VMEM((6, 24, LANES), F32),
            pltpu.VMEM((576, 192), BF),
            pltpu.VMEM((576, 768), BF),
            pltpu.VMEM((NWF, 6, TOK, TOK), BF),
            pltpu.SemaphoreType.DMA((6,)),
        ],
        hbm_out=(0, 1, 2),
        scalars=1,
    )
    row, col, corner = exchanged(pieces, 1)
    fine, coarse_in, queries, pairs = call(
        merge_forward,
        [((576, 192), BF), ((TOK, 384), BF), ((TOK, 384), BF), ((TOK, 768), BF)],
        gather_table(windows, back_pieces(), unrolled_from(quartets)),
        mixed, row, col, corner, w_merge, w_qkv_c,
    )
    far = swapped(pairs, 1)
    result_q, input_back, own_back, far_back, packed_c = call(
        coarse_middle,
        [
            ((576, 192), BF),
            ((TOK, 384), BF),
            ((TOK, 1152), F32),
            ((TOK, 768), BF),
            ((PACKED, 128), BF),
        ],
        parity, queries, pairs, far, coarse_in, fine, up, bias_c, w_proj_c, w_split,
        scratch=[
            pltpu.VMEM((TOK, 384), F32),
            pltpu.VMEM((NWC, 12, HALF, TOK), BF),
            pltpu.VMEM((TOK, 384), F32),
            pltpu.VMEM((PACKED, 128), F32),
            pltpu.VMEM((24, 24, LANES), F32),
        ],
        scalars=1,
    )
    returned = swapped(far_back, 1)
    fine_back, *pieces = call(
        merge_backward,
        [((576, 192), BF)] + piece_shapes,
        send_table(quartets, forward_pieces()),
        own_back, returned, coarse_in, input_back, fine, up, w_merge, w_qkv_c,
    )
    row, col, corner = exchanged(pieces, -1)
    place = {cell: index for index, cell in enumerate(quartets)}
    (result,) = call(
        reordered, [((576, 192), BF)], one_hot([place[cell] for cell in natural], 576), result_q
    )
    grad_rolled, *rest = call(
        fine_backward,
        [((576, 192), BF)] + piece_shapes + [((PACKED, 128), BF)],
        gather_table(quartets, forward_pieces(), rolled_from(windows)),
        last_window_table(),
        fine_back, row, col, corner, x, qkv, weights, w_qkv_f, w_proj_f,
        scratch=[
            pltpu.VMEM((576, 768), BF),
            pltpu.VMEM((PACKED, 128), F32),
            pltpu.VMEM((24, 24, LANES), F32),
            pltpu.VMEM((576, 192), BF),
            pltpu.VMEM((576, 768), BF),
            pltpu.VMEM((NWF, 6, TOK, TOK), BF),
            pltpu.SemaphoreType.DMA((6,)),
        ],
        hbm_in=(6, 7, 8),
    )
    *pieces, packed_f = rest

    row, col, corner = exchanged(pieces, 1)
    sent = jnp.where(odd == 0, packed_f, packed_c)
    kept = jnp.where(odd == 0, packed_c, packed_f)
    kept = kept.astype(F32) + swapped(sent, 1).astype(F32)
    far = lax.axis_index("lon") // 2 % 2
    low, high = kept[: PACKED // 2], kept[PACKED // 2 :]
    sent = jnp.where(far == 0, high, low).astype(BF)
    kept = jnp.where(far == 0, low, high)
    kept = (kept + swapped(sent, 2).astype(F32)).astype(BF)
    kept, row, col, corner = lax.optimization_barrier((kept, row, col, corner))
    step = lax.axis_size("lon") // 2
    while step > 2:
        kept = (kept.astype(F32) + swapped(kept, step).astype(F32)).astype(BF)
        step //= 2
    kept_far = swapped(kept, 2)
    grad_bias_f, grad_bias_c = call(
        unpack,
        [((1, 6, REL, NWF, TOK), F32), ((1, 12, REL, NWC, TOK), F32)],
        jnp.stack([odd, far]).astype(jnp.int32), kept, kept_far, swapped(kept, 1), swapped(kept_far, 1),
        scalars=1,
    )
    grad_bias_f = grad_bias_f.transpose(0, 3, 1, 2, 4)
    grad_bias_c = grad_bias_c.transpose(0, 3, 1, 2, 4)
    (grad_fields,) = call(
        assemble,
        [((576, 192), BF)],
        gather_table(windows, back_pieces(), unrolled_from(natural)),
        grad_rolled, row, col, corner,
    )
    result = result.reshape(2, LON, LAT, 192).transpose(0, 2, 1, 3)
    grad_fields = grad_fields.reshape(2, LON, LAT, 192).transpose(0, 2, 1, 3)
    return (result, grad_fields, grad_bias_f, grad_bias_c)


def solution(mesh):
    grid = P(None, "lat", "lon", None)
    table = P(None, "lat", None, None, None)
    return jax.shard_map(
        on_device,
        mesh=mesh,
        in_specs=(grid, grid, table, table, P(), P(), P(), P(), P(), P()),
        out_specs=(grid, grid, table, table),
        check_vma=False,
    )
```

```python
import math

import jax
import jax.numpy as jnp
import numpy as np
from jax import lax
from jax.experimental import pallas as pl
from jax.experimental.pallas import tpu as pltpu
from jax.sharding import PartitionSpec as P

WIN_Z = 2
WIN_LAT = 6
WIN_LON = 12
ROWS = WIN_Z * WIN_LAT
TOK = ROWS * WIN_LON
HALF = TOK // 2
REL = 2 * WIN_LON - 1
WIDE = REL * ROWS
EPS = 1e-05
MASKED = -1000000000.0
HEAD = 32
SCALE = 1.0 / math.sqrt(HEAD)
LAT = 24
LON = 12
NWF = LAT // WIN_LAT
NWC = LAT // 2 // WIN_LAT
BF = jnp.bfloat16
F32 = jnp.float32
ROW_PIECE, COL_PIECE, CORNER = 48, 288, 48
VMEM = 56 * 1024 * 1024
TABLE = 24 + 3
LANES = 384
PACKED = 24 * TABLE + 8
BATCH = 4


def natural_order():
    return [(z, i, j) for z in range(2) for j in range(LON) for i in range(LAT)]


def window_order():
    return [
        (z, WIN_LAT * w + l, n)
        for w in range(NWF)
        for n in range(LON)
        for z in range(2)
        for l in range(WIN_LAT)
    ]


def quartet_order():
    return [
        (z, 2 * (WIN_LAT * w + l) + di, 2 * n + dj)
        for di in range(2)
        for dj in range(2)
        for w in range(NWC)
        for n in range(LON // 2)
        for z in range(2)
        for l in range(WIN_LAT)
    ]


def one_hot(rows, columns):
    table = np.zeros((len(rows), columns), np.float32)
    for row, column in enumerate(rows):
        if column is not None:
            table[row, column] = 1.0
    return jnp.asarray(table, BF)


def forward_pieces():
    row = [(z, i, j) for z in range(2) for i in range(3) for j in range(6, LON)]
    col = [(z, i, j) for z in range(2) for i in range(LAT) for j in range(6)]
    corner = [(z, i, j) for z in range(2) for i in range(3) for j in range(6)]
    return row, col, corner


def back_pieces():
    row = [(z, i, j) for z in range(2) for i in range(LAT - 3, LAT) for j in range(6)]
    col = [cell for cell in window_order() if cell[2] >= 6]
    corner = [(z, i, j) for z in range(2) for i in range(LAT - 3, LAT) for j in range(6, LON)]
    return row, col, corner


def padded_pieces(pieces):
    sizes = (ROW_PIECE, COL_PIECE, CORNER)
    return [cells + [None] * (size - len(cells)) for cells, size in zip(pieces, sizes)]


def send_table(own_order, pieces):
    place = {cell: index for index, cell in enumerate(own_order)}
    cells = sum(padded_pieces(pieces), [])
    return one_hot([None if cell is None else place[cell] for cell in cells], len(own_order))


def gather_table(own_order, pieces, wanted):
    tables = [{cell: index for index, cell in enumerate(own_order)}]
    starts = [0]
    for cells in pieces:
        tables.append({cell: index for index, cell in enumerate(cells)})
    starts = [0, len(own_order), len(own_order) + ROW_PIECE, len(own_order) + ROW_PIECE + COL_PIECE]
    total = len(own_order) + ROW_PIECE + COL_PIECE + CORNER
    rows = []
    for entry in wanted:
        rows.append(None if entry is None else starts[entry[0]] + tables[entry[0]][entry[1]])
    return one_hot(rows, total)


def window_start(w):
    return (WIN_LAT * w + WIN_LAT // 2) // 8 * 8 if w < NWF - 1 else LAT - 8


def window_table():
    rows = []
    for w in range(NWF):
        offset = WIN_LAT * w + WIN_LAT // 2 - window_start(w)
        for n in range(LON):
            for z in range(2):
                for l in range(WIN_LAT):
                    rows.append(((1 - z) * LON + n) * 16 + offset + l)
    return one_hot(rows, 2 * LON * 16)


def last_window_table():
    place = {cell: index for index, cell in enumerate(window_order()[-TOK:])}
    row, _, corner = padded_pieces(back_pieces())
    return one_hot([None if cell is None else place[cell] for cell in row + corner], TOK)


def rolled_from(cells):
    wanted = []
    for z, i, j in cells:
        z, i, j = 1 - z, i + 3, j + 6
        kind = (1 if i >= LAT else 0) + (2 if j >= LON else 0)
        wanted.append((kind, (z, i % LAT, j % LON)))
    return wanted


def unrolled_from(cells):
    wanted = []
    for cell in cells:
        z, i, j = cell
        z, i, j = 1 - z, i - 3, j - 6
        kind = (1 if i < 0 else 0) + (2 if j < 0 else 0)
        wanted.append((kind, (z, i % LAT, j % LON)))
    return wanted


def dot(a, b):
    return lax.dot_general(a, b, (((1,), (0,)), ((), ())), preferred_element_type=F32)


def dot_nt(a, b):
    return lax.dot_general(a, b, (((1,), (1,)), ((), ())), preferred_element_type=F32)


def dot_tn(a, b):
    return lax.dot_general(a, b, (((0,), (0,)), ((), ())), preferred_element_type=F32)


def normalise(values, count):
    mean = jnp.sum(values, axis=-1, keepdims=True) * (1.0 / count)
    centred = values - mean
    spread = jnp.sum(centred * centred, axis=-1, keepdims=True) * (1.0 / count)
    rstd = lax.rsqrt(spread + EPS)
    return centred * rstd, rstd


def normalise_back(cotangent, normed, rstd, count):
    first = jnp.sum(cotangent, axis=-1, keepdims=True) * (1.0 / count)
    second = jnp.sum(cotangent * normed, axis=-1, keepdims=True) * (1.0 / count)
    return rstd * (cotangent - first - normed * second)


def head_stack(values, heads):
    lanes = lax.broadcasted_iota(jnp.int32, values.shape, 1) // HEAD
    return jnp.concatenate([jnp.where(lanes == h, values, 0.0) for h in range(heads)], axis=0).astype(BF)


def head_sum(stacked, heads):
    rows = stacked.shape[0] // heads
    lanes = lax.broadcasted_iota(jnp.int32, (rows, 128), 1) // HEAD
    total = stacked[:rows]
    for h in range(1, heads):
        total = jnp.where(lanes == h, stacked[h * rows : (h + 1) * rows], total)
    return jnp.where(lanes < heads, total, 0.0)


def softmax(scores, ones):
    highest = jnp.max(scores, axis=-1, keepdims=True)
    powers = jnp.exp(scores - highest)
    rounded = powers.astype(BF)
    inverse = 1.0 / dot(rounded, ones)
    weights = powers * jnp.concatenate([inverse, inverse[:, : TOK - 128]], axis=1)
    return rounded, inverse, weights.astype(BF)


def scores_back(weights, dweights, ones):
    weights32 = weights.astype(F32)
    product = weights32 * dweights
    total = dot(product.astype(BF), ones)
    return product - weights32 * jnp.concatenate([total, total[:, : TOK - 128]], axis=1)


def rotated(value, shift, axis):
    size = value.shape[axis]
    return pltpu.roll(value, shift % size, axis)


def sheared(value, index, bits, lanes):
    for bit in range(bits):
        value = jnp.where((index >> bit) & 1 == 1, rotated(value, lanes << bit, 2), value)
    return value


def strided(value):
    tiles = []
    for start in range(0, value.shape[1], 8):
        tile = pltpu.roll(value[:, start : start + 8], 0, 2, stride=ROWS, stride_axis=1)
        tiles.append(rotated(tile, ROWS * start, 2))
    return jnp.concatenate(tiles, axis=1)


def raised(value, amount, steps):
    for step in steps:
        value = jnp.where(amount & step != 0, rotated(value, step, 1), value)
    return value


def stripes_of(table, stripes_out):
    heads = table.shape[0]
    index = lax.broadcasted_iota(jnp.int32, (1, 24, LANES), 1)
    amount = (lax.broadcasted_iota(jnp.int32, (1, 8, LANES), 2) // ROWS + 10) & 31
    table = jnp.concatenate([table, jnp.zeros((heads, REL, LANES - TOK), F32)], axis=2)
    table = jnp.concatenate([table, jnp.zeros((heads, 1, LANES), F32)], axis=1)
    table = rotated(sheared(table, index, 5, -ROWS), 22 * ROWS, 2)
    tiles = [table[:, 0:8], table[:, 8:16], table[:, 16:24], jnp.zeros((heads, 8, LANES), F32)]
    tiles = [jnp.where(amount & 16 != 0, tiles[k - 2], tiles[k]) for k in range(4)]
    tiles = [jnp.where(amount & 8 != 0, tiles[k - 1], tiles[k]) for k in range(4)]
    stripes = jnp.concatenate([tiles[3], tiles[0], tiles[1]], axis=1)
    stripes = raised(stripes, amount[:, :1], (4, 2, 1))[:, 8:]
    stripes = sheared(stripes, index[:, :16], 4, -ROWS)
    stripes = jnp.where(index[:, :16] < ROWS, stripes, 0.0)
    stripes = jnp.concatenate([stripes, jnp.zeros((heads, 8, LANES), F32)], axis=1)
    stripes_out[...] = stripes + rotated(rotated(stripes, ROWS, 2), ROWS, 1)


def stripes_back(stripes):
    heads = stripes.shape[0]
    index = lax.broadcasted_iota(jnp.int32, (1, 16, LANES), 1)
    amount = (22 - lax.broadcasted_iota(jnp.int32, (1, 8, LANES), 2) // ROWS) & 31
    stripes = stripes + rotated(rotated(stripes, -ROWS, 2), ROWS, 1)
    stripes = strided(jnp.where(index < ROWS, stripes[:, :16], 0.0))
    blank = jnp.zeros((heads, 8, LANES), F32)
    stripes = raised(jnp.concatenate([stripes, blank], axis=1), amount[:, :1], (1, 2, 4))
    tiles = [stripes[:, 0:8], stripes[:, 8:16], stripes[:, 16:24], blank]
    tiles = [jnp.where(amount & 8 != 0, tiles[k - 1], tiles[k]) for k in range(4)]
    tiles = [jnp.where(amount & 16 != 0, tiles[k - 2], tiles[k]) for k in range(3)]
    return rotated(strided(jnp.concatenate(tiles, axis=1)), -22 * ROWS, 2)


def pack_tables(totals, packed):
    packed[24 * TABLE :, :] = jnp.zeros((PACKED - 24 * TABLE, 128), F32)
    rest = jnp.zeros((24, 128), F32)
    for start in range(0, 24, BATCH):
        tables = stripes_back(totals[start : start + BATCH])
        for head in range(start, start + BATCH):
            rest = pack_table(tables[head - start], head, packed, rest)


def pack_table(table, head, packed, rest):
    packed[24 * head : 24 * head + 24, :] = table[:, :128]
    rest = rest + rotated(table[:, 128:256], 16 * (head % 8), 1)
    if head % 8 == 7:
        start = 24 * (24 + head // 8)
        packed[start : start + 24, :] = rest
        rest = jnp.zeros((24, 128), F32)
    return rest


def mask_of(last_row):
    first = lax.broadcasted_iota(jnp.int32, (24, LANES), 0) % ROWS
    second = lax.broadcasted_iota(jnp.int32, (24, LANES), 1) % ROWS
    half = WIN_Z // 2
    level = (first // WIN_LAT >= WIN_Z - half) != (second // WIN_LAT >= WIN_Z - half)
    if last_row is not None:
        half = WIN_LAT // 2
        row = (first % WIN_LAT >= WIN_LAT - half) != (second % WIN_LAT >= WIN_LAT - half)
        level = level | (row & (last_row == 1))
    return jnp.where(level, MASKED, 0.0).astype(F32)


def padded_lanes(weights):
    blocks = []
    for start in range(0, weights.shape[1], 192):
        blocks += [weights[:, start : start + 192], jnp.zeros((weights.shape[0], 64), weights.dtype)]
    return jnp.concatenate(blocks, axis=1)


def cut(fields, row_out, col_out, corner_out):
    row_out[...] = fields[:, 6:, :3]
    col_out[...] = fields[:, :6]
    corner_out[...] = fields[:, :6, :3]


def fine_forward(last, gather, send, fields, row, col, corner, table, w_qkv_in, w_proj_in, x_out, qkv_out, weights_out, mixed_out, row_out, col_out, corner_out, rolled, stripes, x_s, qkv_s, weights_s, sems):
    rolled[:, :, LAT:, :] = jnp.zeros((2, LON, 8, 192), F32)
    rolled[:, :6, :LAT, :] = fields[:, 6:].astype(F32)
    rolled[:, 6:, :LAT, :] = col[...].astype(F32)
    rolled[:, :6, LAT : LAT + 3, :] = row[...].astype(F32)
    rolled[:, 6:, LAT : LAT + 3, :] = corner[...].astype(F32)
    x = []
    for w in range(NWF):
        start = window_start(w)
        sources = rolled[:, :, start : start + 16].reshape(2 * LON * 16, 192).astype(BF)
        x.append(dot(gather[TOK * w : TOK * w + TOK, :], sources))
    x = jnp.concatenate(x, axis=0)
    x_s[...] = x.astype(BF)
    copies = [pltpu.make_async_copy(x_s, x_out, sems.at[0])]
    copies[-1].start()
    normed, _ = normalise(x, 192)
    qkv_s[...] = dot(normed.astype(BF), padded_lanes(w_qkv_in[...])).astype(BF)
    copies.append(pltpu.make_async_copy(qkv_s, qkv_out, sems.at[1]))
    copies[-1].start()
    w_proj = jnp.concatenate([w_proj_in[...], jnp.zeros((64, 192), BF)], axis=0)
    ones = jnp.ones((TOK, 128), BF)
    level_mask = mask_of(None)
    last_mask = mask_of(last[0])
    sent = []
    for w in range(NWF):
        rows = pl.ds(w * TOK, TOK)
        for start in range(0, 6, 3):
            stripes_of(table[0, w, start : start + 3], stripes.at[start : start + 3])
        blended = []
        for group, heads in ((0, 4), (1, 2)):
            queries = qkv_s[rows, 128 * group : 128 * group + 128]
            keys = qkv_s[rows, 256 + 128 * group : 256 + 128 * group + 128]
            values = qkv_s[rows, 512 + 128 * group : 512 + 128 * group + 128]
            bias = []
            for h in range(heads):
                stripe = stripes[4 * group + h] + (last_mask if w == NWF - 1 else level_mask)
                bias += [rotated(stripe, -(11 - 2 * m) * ROWS, 1)[:, :TOK] for m in range(6)]
            bias = jnp.concatenate(bias, axis=0)
            queries = head_stack(queries.astype(F32), heads)
            rounded, inverse, weights = softmax(dot_nt(queries, keys) * SCALE + bias, ones)
            weights_s[w, 4 * TOK * group : 4 * TOK * group + heads * TOK, :] = weights
            blended.append(head_sum(dot(rounded, values) * inverse, heads))
        blended = jnp.concatenate(blended, axis=1).astype(BF)
        mixed = x[w * TOK : (w + 1) * TOK] + dot(blended, w_proj)
        sent.append(mixed[HALF:])
        mixed_out[rows, :] = mixed.astype(BF)
        copies.append(pltpu.make_async_copy(weights_s.at[w], weights_out.at[w], sems.at[2 + w]))
        copies[-1].start()
    col_out[...] = jnp.concatenate(sent, axis=0).astype(BF)
    pieces = dot(send[...], mixed_out[TOK * (NWF - 1) :, :]).astype(BF)
    row_out[...] = pieces[:ROW_PIECE]
    corner_out[...] = pieces[ROW_PIECE:]
    for copy in copies:
        copy.wait()


def fine_backward(gather, send, own, row, col, corner, x, qkv, weights_in, w_qkv_in, w_proj_in, own_out, row_out, col_out, corner_out, packed_out, dqkv, packed, totals):
    sources = jnp.concatenate([own[...], row[...], col[...], corner[...]], axis=0)
    dmix = dot(gather[...], sources).astype(BF)
    w_proj = jnp.concatenate([w_proj_in[...], jnp.zeros((64, 192), BF)], axis=0)
    datt = dot_nt(dmix, w_proj).astype(BF)
    ones = jnp.ones((TOK, 128), BF)
    for w in range(NWF):
        rows = pl.ds(w * TOK, TOK)
        for group, heads in ((0, 4), (1, 2)):
            lanes = slice(128 * group, 128 * group + 128)
            queries = qkv[rows, 128 * group : 128 * group + 128]
            keys = qkv[rows, 256 + 128 * group : 256 + 128 * group + 128]
            values = qkv[rows, 512 + 128 * group : 512 + 128 * group + 128]
            grad = datt[w * TOK : (w + 1) * TOK, lanes]
            queries = head_stack(queries.astype(F32), heads)
            grad = head_stack(grad.astype(F32), heads)
            weights = weights_in[w, 4 * TOK * group : 4 * TOK * group + heads * TOK, :]
            dscores = scores_back(weights, dot_nt(grad, values), ones)
            ds = dscores.astype(BF)
            dq = head_sum(dot(ds, keys), heads)
            dk = dot_tn(ds, queries)
            dv = dot_tn(weights, grad)
            wide = jnp.concatenate([dscores, jnp.zeros((heads * TOK, LANES - TOK), F32)], axis=1)
            for h in range(heads):
                total = jnp.zeros((24, LANES), F32)
                for m in range(6):
                    block = wide[TOK * h + 24 * m : TOK * h + 24 * m + 24]
                    total = total + rotated(block, (11 - 2 * m) * ROWS, 1)
                totals[6 * w + 4 * group + h] = total
            dqkv[rows, 128 * group : 128 * group + 128] = (dq * SCALE).astype(BF)
            dqkv[rows, 256 + 128 * group : 256 + 128 * group + 128] = (dk * SCALE).astype(BF)
            dqkv[rows, 512 + 128 * group : 512 + 128 * group + 128] = dv.astype(BF)
    pack_tables(totals, packed)
    packed_out[...] = packed[...].astype(BF)
    dnormed = dot_nt(dqkv[...], padded_lanes(w_qkv_in[...])).astype(BF).astype(F32)
    normed, rstd = normalise(x[...].astype(F32), 192)
    dx = normalise_back(dnormed, normed, rstd, 192).astype(BF).astype(F32)
    grad_rolled = dmix.astype(F32) + dx
    own_out[...] = grad_rolled.astype(BF)
    sent = [grad_rolled[TOK * w + HALF : TOK * w + TOK] for w in range(NWF)]
    col_out[...] = jnp.concatenate(sent, axis=0).astype(BF)
    pieces = dot(send[...], own_out[TOK * (NWF - 1) :, :]).astype(BF)
    row_out[...] = pieces[:ROW_PIECE]
    corner_out[...] = pieces[ROW_PIECE:]


def reordered(gather, values, out):
    out[...] = dot(gather[...], values[...]).astype(BF)


def unpack(bits, kept, kept_far, other, other_far, fine_out, coarse_out):
    even, low = bits[0] == 0, bits[1] == 0
    halves = [part[...].astype(F32) for part in (kept, kept_far, other, other_far)]
    tables = []
    for near, far in (halves[:2], halves[2:]):
        tables.append(
            jnp.concatenate([jnp.where(low, near, far), jnp.where(low, far, near)], axis=0)
        )
    coarse = jnp.where(even, tables[0], tables[1])
    fine = jnp.where(even, tables[1], tables[0])
    for packed, out, heads in ((fine, fine_out, 6), (coarse, coarse_out, 12)):
        for head in range(24):
            rest = 24 * (24 + head // 8)
            rest = rotated(packed[rest : rest + 24], -16 * (head % 8), 1)[:, : TOK - 128]
            table = jnp.concatenate([packed[24 * head : 24 * head + 24], rest], axis=1)
            out[0, head % heads, :, head // heads, :] = table[:REL]


def assemble(gather, own, row, col, corner, out):
    sources = jnp.concatenate([own[...], row[...], col[...], corner[...]], axis=0)
    out[...] = dot(gather[...], sources).astype(BF)


def merge_forward(gather, own, row, col, corner, w_merge, w_qkv, fine_out, coarse_out, queries_out, pairs_out):
    sources = jnp.concatenate([own[...], row[...], col[...], corner[...]], axis=0)
    fine = dot(gather[...], sources)
    fine_out[...] = fine.astype(BF)
    quarter = [fine[TOK * d : TOK * (d + 1)] for d in range(4)]
    mean = sum(jnp.sum(q, axis=-1, keepdims=True) for q in quarter) * (1.0 / 768)
    centred = [q - mean for q in quarter]
    spread = sum(jnp.sum(c * c, axis=-1, keepdims=True) for c in centred) * (1.0 / 768)
    rstd = lax.rsqrt(spread + EPS)
    coarse = jnp.zeros((TOK, 384), F32)
    for d in range(4):
        coarse = coarse + dot((centred[d] * rstd).astype(BF), w_merge[192 * d : 192 * d + 192, :])
    coarse = coarse.astype(BF)
    coarse_out[...] = coarse
    normed, _ = normalise(coarse.astype(F32), 384)
    projected = dot(normed.astype(BF), w_qkv[...])
    queries_out[...] = projected[:, :384].astype(BF)
    pairs_out[...] = projected[:, 384:].astype(BF)


def coarse_middle(parity, queries_in, pairs_in, far_in, coarse_in, fine, upstream, table, w_proj, w_split, result_out, input_back_out, own_back_out, far_back_out, packed_out, attended, weights_ref, dattended, packed, totals):
    pairs = pairs_in[...].astype(F32)
    far = far_in[...].astype(F32)
    queries32 = queries_in[...].astype(F32)
    joined = []
    first = parity[0] == 0
    ones = jnp.ones((TOK, 128), BF)
    lanes = lax.broadcasted_iota(jnp.int32, (24, 128), 1)
    for w in range(NWC):
        joined.append(
            jnp.concatenate([pairs[HALF * w : HALF * w + HALF], far[HALF * w : HALF * w + HALF]], axis=0).astype(BF)
        )
    for w in range(NWC):
        for start in range(0, 12, BATCH):
            stripes_of(table[0, w, start : start + BATCH], totals.at[start : start + BATCH])
        for group in range(3):
            queries = queries32[HALF * w : HALF * w + HALF, 128 * group : 128 * group + 128]
            keys = joined[w][:, 128 * group : 128 * group + 128]
            values = joined[w][:, 384 + 128 * group : 384 + 128 * group + 128]
            bias = []
            for h in range(4):
                stripe = totals[4 * group + h]
                near = rotated(stripe, -84, 1)[:, :128]
                other = jnp.where(first, rotated(stripe, -84, 1), rotated(stripe, 60, 1))[:, :256]
                for m in range(3):
                    offset = 48 - 24 * m
                    left = rotated(near, -offset, 1)
                    right = rotated(other, -offset, 1)[:, :TOK]
                    left = jnp.where(lanes < HALF, left, right[:, :128])
                    bias.append(jnp.concatenate([left, right[:, 128:]], axis=1))
            bias = jnp.concatenate(bias, axis=0)
            scores = dot_nt(head_stack(queries, 4), keys) * SCALE + bias
            rounded, inverse, weights = softmax(scores, ones)
            weights_ref[w, group] = weights
            total = head_sum(dot(rounded, values) * inverse, 4)
            attended[HALF * w : HALF * w + HALF, 128 * group : 128 * group + 128] = total
    coarse32 = coarse_in[...].astype(F32)
    coarse_out = (coarse32 + dot(attended[...].astype(BF), w_proj[...])).astype(BF)
    normed, rstd = normalise(coarse_out.astype(F32), 384)
    normed_b = normed.astype(BF)
    back = jnp.zeros((TOK, 384), F32)
    for d in range(4):
        part = w_split[:, 192 * d : 192 * d + 192]
        up = upstream[TOK * d : TOK * d + TOK, :]
        widened = dot(normed_b, part)
        result_out[TOK * d : TOK * d + TOK, :] = (fine[TOK * d : TOK * d + TOK, :].astype(F32) + widened).astype(BF)
        back = back + dot_nt(up, part)
    back = back.astype(BF).astype(F32)
    input_back = normalise_back(back, normed, rstd, 384).astype(BF)
    input_back_out[...] = input_back
    dattended[...] = dot_nt(input_back, w_proj[...]).astype(BF).astype(F32)
    for w in range(NWC):
        for group in range(3):
            queries = queries32[HALF * w : HALF * w + HALF, 128 * group : 128 * group + 128]
            keys = joined[w][:, 128 * group : 128 * group + 128]
            values = joined[w][:, 384 + 128 * group : 384 + 128 * group + 128]
            grad = dattended[HALF * w : HALF * w + HALF, 128 * group : 128 * group + 128]
            queries = head_stack(queries, 4)
            grad = head_stack(grad, 4)
            weights = weights_ref[w, group]
            dscores = scores_back(weights, dot_nt(grad, values), ones)
            ds = dscores.astype(BF)
            dq = head_sum(dot(ds, keys), 4)
            dk = dot_tn(ds, queries)
            dv = dot_tn(weights, grad)
            blank = jnp.zeros((24, 256 - TOK), F32)
            for h in range(4):
                near = jnp.zeros((24, 128), F32)
                other = jnp.zeros((24, 256), F32)
                for m in range(3):
                    offset = 48 - 24 * m
                    block = dscores[HALF * h + 24 * m : HALF * h + 24 * m + 24]
                    left = jnp.where(lanes < HALF, block[:, :128], 0.0)
                    right = jnp.concatenate([block[:, :128] - left, block[:, 128:], blank], axis=1)
                    near = near + rotated(left, offset, 1)
                    other = other + rotated(right, offset - HALF, 1)
                blank_lanes = jnp.zeros((24, LANES - 128), F32)
                near = rotated(jnp.concatenate([near, blank_lanes], axis=1), 84, 1)
                other = jnp.concatenate([other[:, :128], blank_lanes], axis=1)
                other = jnp.where(first, rotated(other, 156, 1), rotated(other, 12, 1))
                totals[12 * w + 4 * group + h] = near + other
            part = slice(HALF * w, HALF * w + HALF)
            cols = slice(128 * group, 128 * group + 128)
            own_back_out[part, cols] = dq * SCALE
            own_back_out[part, 384 + 128 * group : 384 + 128 * group + 128] = dk[:HALF] * SCALE
            own_back_out[part, 768 + 128 * group : 768 + 128 * group + 128] = dv[:HALF]
            far_back_out[part, cols] = (dk[HALF:] * SCALE).astype(BF)
            far_back_out[part, 384 + 128 * group : 384 + 128 * group + 128] = dv[HALF:].astype(BF)
    pack_tables(totals, packed)
    packed_out[...] = packed[...].astype(BF)


def merge_backward(send, own_back, returned, coarse_in, input_back, fine, upstream, w_merge, w_qkv, own_out, row_out, col_out, corner_out):
    returned32 = returned[...].astype(F32)
    dq = own_back[:, :384].astype(BF)
    dkv = (own_back[:, 384:] + returned32).astype(BF)
    dnormed = dot_nt(dq, w_qkv[:, :384]) + dot_nt(dkv, w_qkv[:, 384:])
    dnormed = dnormed.astype(BF).astype(F32)
    normed, rstd = normalise(coarse_in[...].astype(F32), 384)
    dx = normalise_back(dnormed, normed, rstd, 384).astype(BF)
    dcoarse = (input_back[...].astype(F32) + dx.astype(F32)).astype(BF)
    quarter = [fine[TOK * d : TOK * (d + 1), :].astype(F32) for d in range(4)]
    mean = sum(jnp.sum(q, axis=-1, keepdims=True) for q in quarter) * (1.0 / 768)
    centred = [q - mean for q in quarter]
    spread = sum(jnp.sum(c * c, axis=-1, keepdims=True) for c in centred) * (1.0 / 768)
    rstd = lax.rsqrt(spread + EPS)
    normed = [c * rstd for c in centred]
    dmerged = [
        dot_nt(dcoarse, w_merge[192 * d : 192 * d + 192, :]).astype(BF).astype(F32) for d in range(4)
    ]
    first = sum(jnp.sum(g, axis=-1, keepdims=True) for g in dmerged) * (1.0 / 768)
    second = sum(jnp.sum(g * n, axis=-1, keepdims=True) for g, n in zip(dmerged, normed)) * (1.0 / 768)
    for d in range(4):
        dfine = (rstd * (dmerged[d] - first - normed[d] * second)).astype(BF).astype(F32)
        up = upstream[TOK * d : TOK * (d + 1), :].astype(F32)
        own_out[TOK * d : TOK * (d + 1), :] = (up + dfine).astype(BF)
    pieces = dot(send[...], own_out[...]).astype(BF)
    row_out[...] = pieces[:ROW_PIECE]
    col_out[...] = pieces[ROW_PIECE : ROW_PIECE + COL_PIECE]
    corner_out[...] = pieces[ROW_PIECE + COL_PIECE :]


def moved(value, lat, lon):
    lats, lons = lax.axis_size("lat"), lax.axis_size("lon")
    if lat == 0:
        pairs = [(source, (source + lon) % lons) for source in range(lons)]
        return lax.ppermute(value, "lon", pairs)
    if lon == 0:
        pairs = [(source, (source + lat) % lats) for source in range(lats)]
        return lax.ppermute(value, "lat", pairs)
    pairs = [
        (a * lons + b, (a + lat) % lats * lons + (b + lon) % lons)
        for a in range(lats)
        for b in range(lons)
    ]
    return lax.ppermute(value, ("lat", "lon"), pairs)


def exchanged(pieces, step):
    row, col, corner = pieces
    return moved(row, step, 0), moved(col, 0, step), moved(corner, step, step)


class Arriving:
    def __init__(self, source, target, semaphore):
        self.copy = pltpu.make_async_copy(source, target, semaphore)
        self.target = target
        self.waiting = True
        self.copy.start()

    def __getitem__(self, index):
        if self.waiting:
            self.copy.wait()
            self.waiting = False
        return self.target[index]


def call(kernel, out_shapes, *operands, scratch=(), scalars=0, late=(), hbm_out=()):
    shapes = [jax.ShapeDtypeStruct(shape, dtype) for shape, dtype in out_shapes]
    scalar, array = pl.BlockSpec(memory_space=pltpu.SMEM), pl.BlockSpec(memory_space=pltpu.VMEM)
    remote = pl.BlockSpec(memory_space=pltpu.HBM)
    count = len(operands)
    order = [i for i in range(scalars, count) if i not in late] + list(late)
    landing = [pltpu.VMEM(operands[i].shape, operands[i].dtype) for i in order]
    landing.append(pltpu.SemaphoreType.DMA((len(order),)))

    def whole(*refs):
        inputs, others = list(refs[:count]), refs[count : len(refs) - len(landing)]
        spaces = refs[len(refs) - len(landing) :]
        for k, i in enumerate(order):
            inputs[i] = Arriving(inputs[i], spaces[k], spaces[-1].at[k])
        kernel(*inputs, *others)

    return pl.pallas_call(
        whole,
        out_shape=shapes,
        in_specs=[scalar if i < scalars else remote for i in range(count)],
        out_specs=[remote if i in hbm_out else array for i in range(len(shapes))],
        scratch_shapes=list(scratch) + landing,
        compiler_params=pltpu.CompilerParams(vmem_limit_bytes=VMEM),
        name=kernel.__name__,
    )(*operands)


def swapped(value, step):
    pairs = [(source, source ^ step) for source in range(lax.axis_size("lon"))]
    return lax.ppermute(value, "lon", pairs)


def on_device(fields, upstream, bias_f, bias_c, w_qkv_f, w_proj_f, w_merge, w_qkv_c, w_proj_c, w_split):
    windows, quartets = window_order(), quartet_order()
    last = (lax.axis_index("lat") == lax.axis_size("lat") - 1).astype(jnp.int32).reshape(1)
    odd = lax.axis_index("lon") % 2
    parity = odd.astype(jnp.int32).reshape(1)

    fields = fields.transpose(0, 2, 1, 3)
    upstream = upstream.transpose(0, 2, 1, 3).reshape(576, 192)
    natural = natural_order()
    place = {cell: index for index, cell in enumerate(natural)}
    pieces = call(cut, [((2, 6, 3, 192), BF), ((2, 6, LAT, 192), BF), ((2, 6, 3, 192), BF)], fields)
    row, col, corner = exchanged(pieces, -1)
    (up,) = call(
        reordered, [((576, 192), BF)], one_hot([place[cell] for cell in quartets], 576), upstream
    )
    piece_shapes = [((size, 192), BF) for size in (ROW_PIECE, COL_PIECE, CORNER)]
    x, qkv, weights, mixed, *pieces = call(
        fine_forward,
        [((576, 192), BF), ((576, 768), BF), ((NWF, 6 * TOK, TOK), BF), ((576, 192), BF)] + piece_shapes,
        last, window_table(), last_window_table(), fields, row, col, corner, bias_f, w_qkv_f, w_proj_f,
        scratch=[
            pltpu.VMEM((2, LON, LAT + 8, 192), F32),
            pltpu.VMEM((6, 24, LANES), F32),
            pltpu.VMEM((576, 192), BF),
            pltpu.VMEM((576, 768), BF),
            pltpu.VMEM((NWF, 6 * TOK, TOK), BF),
            pltpu.SemaphoreType.DMA((6,)),
        ],
        late=(8, 7, 9, 2),
        hbm_out=(0, 1, 2),
        scalars=1,
    )
    row, col, corner = exchanged(pieces, 1)
    fine, coarse_in, queries, pairs = call(
        merge_forward,
        [((576, 192), BF), ((TOK, 384), BF), ((TOK, 384), BF), ((TOK, 768), BF)],
        gather_table(windows, back_pieces(), unrolled_from(quartets)),
        mixed, row, col, corner, w_merge, w_qkv_c,
        late=(5, 6),
    )
    far = swapped(pairs, 1)
    result_q, input_back, own_back, far_back, packed_c = call(
        coarse_middle,
        [
            ((576, 192), BF),
            ((TOK, 384), BF),
            ((TOK, 1152), F32),
            ((TOK, 768), BF),
            ((PACKED, 128), BF),
        ],
        parity, queries, pairs, far, coarse_in, fine, up, bias_c, w_proj_c, w_split,
        scratch=[
            pltpu.VMEM((TOK, 384), F32),
            pltpu.VMEM((NWC, 3, 4 * HALF, TOK), BF),
            pltpu.VMEM((TOK, 384), F32),
            pltpu.VMEM((PACKED, 128), F32),
            pltpu.VMEM((24, 24, LANES), F32),
        ],
        scalars=1,
        late=(4, 8, 9, 5, 6),
    )
    returned = swapped(far_back, 1)
    fine_back, *pieces = call(
        merge_backward,
        [((576, 192), BF)] + piece_shapes,
        send_table(quartets, forward_pieces()),
        own_back, returned, coarse_in, input_back, fine, up, w_merge, w_qkv_c,
        late=(3, 4, 5, 7, 6, 0),
    )
    row, col, corner = exchanged(pieces, -1)
    grad_rolled, *rest = call(
        fine_backward,
        [((576, 192), BF)] + piece_shapes + [((PACKED, 128), BF)],
        gather_table(quartets, forward_pieces(), rolled_from(windows)),
        last_window_table(),
        fine_back, row, col, corner, x, qkv, weights, w_qkv_f, w_proj_f,
        scratch=[
            pltpu.VMEM((576, 768), BF),
            pltpu.VMEM((PACKED, 128), F32),
            pltpu.VMEM((24, 24, LANES), F32),
        ],
        late=(10, 7, 8, 9, 6, 1),
    )
    *pieces, packed_f = rest

    row, col, corner = exchanged(pieces, 1)
    sent = jnp.where(odd == 0, packed_f, packed_c)
    kept = jnp.where(odd == 0, packed_c, packed_f)
    kept = kept.astype(F32) + swapped(sent, 1).astype(F32)
    far = lax.axis_index("lon") // 2 % 2
    low, high = kept[: PACKED // 2], kept[PACKED // 2 :]
    sent = jnp.where(far == 0, high, low).astype(BF)
    kept = jnp.where(far == 0, low, high)
    kept = (kept + swapped(sent, 2).astype(F32)).astype(BF)
    recv = swapped(kept, 4)
    kept, recv, row, col, corner = lax.optimization_barrier((kept, recv, row, col, corner))
    kept = (kept.astype(F32) + recv.astype(F32)).astype(BF)
    recv = swapped(kept, 12)
    (grad_fields,) = call(
        assemble,
        [((576, 192), BF)],
        gather_table(windows, back_pieces(), unrolled_from(natural)),
        grad_rolled, row, col, corner,
    )
    kept, recv, grad_fields = lax.optimization_barrier((kept, recv, grad_fields))
    kept = (kept.astype(F32) + recv.astype(F32)).astype(BF)
    recv = swapped(kept, 16)
    place = {cell: index for index, cell in enumerate(quartets)}
    (result,) = call(
        reordered, [((576, 192), BF)], one_hot([place[cell] for cell in natural], 576), result_q
    )
    kept, recv, result = lax.optimization_barrier((kept, recv, result))
    kept = (kept.astype(F32) + recv.astype(F32)).astype(BF)
    kept_far = swapped(kept, 2)
    grad_bias_f, grad_bias_c = call(
        unpack,
        [((1, 6, REL, NWF, TOK), F32), ((1, 12, REL, NWC, TOK), F32)],
        jnp.stack([odd, far]).astype(jnp.int32), kept, kept_far, swapped(kept, 1), swapped(kept_far, 1),
        scalars=1,
    )
    grad_bias_f = grad_bias_f.transpose(0, 3, 1, 2, 4)
    grad_bias_c = grad_bias_c.transpose(0, 3, 1, 2, 4)
    result = result.reshape(2, LON, LAT, 192).transpose(0, 2, 1, 3)
    grad_fields = grad_fields.reshape(2, LON, LAT, 192).transpose(0, 2, 1, 3)
    return (result, grad_fields, grad_bias_f, grad_bias_c)


def solution(mesh):
    grid = P(None, "lat", "lon", None)
    table = P(None, "lat", None, None, None)
    return jax.shard_map(
        on_device,
        mesh=mesh,
        in_specs=(grid, grid, table, table, P(), P(), P(), P(), P(), P()),
        out_specs=(grid, grid, table, table),
        check_vma=False,
    )
```

```python
import math

import jax
import jax.numpy as jnp
import numpy as np
from jax import lax
from jax.experimental import pallas as pl
from jax.experimental.pallas import tpu as pltpu
from jax.sharding import PartitionSpec as P

WIN_Z = 2
WIN_LAT = 6
WIN_LON = 12
ROWS = WIN_Z * WIN_LAT
TOK = ROWS * WIN_LON
HALF = TOK // 2
REL = 2 * WIN_LON - 1
WIDE = REL * ROWS
EPS = 1e-05
MASKED = -1000000000.0
HEAD = 32
SCALE = 1.0 / math.sqrt(HEAD)
LAT = 24
LON = 12
NWF = LAT // WIN_LAT
NWC = LAT // 2 // WIN_LAT
BF = jnp.bfloat16
F32 = jnp.float32
ROW_PIECE, COL_PIECE, CORNER = 48, 288, 48
VMEM = 56 * 1024 * 1024
TABLE = 24 + 3
LANES = 384
PACKED = 24 * TABLE + 8
BATCH = 4


def natural_order():
    return [(z, i, j) for z in range(2) for j in range(LON) for i in range(LAT)]


def window_order():
    return [
        (z, WIN_LAT * w + l, n)
        for w in range(NWF)
        for n in range(LON)
        for z in range(2)
        for l in range(WIN_LAT)
    ]


def quartet_order():
    return [
        (z, 2 * (WIN_LAT * w + l) + di, 2 * n + dj)
        for di in range(2)
        for dj in range(2)
        for w in range(NWC)
        for n in range(LON // 2)
        for z in range(2)
        for l in range(WIN_LAT)
    ]


def one_hot(rows, columns):
    table = np.zeros((len(rows), columns), np.float32)
    for row, column in enumerate(rows):
        if column is not None:
            table[row, column] = 1.0
    return jnp.asarray(table, BF)


def forward_pieces():
    row = [(z, i, j) for z in range(2) for i in range(3) for j in range(6, LON)]
    col = [(z, i, j) for z in range(2) for i in range(LAT) for j in range(6)]
    corner = [(z, i, j) for z in range(2) for i in range(3) for j in range(6)]
    return row, col, corner


def back_pieces():
    row = [(z, i, j) for z in range(2) for i in range(LAT - 3, LAT) for j in range(6)]
    col = [cell for cell in window_order() if cell[2] >= 6]
    corner = [(z, i, j) for z in range(2) for i in range(LAT - 3, LAT) for j in range(6, LON)]
    return row, col, corner


def padded_pieces(pieces):
    sizes = (ROW_PIECE, COL_PIECE, CORNER)
    return [cells + [None] * (size - len(cells)) for cells, size in zip(pieces, sizes)]


def send_table(own_order, pieces):
    place = {cell: index for index, cell in enumerate(own_order)}
    cells = sum(padded_pieces(pieces), [])
    return one_hot([None if cell is None else place[cell] for cell in cells], len(own_order))


def gather_table(own_order, pieces, wanted):
    tables = [{cell: index for index, cell in enumerate(own_order)}]
    starts = [0]
    for cells in pieces:
        tables.append({cell: index for index, cell in enumerate(cells)})
    starts = [0, len(own_order), len(own_order) + ROW_PIECE, len(own_order) + ROW_PIECE + COL_PIECE]
    total = len(own_order) + ROW_PIECE + COL_PIECE + CORNER
    rows = []
    for entry in wanted:
        rows.append(None if entry is None else starts[entry[0]] + tables[entry[0]][entry[1]])
    return one_hot(rows, total)


def window_start(w):
    return (WIN_LAT * w + WIN_LAT // 2) // 8 * 8 if w < NWF - 1 else LAT - 8


def window_table():
    rows = []
    for w in range(NWF):
        offset = WIN_LAT * w + WIN_LAT // 2 - window_start(w)
        for n in range(LON):
            for z in range(2):
                for l in range(WIN_LAT):
                    rows.append(((1 - z) * LON + n) * 16 + offset + l)
    return one_hot(rows, 2 * LON * 16)


def last_window_table():
    place = {cell: index for index, cell in enumerate(window_order()[-TOK:])}
    row, _, corner = padded_pieces(back_pieces())
    return one_hot([None if cell is None else place[cell] for cell in row + corner], TOK)


def rolled_from(cells):
    wanted = []
    for z, i, j in cells:
        z, i, j = 1 - z, i + 3, j + 6
        kind = (1 if i >= LAT else 0) + (2 if j >= LON else 0)
        wanted.append((kind, (z, i % LAT, j % LON)))
    return wanted


def unrolled_from(cells):
    wanted = []
    for cell in cells:
        z, i, j = cell
        z, i, j = 1 - z, i - 3, j - 6
        kind = (1 if i < 0 else 0) + (2 if j < 0 else 0)
        wanted.append((kind, (z, i % LAT, j % LON)))
    return wanted


def dot(a, b):
    return lax.dot_general(a, b, (((1,), (0,)), ((), ())), preferred_element_type=F32)


def dot_nt(a, b):
    return lax.dot_general(a, b, (((1,), (1,)), ((), ())), preferred_element_type=F32)


def dot_tn(a, b):
    return lax.dot_general(a, b, (((0,), (0,)), ((), ())), preferred_element_type=F32)


def normalise(values, count):
    mean = jnp.sum(values, axis=-1, keepdims=True) * (1.0 / count)
    centred = values - mean
    spread = jnp.sum(centred * centred, axis=-1, keepdims=True) * (1.0 / count)
    rstd = lax.rsqrt(spread + EPS)
    return centred * rstd, rstd


def normalise_back(cotangent, normed, rstd, count):
    first = jnp.sum(cotangent, axis=-1, keepdims=True) * (1.0 / count)
    second = jnp.sum(cotangent * normed, axis=-1, keepdims=True) * (1.0 / count)
    return rstd * (cotangent - first - normed * second)


def head_stack(values, heads):
    lanes = lax.broadcasted_iota(jnp.int32, values.shape, 1) // HEAD
    return jnp.concatenate([jnp.where(lanes == h, values, 0.0) for h in range(heads)], axis=0).astype(BF)


def head_sum(stacked, heads):
    rows = stacked.shape[0] // heads
    lanes = lax.broadcasted_iota(jnp.int32, (rows, 128), 1) // HEAD
    total = stacked[:rows]
    for h in range(1, heads):
        total = jnp.where(lanes == h, stacked[h * rows : (h + 1) * rows], total)
    return jnp.where(lanes < heads, total, 0.0)


def softmax(scores, ones):
    highest = jnp.max(scores, axis=-1, keepdims=True)
    powers = jnp.exp(scores - highest)
    rounded = powers.astype(BF)
    inverse = 1.0 / dot(rounded, ones)
    weights = powers * jnp.concatenate([inverse, inverse[:, : TOK - 128]], axis=1)
    return rounded, inverse, weights.astype(BF)


def scores_back(weights, dweights, ones):
    weights32 = weights.astype(F32)
    product = weights32 * dweights
    total = dot(product.astype(BF), ones)
    return product - weights32 * jnp.concatenate([total, total[:, : TOK - 128]], axis=1)


def rotated(value, shift, axis):
    size = value.shape[axis]
    return pltpu.roll(value, shift % size, axis)


def sheared(value, index, bits, lanes):
    for bit in range(bits):
        value = jnp.where((index >> bit) & 1 == 1, rotated(value, lanes << bit, 2), value)
    return value


def strided(value):
    tiles = []
    for start in range(0, value.shape[1], 8):
        tile = pltpu.roll(value[:, start : start + 8], 0, 2, stride=ROWS, stride_axis=1)
        tiles.append(rotated(tile, ROWS * start, 2))
    return jnp.concatenate(tiles, axis=1)


def raised(value, amount, steps):
    for step in steps:
        value = jnp.where(amount & step != 0, rotated(value, step, 1), value)
    return value


def stripes_of(table, stripes_out):
    heads = table.shape[0]
    index = lax.broadcasted_iota(jnp.int32, (1, 24, LANES), 1)
    amount = (lax.broadcasted_iota(jnp.int32, (1, 8, LANES), 2) // ROWS + 10) & 31
    table = jnp.concatenate([table, jnp.zeros((heads, REL, LANES - TOK), F32)], axis=2)
    table = jnp.concatenate([table, jnp.zeros((heads, 1, LANES), F32)], axis=1)
    table = rotated(sheared(table, index, 5, -ROWS), 22 * ROWS, 2)
    tiles = [table[:, 0:8], table[:, 8:16], table[:, 16:24], jnp.zeros((heads, 8, LANES), F32)]
    tiles = [jnp.where(amount & 16 != 0, tiles[k - 2], tiles[k]) for k in range(4)]
    tiles = [jnp.where(amount & 8 != 0, tiles[k - 1], tiles[k]) for k in range(4)]
    stripes = jnp.concatenate([tiles[3], tiles[0], tiles[1]], axis=1)
    stripes = raised(stripes, amount[:, :1], (4, 2, 1))[:, 8:]
    stripes = sheared(stripes, index[:, :16], 4, -ROWS)
    stripes = jnp.where(index[:, :16] < ROWS, stripes, 0.0)
    stripes = jnp.concatenate([stripes, jnp.zeros((heads, 8, LANES), F32)], axis=1)
    stripes_out[...] = stripes + rotated(rotated(stripes, ROWS, 2), ROWS, 1)


def stripes_back(stripes):
    heads = stripes.shape[0]
    index = lax.broadcasted_iota(jnp.int32, (1, 16, LANES), 1)
    amount = (22 - lax.broadcasted_iota(jnp.int32, (1, 8, LANES), 2) // ROWS) & 31
    stripes = stripes + rotated(rotated(stripes, -ROWS, 2), ROWS, 1)
    stripes = strided(jnp.where(index < ROWS, stripes[:, :16], 0.0))
    blank = jnp.zeros((heads, 8, LANES), F32)
    stripes = raised(jnp.concatenate([stripes, blank], axis=1), amount[:, :1], (1, 2, 4))
    tiles = [stripes[:, 0:8], stripes[:, 8:16], stripes[:, 16:24], blank]
    tiles = [jnp.where(amount & 8 != 0, tiles[k - 1], tiles[k]) for k in range(4)]
    tiles = [jnp.where(amount & 16 != 0, tiles[k - 2], tiles[k]) for k in range(3)]
    return rotated(strided(jnp.concatenate(tiles, axis=1)), -22 * ROWS, 2)


def expand(table, stripes_out):
    _, heads, _, windows, _ = table.shape
    batch = BATCH if heads % BATCH == 0 else 3
    for w in range(windows):
        for start in range(0, heads, batch):
            place = stripes_out.at[heads * w + start : heads * w + start + batch]
            stripes_of(table[0, start : start + batch, :, w, :], place)


def pack(totals, packed_out, packed):
    pack_tables(totals, packed)
    packed_out[...] = packed[...].astype(BF)


def pack_tables(totals, packed):
    packed[24 * TABLE :, :] = jnp.zeros((PACKED - 24 * TABLE, 128), F32)
    rest = jnp.zeros((24, 128), F32)
    for start in range(0, 24, BATCH):
        tables = stripes_back(totals[start : start + BATCH])
        for head in range(start, start + BATCH):
            rest = pack_table(tables[head - start], head, packed, rest)


def pack_table(table, head, packed, rest):
    packed[24 * head : 24 * head + 24, :] = table[:, :128]
    rest = rest + rotated(table[:, 128:256], 16 * (head % 8), 1)
    if head % 8 == 7:
        start = 24 * (24 + head // 8)
        packed[start : start + 24, :] = rest
        rest = jnp.zeros((24, 128), F32)
    return rest


def mask_of(last_row):
    first = lax.broadcasted_iota(jnp.int32, (24, LANES), 0) % ROWS
    second = lax.broadcasted_iota(jnp.int32, (24, LANES), 1) % ROWS
    half = WIN_Z // 2
    level = (first // WIN_LAT >= WIN_Z - half) != (second // WIN_LAT >= WIN_Z - half)
    if last_row is not None:
        half = WIN_LAT // 2
        row = (first % WIN_LAT >= WIN_LAT - half) != (second % WIN_LAT >= WIN_LAT - half)
        level = level | (row & (last_row == 1))
    return jnp.where(level, MASKED, 0.0).astype(F32)


def padded_lanes(weights):
    blocks = []
    for start in range(0, weights.shape[1], 192):
        blocks += [weights[:, start : start + 192], jnp.zeros((weights.shape[0], 64), weights.dtype)]
    return jnp.concatenate(blocks, axis=1)


def cut(fields, row_out, col_out, corner_out):
    row_out[...] = fields[:, 6:, :3]
    col_out[...] = fields[:, :6]
    corner_out[...] = fields[:, :6, :3]


def fine_forward(last, gather, send, fields, row, col, corner, stripes, w_qkv_in, w_proj_in, x_out, qkv_out, weights_out, mixed_out, row_out, col_out, corner_out, rolled, x_s, qkv_s, weights_s, sems):
    rolled[:, :, LAT:, :] = jnp.zeros((2, LON, 8, 192), F32)
    rolled[:, :6, :LAT, :] = fields[:, 6:].astype(F32)
    rolled[:, 6:, :LAT, :] = col[...].astype(F32)
    rolled[:, :6, LAT : LAT + 3, :] = row[...].astype(F32)
    rolled[:, 6:, LAT : LAT + 3, :] = corner[...].astype(F32)
    x = []
    for w in range(NWF):
        start = window_start(w)
        sources = rolled[:, :, start : start + 16].reshape(2 * LON * 16, 192).astype(BF)
        x.append(dot(gather[TOK * w : TOK * w + TOK, :], sources))
    x = jnp.concatenate(x, axis=0)
    x_s[...] = x.astype(BF)
    copies = [pltpu.make_async_copy(x_s, x_out, sems.at[0])]
    copies[-1].start()
    normed, _ = normalise(x, 192)
    qkv_s[...] = dot(normed.astype(BF), padded_lanes(w_qkv_in[...])).astype(BF)
    copies.append(pltpu.make_async_copy(qkv_s, qkv_out, sems.at[1]))
    copies[-1].start()
    w_proj = jnp.concatenate([w_proj_in[...], jnp.zeros((64, 192), BF)], axis=0)
    ones = jnp.ones((TOK, 128), BF)
    level_mask = mask_of(None)
    last_mask = mask_of(last[0])
    sent = []
    for w in range(NWF):
        rows = pl.ds(w * TOK, TOK)
        blended = []
        for group, heads in ((0, 4), (1, 2)):
            queries = qkv_s[rows, 128 * group : 128 * group + 128]
            keys = qkv_s[rows, 256 + 128 * group : 256 + 128 * group + 128]
            values = qkv_s[rows, 512 + 128 * group : 512 + 128 * group + 128]
            bias = []
            for h in range(heads):
                stripe = stripes[6 * w + 4 * group + h] + (last_mask if w == NWF - 1 else level_mask)
                bias += [rotated(stripe, -(11 - 2 * m) * ROWS, 1)[:, :TOK] for m in range(6)]
            bias = jnp.concatenate(bias, axis=0)
            queries = head_stack(queries.astype(F32), heads)
            rounded, inverse, weights = softmax(dot_nt(queries, keys) * SCALE + bias, ones)
            weights_s[w, 4 * TOK * group : 4 * TOK * group + heads * TOK, :] = weights
            blended.append(head_sum(dot(rounded, values) * inverse, heads))
        blended = jnp.concatenate(blended, axis=1).astype(BF)
        mixed = x[w * TOK : (w + 1) * TOK] + dot(blended, w_proj)
        sent.append(mixed[HALF:])
        mixed_out[rows, :] = mixed.astype(BF)
        copies.append(pltpu.make_async_copy(weights_s.at[w], weights_out.at[w], sems.at[2 + w]))
        copies[-1].start()
    col_out[...] = jnp.concatenate(sent, axis=0).astype(BF)
    pieces = dot(send[...], mixed_out[TOK * (NWF - 1) :, :]).astype(BF)
    row_out[...] = pieces[:ROW_PIECE]
    corner_out[...] = pieces[ROW_PIECE:]
    for copy in copies:
        copy.wait()


def fine_backward(gather, send, own, row, col, corner, x, qkv, weights_in, w_qkv_in, w_proj_in, own_out, row_out, col_out, corner_out, packed_out, dqkv, packed, totals):
    sources = jnp.concatenate([own[...], row[...], col[...], corner[...]], axis=0)
    dmix = dot(gather[...], sources).astype(BF)
    w_proj = jnp.concatenate([w_proj_in[...], jnp.zeros((64, 192), BF)], axis=0)
    datt = dot_nt(dmix, w_proj).astype(BF)
    ones = jnp.ones((TOK, 128), BF)
    for w in range(NWF):
        rows = pl.ds(w * TOK, TOK)
        for group, heads in ((0, 4), (1, 2)):
            lanes = slice(128 * group, 128 * group + 128)
            queries = qkv[rows, 128 * group : 128 * group + 128]
            keys = qkv[rows, 256 + 128 * group : 256 + 128 * group + 128]
            values = qkv[rows, 512 + 128 * group : 512 + 128 * group + 128]
            grad = datt[w * TOK : (w + 1) * TOK, lanes]
            queries = head_stack(queries.astype(F32), heads)
            grad = head_stack(grad.astype(F32), heads)
            weights = weights_in[w, 4 * TOK * group : 4 * TOK * group + heads * TOK, :]
            dscores = scores_back(weights, dot_nt(grad, values), ones)
            ds = dscores.astype(BF)
            dq = head_sum(dot(ds, keys), heads)
            dk = dot_tn(ds, queries)
            dv = dot_tn(weights, grad)
            wide = jnp.concatenate([dscores, jnp.zeros((heads * TOK, LANES - TOK), F32)], axis=1)
            for h in range(heads):
                total = jnp.zeros((24, LANES), F32)
                for m in range(6):
                    block = wide[TOK * h + 24 * m : TOK * h + 24 * m + 24]
                    total = total + rotated(block, (11 - 2 * m) * ROWS, 1)
                totals[6 * w + 4 * group + h] = total
            dqkv[rows, 128 * group : 128 * group + 128] = (dq * SCALE).astype(BF)
            dqkv[rows, 256 + 128 * group : 256 + 128 * group + 128] = (dk * SCALE).astype(BF)
            dqkv[rows, 512 + 128 * group : 512 + 128 * group + 128] = dv.astype(BF)
    pack_tables(totals, packed)
    packed_out[...] = packed[...].astype(BF)
    dnormed = dot_nt(dqkv[...], padded_lanes(w_qkv_in[...])).astype(BF).astype(F32)
    normed, rstd = normalise(x[...].astype(F32), 192)
    dx = normalise_back(dnormed, normed, rstd, 192).astype(BF).astype(F32)
    grad_rolled = dmix.astype(F32) + dx
    own_out[...] = grad_rolled.astype(BF)
    sent = [grad_rolled[TOK * w + HALF : TOK * w + TOK] for w in range(NWF)]
    col_out[...] = jnp.concatenate(sent, axis=0).astype(BF)
    pieces = dot(send[...], own_out[TOK * (NWF - 1) :, :]).astype(BF)
    row_out[...] = pieces[:ROW_PIECE]
    corner_out[...] = pieces[ROW_PIECE:]


def reordered(gather, values, out):
    out[...] = dot(gather[...], values[...]).astype(BF)


def unpack(bits, kept, kept_far, other, other_far, fine_out, coarse_out):
    even, low = bits[0] == 0, bits[1] == 0
    halves = [part[...].astype(F32) for part in (kept, kept_far, other, other_far)]
    tables = []
    for near, far in (halves[:2], halves[2:]):
        tables.append(
            jnp.concatenate([jnp.where(low, near, far), jnp.where(low, far, near)], axis=0)
        )
    coarse = jnp.where(even, tables[0], tables[1])
    fine = jnp.where(even, tables[1], tables[0])
    for packed, out, heads in ((fine, fine_out, 6), (coarse, coarse_out, 12)):
        for head in range(24):
            rest = 24 * (24 + head // 8)
            rest = rotated(packed[rest : rest + 24], -16 * (head % 8), 1)[:, : TOK - 128]
            table = jnp.concatenate([packed[24 * head : 24 * head + 24], rest], axis=1)
            out[0, head % heads, :, head // heads, :] = table[:REL]


def assemble(gather, own, row, col, corner, out):
    sources = jnp.concatenate([own[...], row[...], col[...], corner[...]], axis=0)
    out[...] = dot(gather[...], sources).astype(BF)


def merge_forward(gather, own, row, col, corner, w_merge, w_qkv, fine_out, coarse_out, queries_out, pairs_out):
    sources = jnp.concatenate([own[...], row[...], col[...], corner[...]], axis=0)
    fine = dot(gather[...], sources)
    fine_out[...] = fine.astype(BF)
    quarter = [fine[TOK * d : TOK * (d + 1)] for d in range(4)]
    mean = sum(jnp.sum(q, axis=-1, keepdims=True) for q in quarter) * (1.0 / 768)
    centred = [q - mean for q in quarter]
    spread = sum(jnp.sum(c * c, axis=-1, keepdims=True) for c in centred) * (1.0 / 768)
    rstd = lax.rsqrt(spread + EPS)
    coarse = jnp.zeros((TOK, 384), F32)
    for d in range(4):
        coarse = coarse + dot((centred[d] * rstd).astype(BF), w_merge[192 * d : 192 * d + 192, :])
    coarse = coarse.astype(BF)
    coarse_out[...] = coarse
    normed, _ = normalise(coarse.astype(F32), 384)
    projected = dot(normed.astype(BF), w_qkv[...])
    queries_out[...] = projected[:, :384].astype(BF)
    pairs_out[...] = projected[:, 384:].astype(BF)


def coarse_middle(parity, queries_in, pairs_in, far_in, coarse_in, fine, upstream, stripes, w_proj, w_split, result_out, input_back_out, own_back_out, far_back_out, totals, attended, weights_ref, dattended):
    pairs = pairs_in[...].astype(F32)
    far = far_in[...].astype(F32)
    queries32 = queries_in[...].astype(F32)
    joined = []
    first = parity[0] == 0
    ones = jnp.ones((TOK, 128), BF)
    lanes = lax.broadcasted_iota(jnp.int32, (24, 128), 1)
    for w in range(NWC):
        joined.append(
            jnp.concatenate([pairs[HALF * w : HALF * w + HALF], far[HALF * w : HALF * w + HALF]], axis=0).astype(BF)
        )
    for w in range(NWC):
        for group in range(3):
            queries = queries32[HALF * w : HALF * w + HALF, 128 * group : 128 * group + 128]
            keys = joined[w][:, 128 * group : 128 * group + 128]
            values = joined[w][:, 384 + 128 * group : 384 + 128 * group + 128]
            bias = []
            for h in range(4):
                stripe = stripes[12 * w + 4 * group + h]
                near = rotated(stripe, -84, 1)[:, :128]
                other = jnp.where(first, rotated(stripe, -84, 1), rotated(stripe, 60, 1))[:, :256]
                for m in range(3):
                    offset = 48 - 24 * m
                    left = rotated(near, -offset, 1)
                    right = rotated(other, -offset, 1)[:, :TOK]
                    left = jnp.where(lanes < HALF, left, right[:, :128])
                    bias.append(jnp.concatenate([left, right[:, 128:]], axis=1))
            bias = jnp.concatenate(bias, axis=0)
            scores = dot_nt(head_stack(queries, 4), keys) * SCALE + bias
            rounded, inverse, weights = softmax(scores, ones)
            weights_ref[w, group] = weights
            total = head_sum(dot(rounded, values) * inverse, 4)
            attended[HALF * w : HALF * w + HALF, 128 * group : 128 * group + 128] = total
    coarse32 = coarse_in[...].astype(F32)
    coarse_out = (coarse32 + dot(attended[...].astype(BF), w_proj[...])).astype(BF)
    normed, rstd = normalise(coarse_out.astype(F32), 384)
    normed_b = normed.astype(BF)
    back = jnp.zeros((TOK, 384), F32)
    for d in range(4):
        part = w_split[:, 192 * d : 192 * d + 192]
        up = upstream[TOK * d : TOK * d + TOK, :]
        widened = dot(normed_b, part)
        result_out[TOK * d : TOK * d + TOK, :] = (fine[TOK * d : TOK * d + TOK, :].astype(F32) + widened).astype(BF)
        back = back + dot_nt(up, part)
    back = back.astype(BF).astype(F32)
    input_back = normalise_back(back, normed, rstd, 384).astype(BF)
    input_back_out[...] = input_back
    dattended[...] = dot_nt(input_back, w_proj[...]).astype(BF).astype(F32)
    for w in range(NWC):
        for group in range(3):
            queries = queries32[HALF * w : HALF * w + HALF, 128 * group : 128 * group + 128]
            keys = joined[w][:, 128 * group : 128 * group + 128]
            values = joined[w][:, 384 + 128 * group : 384 + 128 * group + 128]
            grad = dattended[HALF * w : HALF * w + HALF, 128 * group : 128 * group + 128]
            queries = head_stack(queries, 4)
            grad = head_stack(grad, 4)
            weights = weights_ref[w, group]
            dscores = scores_back(weights, dot_nt(grad, values), ones)
            ds = dscores.astype(BF)
            dq = head_sum(dot(ds, keys), 4)
            dk = dot_tn(ds, queries)
            dv = dot_tn(weights, grad)
            blank = jnp.zeros((24, 256 - TOK), F32)
            for h in range(4):
                near = jnp.zeros((24, 128), F32)
                other = jnp.zeros((24, 256), F32)
                for m in range(3):
                    offset = 48 - 24 * m
                    block = dscores[HALF * h + 24 * m : HALF * h + 24 * m + 24]
                    left = jnp.where(lanes < HALF, block[:, :128], 0.0)
                    right = jnp.concatenate([block[:, :128] - left, block[:, 128:], blank], axis=1)
                    near = near + rotated(left, offset, 1)
                    other = other + rotated(right, offset - HALF, 1)
                blank_lanes = jnp.zeros((24, LANES - 128), F32)
                near = rotated(jnp.concatenate([near, blank_lanes], axis=1), 84, 1)
                other = jnp.concatenate([other[:, :128], blank_lanes], axis=1)
                other = jnp.where(first, rotated(other, 156, 1), rotated(other, 12, 1))
                totals[12 * w + 4 * group + h] = near + other
            part = slice(HALF * w, HALF * w + HALF)
            cols = slice(128 * group, 128 * group + 128)
            own_back_out[part, cols] = dq * SCALE
            own_back_out[part, 384 + 128 * group : 384 + 128 * group + 128] = dk[:HALF] * SCALE
            own_back_out[part, 768 + 128 * group : 768 + 128 * group + 128] = dv[:HALF]
            far_back_out[part, cols] = (dk[HALF:] * SCALE).astype(BF)
            far_back_out[part, 384 + 128 * group : 384 + 128 * group + 128] = dv[HALF:].astype(BF)


def merge_backward(send, own_back, returned, coarse_in, input_back, fine, upstream, w_merge, w_qkv, own_out, row_out, col_out, corner_out):
    returned32 = returned[...].astype(F32)
    dq = own_back[:, :384].astype(BF)
    dkv = (own_back[:, 384:] + returned32).astype(BF)
    dnormed = dot_nt(dq, w_qkv[:, :384]) + dot_nt(dkv, w_qkv[:, 384:])
    dnormed = dnormed.astype(BF).astype(F32)
    normed, rstd = normalise(coarse_in[...].astype(F32), 384)
    dx = normalise_back(dnormed, normed, rstd, 384).astype(BF)
    dcoarse = (input_back[...].astype(F32) + dx.astype(F32)).astype(BF)
    quarter = [fine[TOK * d : TOK * (d + 1), :].astype(F32) for d in range(4)]
    mean = sum(jnp.sum(q, axis=-1, keepdims=True) for q in quarter) * (1.0 / 768)
    centred = [q - mean for q in quarter]
    spread = sum(jnp.sum(c * c, axis=-1, keepdims=True) for c in centred) * (1.0 / 768)
    rstd = lax.rsqrt(spread + EPS)
    normed = [c * rstd for c in centred]
    dmerged = [
        dot_nt(dcoarse, w_merge[192 * d : 192 * d + 192, :]).astype(BF).astype(F32) for d in range(4)
    ]
    first = sum(jnp.sum(g, axis=-1, keepdims=True) for g in dmerged) * (1.0 / 768)
    second = sum(jnp.sum(g * n, axis=-1, keepdims=True) for g, n in zip(dmerged, normed)) * (1.0 / 768)
    for d in range(4):
        dfine = (rstd * (dmerged[d] - first - normed[d] * second)).astype(BF).astype(F32)
        up = upstream[TOK * d : TOK * (d + 1), :].astype(F32)
        own_out[TOK * d : TOK * (d + 1), :] = (up + dfine).astype(BF)
    pieces = dot(send[...], own_out[...]).astype(BF)
    row_out[...] = pieces[:ROW_PIECE]
    col_out[...] = pieces[ROW_PIECE : ROW_PIECE + COL_PIECE]
    corner_out[...] = pieces[ROW_PIECE + COL_PIECE :]


def moved(value, lat, lon):
    lats, lons = lax.axis_size("lat"), lax.axis_size("lon")
    if lat == 0:
        pairs = [(source, (source + lon) % lons) for source in range(lons)]
        return lax.ppermute(value, "lon", pairs)
    if lon == 0:
        pairs = [(source, (source + lat) % lats) for source in range(lats)]
        return lax.ppermute(value, "lat", pairs)
    pairs = [
        (a * lons + b, (a + lat) % lats * lons + (b + lon) % lons)
        for a in range(lats)
        for b in range(lons)
    ]
    return lax.ppermute(value, ("lat", "lon"), pairs)


def exchanged(pieces, step):
    row, col, corner = pieces
    return moved(row, step, 0), moved(col, 0, step), moved(corner, step, step)


class Arriving:
    def __init__(self, source, target, semaphore):
        self.copy = pltpu.make_async_copy(source, target, semaphore)
        self.target = target
        self.shape = target.shape
        self.waiting = True
        self.copy.start()

    def __getitem__(self, index):
        if self.waiting:
            self.copy.wait()
            self.waiting = False
        return self.target[index]


def call(kernel, out_shapes, *operands, scratch=(), scalars=0, late=(), hbm_out=()):
    shapes = [jax.ShapeDtypeStruct(shape, dtype) for shape, dtype in out_shapes]
    scalar, array = pl.BlockSpec(memory_space=pltpu.SMEM), pl.BlockSpec(memory_space=pltpu.VMEM)
    remote = pl.BlockSpec(memory_space=pltpu.HBM)
    count = len(operands)
    order = [i for i in range(scalars, count) if i not in late] + list(late)
    landing = [pltpu.VMEM(operands[i].shape, operands[i].dtype) for i in order]
    landing.append(pltpu.SemaphoreType.DMA((len(order),)))

    def whole(*refs):
        inputs, others = list(refs[:count]), refs[count : len(refs) - len(landing)]
        spaces = refs[len(refs) - len(landing) :]
        for k, i in enumerate(order):
            inputs[i] = Arriving(inputs[i], spaces[k], spaces[-1].at[k])
        kernel(*inputs, *others)

    return pl.pallas_call(
        whole,
        out_shape=shapes,
        in_specs=[scalar if i < scalars else remote for i in range(count)],
        out_specs=[remote if i in hbm_out else array for i in range(len(shapes))],
        scratch_shapes=list(scratch) + landing,
        compiler_params=pltpu.CompilerParams(vmem_limit_bytes=VMEM),
        name=kernel.__name__,
    )(*operands)


def swapped(value, step):
    pairs = [(source, source ^ step) for source in range(lax.axis_size("lon"))]
    return lax.ppermute(value, "lon", pairs)


def on_device(fields, upstream, bias_f, bias_c, w_qkv_f, w_proj_f, w_merge, w_qkv_c, w_proj_c, w_split):
    windows, quartets = window_order(), quartet_order()
    last = (lax.axis_index("lat") == lax.axis_size("lat") - 1).astype(jnp.int32).reshape(1)
    odd = lax.axis_index("lon") % 2
    parity = odd.astype(jnp.int32).reshape(1)

    fields = fields.transpose(0, 2, 1, 3)
    upstream = upstream.transpose(0, 2, 1, 3).reshape(576, 192)
    natural = natural_order()
    place = {cell: index for index, cell in enumerate(natural)}
    pieces = call(cut, [((2, 6, 3, 192), BF), ((2, 6, LAT, 192), BF), ((2, 6, 3, 192), BF)], fields)
    row, col, corner = exchanged(pieces, -1)
    (stripes_f,) = call(expand, [((24, 24, LANES), F32)], bias_f.transpose(0, 2, 3, 1, 4))
    row, col, corner, stripes_f = lax.optimization_barrier((row, col, corner, stripes_f))
    (up,) = call(
        reordered, [((576, 192), BF)], one_hot([place[cell] for cell in quartets], 576), upstream
    )
    piece_shapes = [((size, 192), BF) for size in (ROW_PIECE, COL_PIECE, CORNER)]
    x, qkv, weights, mixed, *pieces = call(
        fine_forward,
        [((576, 192), BF), ((576, 768), BF), ((NWF, 6 * TOK, TOK), BF), ((576, 192), BF)] + piece_shapes,
        last, window_table(), last_window_table(), fields, row, col, corner, stripes_f, w_qkv_f, w_proj_f,
        scratch=[
            pltpu.VMEM((2, LON, LAT + 8, 192), F32),
            pltpu.VMEM((576, 192), BF),
            pltpu.VMEM((576, 768), BF),
            pltpu.VMEM((NWF, 6 * TOK, TOK), BF),
            pltpu.SemaphoreType.DMA((6,)),
        ],
        late=(8, 7, 9, 2),
        hbm_out=(0, 1, 2),
        scalars=1,
    )
    row, col, corner = exchanged(pieces, 1)
    (stripes_c,) = call(expand, [((24, 24, LANES), F32)], bias_c.transpose(0, 2, 3, 1, 4))
    row, col, corner, stripes_c, up = lax.optimization_barrier((row, col, corner, stripes_c, up))
    fine, coarse_in, queries, pairs = call(
        merge_forward,
        [((576, 192), BF), ((TOK, 384), BF), ((TOK, 384), BF), ((TOK, 768), BF)],
        gather_table(windows, back_pieces(), unrolled_from(quartets)),
        mixed, row, col, corner, w_merge, w_qkv_c,
        late=(5, 6),
    )
    far = swapped(pairs, 1)
    result_q, input_back, own_back, far_back, totals_c = call(
        coarse_middle,
        [
            ((576, 192), BF),
            ((TOK, 384), BF),
            ((TOK, 1152), F32),
            ((TOK, 768), BF),
            ((24, 24, LANES), F32),
        ],
        parity, queries, pairs, far, coarse_in, fine, up, stripes_c, w_proj_c, w_split,
        scratch=[
            pltpu.VMEM((TOK, 384), F32),
            pltpu.VMEM((NWC, 3, 4 * HALF, TOK), BF),
            pltpu.VMEM((TOK, 384), F32),
        ],
        scalars=1,
        late=(4, 8, 9, 5, 6),
    )
    returned = swapped(far_back, 1)
    fine_back, *pieces = call(
        merge_backward,
        [((576, 192), BF)] + piece_shapes,
        send_table(quartets, forward_pieces()),
        own_back, returned, coarse_in, input_back, fine, up, w_merge, w_qkv_c,
        late=(3, 4, 5, 7, 6, 0),
    )
    row, col, corner = exchanged(pieces, -1)
    (packed_c,) = call(
        pack, [((PACKED, 128), BF)], totals_c, scratch=[pltpu.VMEM((PACKED, 128), F32)]
    )
    row, col, corner, packed_c = lax.optimization_barrier((row, col, corner, packed_c))
    grad_rolled, *rest = call(
        fine_backward,
        [((576, 192), BF)] + piece_shapes + [((PACKED, 128), BF)],
        gather_table(quartets, forward_pieces(), rolled_from(windows)),
        last_window_table(),
        fine_back, row, col, corner, x, qkv, weights, w_qkv_f, w_proj_f,
        scratch=[
            pltpu.VMEM((576, 768), BF),
            pltpu.VMEM((PACKED, 128), F32),
            pltpu.VMEM((24, 24, LANES), F32),
        ],
        late=(10, 7, 8, 9, 6, 1),
    )
    *pieces, packed_f = rest

    row, col, corner = exchanged(pieces, 1)
    sent = jnp.where(odd == 0, packed_f, packed_c)
    kept = jnp.where(odd == 0, packed_c, packed_f)
    kept = kept.astype(F32) + swapped(sent, 1).astype(F32)
    far = lax.axis_index("lon") // 2 % 2
    low, high = kept[: PACKED // 2], kept[PACKED // 2 :]
    sent = jnp.where(far == 0, high, low).astype(BF)
    kept = jnp.where(far == 0, low, high)
    kept = (kept + swapped(sent, 2).astype(F32)).astype(BF)
    recv = swapped(kept, 4)
    place = {cell: index for index, cell in enumerate(quartets)}
    (result,) = call(
        reordered, [((576, 192), BF)], one_hot([place[cell] for cell in natural], 576), result_q
    )
    kept, recv, result = lax.optimization_barrier((kept, recv, result))
    kept = (kept.astype(F32) + recv.astype(F32)).astype(BF)
    recv = swapped(kept, 12)
    kept, recv, row, col, corner = lax.optimization_barrier((kept, recv, row, col, corner))
    kept = (kept.astype(F32) + recv.astype(F32)).astype(BF)
    recv = swapped(kept, 16)
    (grad_fields,) = call(
        assemble,
        [((576, 192), BF)],
        gather_table(windows, back_pieces(), unrolled_from(natural)),
        grad_rolled, row, col, corner,
    )
    kept, recv, grad_fields = lax.optimization_barrier((kept, recv, grad_fields))
    kept = (kept.astype(F32) + recv.astype(F32)).astype(BF)
    kept_far = swapped(kept, 2)
    grad_bias_f, grad_bias_c = call(
        unpack,
        [((1, 6, REL, NWF, TOK), F32), ((1, 12, REL, NWC, TOK), F32)],
        jnp.stack([odd, far]).astype(jnp.int32), kept, kept_far, swapped(kept, 1), swapped(kept_far, 1),
        scalars=1,
    )
    grad_bias_f = grad_bias_f.transpose(0, 3, 1, 2, 4)
    grad_bias_c = grad_bias_c.transpose(0, 3, 1, 2, 4)
    result = result.reshape(2, LON, LAT, 192).transpose(0, 2, 1, 3)
    grad_fields = grad_fields.reshape(2, LON, LAT, 192).transpose(0, 2, 1, 3)
    return (result, grad_fields, grad_bias_f, grad_bias_c)


def solution(mesh):
    grid = P(None, "lat", "lon", None)
    table = P(None, "lat", None, None, None)
    return jax.shard_map(
        on_device,
        mesh=mesh,
        in_specs=(grid, grid, table, table, P(), P(), P(), P(), P(), P()),
        out_specs=(grid, grid, table, table),
        check_vma=False,
    )
```

```python
import math

import jax
import jax.numpy as jnp
import numpy as np
from jax import lax
from jax.experimental import pallas as pl
from jax.experimental.pallas import tpu as pltpu
from jax.sharding import PartitionSpec as P

WIN_Z = 2
WIN_LAT = 6
WIN_LON = 12
ROWS = WIN_Z * WIN_LAT
TOK = ROWS * WIN_LON
HALF = TOK // 2
REL = 2 * WIN_LON - 1
WIDE = REL * ROWS
EPS = 1e-05
MASKED = -1000000000.0
HEAD = 32
SCALE = 1.0 / math.sqrt(HEAD)
LAT = 24
LON = 12
NWF = LAT // WIN_LAT
NWC = LAT // 2 // WIN_LAT
BF = jnp.bfloat16
F32 = jnp.float32
ROW_PIECE, COL_PIECE, CORNER = 48, 288, 48
VMEM = 56 * 1024 * 1024
TABLE = 24 + 3
LANES = 384
PACKED = 24 * TABLE + 8
BATCH = 4


def natural_order():
    return [(z, i, j) for z in range(2) for j in range(LON) for i in range(LAT)]


def window_order():
    return [
        (z, WIN_LAT * w + l, n)
        for w in range(NWF)
        for n in range(LON)
        for z in range(2)
        for l in range(WIN_LAT)
    ]


def quartet_order():
    return [
        (z, 2 * (WIN_LAT * w + l) + di, 2 * n + dj)
        for di in range(2)
        for dj in range(2)
        for w in range(NWC)
        for n in range(LON // 2)
        for z in range(2)
        for l in range(WIN_LAT)
    ]


def one_hot(rows, columns):
    table = np.zeros((len(rows), columns), np.float32)
    for row, column in enumerate(rows):
        if column is not None:
            table[row, column] = 1.0
    return jnp.asarray(table, BF)


def forward_pieces():
    row = [(z, i, j) for z in range(2) for i in range(3) for j in range(6, LON)]
    col = [(z, i, j) for z in range(2) for i in range(LAT) for j in range(6)]
    corner = [(z, i, j) for z in range(2) for i in range(3) for j in range(6)]
    return row, col, corner


def back_pieces():
    row = [(z, i, j) for z in range(2) for i in range(LAT - 3, LAT) for j in range(6)]
    col = [cell for cell in window_order() if cell[2] >= 6]
    corner = [(z, i, j) for z in range(2) for i in range(LAT - 3, LAT) for j in range(6, LON)]
    return row, col, corner


def padded_pieces(pieces):
    sizes = (ROW_PIECE, COL_PIECE, CORNER)
    return [cells + [None] * (size - len(cells)) for cells, size in zip(pieces, sizes)]


def send_table(own_order, pieces):
    place = {cell: index for index, cell in enumerate(own_order)}
    cells = sum(padded_pieces(pieces), [])
    return one_hot([None if cell is None else place[cell] for cell in cells], len(own_order))


def gather_table(own_order, pieces, wanted):
    tables = [{cell: index for index, cell in enumerate(own_order)}]
    starts = [0]
    for cells in pieces:
        tables.append({cell: index for index, cell in enumerate(cells)})
    starts = [0, len(own_order), len(own_order) + ROW_PIECE, len(own_order) + ROW_PIECE + COL_PIECE]
    total = len(own_order) + ROW_PIECE + COL_PIECE + CORNER
    rows = []
    for entry in wanted:
        rows.append(None if entry is None else starts[entry[0]] + tables[entry[0]][entry[1]])
    return one_hot(rows, total)


def window_start(w):
    return (WIN_LAT * w + WIN_LAT // 2) // 8 * 8 if w < NWF - 1 else LAT - 8


def window_table():
    rows = []
    for w in range(NWF):
        offset = WIN_LAT * w + WIN_LAT // 2 - window_start(w)
        for n in range(LON):
            for z in range(2):
                for l in range(WIN_LAT):
                    rows.append(((1 - z) * LON + n) * 16 + offset + l)
    return one_hot(rows, 2 * LON * 16)


def last_window_table():
    place = {cell: index for index, cell in enumerate(window_order()[-TOK:])}
    row, _, corner = padded_pieces(back_pieces())
    return one_hot([None if cell is None else place[cell] for cell in row + corner], TOK)


def rolled_from(cells):
    wanted = []
    for z, i, j in cells:
        z, i, j = 1 - z, i + 3, j + 6
        kind = (1 if i >= LAT else 0) + (2 if j >= LON else 0)
        wanted.append((kind, (z, i % LAT, j % LON)))
    return wanted


def unrolled_from(cells):
    wanted = []
    for cell in cells:
        z, i, j = cell
        z, i, j = 1 - z, i - 3, j - 6
        kind = (1 if i < 0 else 0) + (2 if j < 0 else 0)
        wanted.append((kind, (z, i % LAT, j % LON)))
    return wanted


def dot(a, b):
    return lax.dot_general(a, b, (((1,), (0,)), ((), ())), preferred_element_type=F32)


def dot_nt(a, b):
    return lax.dot_general(a, b, (((1,), (1,)), ((), ())), preferred_element_type=F32)


def dot_tn(a, b):
    return lax.dot_general(a, b, (((0,), (0,)), ((), ())), preferred_element_type=F32)


def normalise(values, count):
    mean = jnp.sum(values, axis=-1, keepdims=True) * (1.0 / count)
    centred = values - mean
    spread = jnp.sum(centred * centred, axis=-1, keepdims=True) * (1.0 / count)
    rstd = lax.rsqrt(spread + EPS)
    return centred * rstd, rstd


def normalise_back(cotangent, normed, rstd, count):
    first = jnp.sum(cotangent, axis=-1, keepdims=True) * (1.0 / count)
    second = jnp.sum(cotangent * normed, axis=-1, keepdims=True) * (1.0 / count)
    return rstd * (cotangent - first - normed * second)


def head_stack(values, heads):
    lanes = lax.broadcasted_iota(jnp.int32, values.shape, 1) // HEAD
    return jnp.concatenate([jnp.where(lanes == h, values, 0.0) for h in range(heads)], axis=0).astype(BF)


def head_sum(stacked, heads):
    rows = stacked.shape[0] // heads
    lanes = lax.broadcasted_iota(jnp.int32, (rows, 128), 1) // HEAD
    total = stacked[:rows]
    for h in range(1, heads):
        total = jnp.where(lanes == h, stacked[h * rows : (h + 1) * rows], total)
    return jnp.where(lanes < heads, total, 0.0)


def softmax(scores, ones):
    highest = jnp.max(scores, axis=-1, keepdims=True)
    powers = jnp.exp(scores - highest)
    rounded = powers.astype(BF)
    inverse = 1.0 / dot(rounded, ones)
    weights = powers * jnp.concatenate([inverse, inverse[:, : TOK - 128]], axis=1)
    return rounded, inverse, weights.astype(BF)


def scores_back(weights, dweights, ones):
    weights32 = weights.astype(F32)
    product = weights32 * dweights
    total = dot(product.astype(BF), ones)
    return product - weights32 * jnp.concatenate([total, total[:, : TOK - 128]], axis=1)


def rotated(value, shift, axis):
    size = value.shape[axis]
    return pltpu.roll(value, shift % size, axis)


def sheared(value, index, bits, lanes):
    for bit in range(bits):
        value = jnp.where((index >> bit) & 1 == 1, rotated(value, lanes << bit, 2), value)
    return value


def strided(value):
    tiles = []
    for start in range(0, value.shape[1], 8):
        tile = pltpu.roll(value[:, start : start + 8], 0, 2, stride=ROWS, stride_axis=1)
        tiles.append(rotated(tile, ROWS * start, 2))
    return jnp.concatenate(tiles, axis=1)


def raised(value, amount, steps):
    for step in steps:
        value = jnp.where(amount & step != 0, rotated(value, step, 1), value)
    return value


def stripes_of(table, stripes_out):
    heads = table.shape[0]
    index = lax.broadcasted_iota(jnp.int32, (1, 24, LANES), 1)
    amount = (lax.broadcasted_iota(jnp.int32, (1, 8, LANES), 2) // ROWS + 10) & 31
    table = jnp.concatenate([table, jnp.zeros((heads, REL, LANES - TOK), F32)], axis=2)
    table = jnp.concatenate([table, jnp.zeros((heads, 1, LANES), F32)], axis=1)
    table = rotated(sheared(table, index, 5, -ROWS), 22 * ROWS, 2)
    tiles = [table[:, 0:8], table[:, 8:16], table[:, 16:24], jnp.zeros((heads, 8, LANES), F32)]
    tiles = [jnp.where(amount & 16 != 0, tiles[k - 2], tiles[k]) for k in range(4)]
    tiles = [jnp.where(amount & 8 != 0, tiles[k - 1], tiles[k]) for k in range(4)]
    stripes = jnp.concatenate([tiles[3], tiles[0], tiles[1]], axis=1)
    stripes = raised(stripes, amount[:, :1], (4, 2, 1))[:, 8:]
    stripes = sheared(stripes, index[:, :16], 4, -ROWS)
    stripes = jnp.where(index[:, :16] < ROWS, stripes, 0.0)
    stripes = jnp.concatenate([stripes, jnp.zeros((heads, 8, LANES), F32)], axis=1)
    stripes_out[...] = stripes + rotated(rotated(stripes, ROWS, 2), ROWS, 1)


def stripes_back(stripes):
    heads = stripes.shape[0]
    index = lax.broadcasted_iota(jnp.int32, (1, 16, LANES), 1)
    amount = (22 - lax.broadcasted_iota(jnp.int32, (1, 8, LANES), 2) // ROWS) & 31
    stripes = stripes + rotated(rotated(stripes, -ROWS, 2), ROWS, 1)
    stripes = strided(jnp.where(index < ROWS, stripes[:, :16], 0.0))
    blank = jnp.zeros((heads, 8, LANES), F32)
    stripes = raised(jnp.concatenate([stripes, blank], axis=1), amount[:, :1], (1, 2, 4))
    tiles = [stripes[:, 0:8], stripes[:, 8:16], stripes[:, 16:24], blank]
    tiles = [jnp.where(amount & 8 != 0, tiles[k - 1], tiles[k]) for k in range(4)]
    tiles = [jnp.where(amount & 16 != 0, tiles[k - 2], tiles[k]) for k in range(3)]
    return rotated(strided(jnp.concatenate(tiles, axis=1)), -22 * ROWS, 2)


def expand(table, stripes_out):
    _, heads, _, windows, _ = table.shape
    batch = BATCH if heads % BATCH == 0 else 3
    for w in range(windows):
        for start in range(0, heads, batch):
            place = stripes_out.at[heads * w + start : heads * w + start + batch]
            stripes_of(table[0, start : start + batch, :, w, :], place)


def pack(totals, packed_out, packed):
    pack_tables(totals, packed)
    packed_out[...] = packed[...].astype(BF)


def pack_tables(totals, packed):
    packed[24 * TABLE :, :] = jnp.zeros((PACKED - 24 * TABLE, 128), F32)
    rest = jnp.zeros((24, 128), F32)
    for start in range(0, 24, BATCH):
        tables = stripes_back(totals[start : start + BATCH])
        for head in range(start, start + BATCH):
            rest = pack_table(tables[head - start], head, packed, rest)


def pack_table(table, head, packed, rest):
    packed[24 * head : 24 * head + 24, :] = table[:, :128]
    rest = rest + rotated(table[:, 128:256], 16 * (head % 8), 1)
    if head % 8 == 7:
        start = 24 * (24 + head // 8)
        packed[start : start + 24, :] = rest
        rest = jnp.zeros((24, 128), F32)
    return rest


def mask_of(last_row):
    first = lax.broadcasted_iota(jnp.int32, (24, LANES), 0) % ROWS
    second = lax.broadcasted_iota(jnp.int32, (24, LANES), 1) % ROWS
    half = WIN_Z // 2
    level = (first // WIN_LAT >= WIN_Z - half) != (second // WIN_LAT >= WIN_Z - half)
    if last_row is not None:
        half = WIN_LAT // 2
        row = (first % WIN_LAT >= WIN_LAT - half) != (second % WIN_LAT >= WIN_LAT - half)
        level = level | (row & (last_row == 1))
    return jnp.where(level, MASKED, 0.0).astype(F32)


def padded_lanes(weights):
    blocks = []
    for start in range(0, weights.shape[1], 192):
        blocks += [weights[:, start : start + 192], jnp.zeros((weights.shape[0], 64), weights.dtype)]
    return jnp.concatenate(blocks, axis=1)


def cut(fields, row_out, col_out, corner_out):
    row_out[...] = fields[:, 6:, :3]
    col_out[...] = fields[:, :6]
    corner_out[...] = fields[:, :6, :3]


def fine_forward(last, gather, send, fields, row, col, corner, table, w_qkv_in, w_proj_in, x_out, qkv_out, weights_out, mixed_out, row_out, col_out, corner_out, rolled, stripes, x_s, qkv_s, weights_s, sems):
    rolled[:, :, LAT:, :] = jnp.zeros((2, LON, 8, 192), F32)
    rolled[:, :6, :LAT, :] = fields[:, 6:].astype(F32)
    rolled[:, 6:, :LAT, :] = col[...].astype(F32)
    rolled[:, :6, LAT : LAT + 3, :] = row[...].astype(F32)
    rolled[:, 6:, LAT : LAT + 3, :] = corner[...].astype(F32)
    x = []
    for w in range(NWF):
        start = window_start(w)
        sources = rolled[:, :, start : start + 16].reshape(2 * LON * 16, 192).astype(BF)
        x.append(dot(gather[TOK * w : TOK * w + TOK, :], sources))
    x = jnp.concatenate(x, axis=0)
    x_s[...] = x.astype(BF)
    copies = [pltpu.make_async_copy(x_s, x_out, sems.at[0])]
    copies[-1].start()
    normed, _ = normalise(x, 192)
    qkv_s[...] = dot(normed.astype(BF), padded_lanes(w_qkv_in[...])).astype(BF)
    copies.append(pltpu.make_async_copy(qkv_s, qkv_out, sems.at[1]))
    copies[-1].start()
    w_proj = jnp.concatenate([w_proj_in[...], jnp.zeros((64, 192), BF)], axis=0)
    ones = jnp.ones((TOK, 128), BF)
    level_mask = mask_of(None)
    last_mask = mask_of(last[0])
    sent = []
    for w in range(NWF):
        rows = pl.ds(w * TOK, TOK)
        for start in range(0, 6, 3):
            stripes_of(table[0, start : start + 3, :, w, :], stripes.at[start : start + 3])
        blended = []
        for group, heads in ((0, 4), (1, 2)):
            queries = qkv_s[rows, 128 * group : 128 * group + 128]
            keys = qkv_s[rows, 256 + 128 * group : 256 + 128 * group + 128]
            values = qkv_s[rows, 512 + 128 * group : 512 + 128 * group + 128]
            bias = []
            for h in range(heads):
                stripe = stripes[4 * group + h] + (last_mask if w == NWF - 1 else level_mask)
                bias += [rotated(stripe, -(11 - 2 * m) * ROWS, 1)[:, :TOK] for m in range(6)]
            bias = jnp.concatenate(bias, axis=0)
            queries = head_stack(queries.astype(F32), heads)
            rounded, inverse, weights = softmax(dot_nt(queries, keys) * SCALE + bias, ones)
            weights_s[w, 4 * TOK * group : 4 * TOK * group + heads * TOK, :] = weights
            blended.append(head_sum(dot(rounded, values) * inverse, heads))
        blended = jnp.concatenate(blended, axis=1).astype(BF)
        mixed = x[w * TOK : (w + 1) * TOK] + dot(blended, w_proj)
        sent.append(mixed[HALF:])
        mixed_out[rows, :] = mixed.astype(BF)
        copies.append(pltpu.make_async_copy(weights_s.at[w], weights_out.at[w], sems.at[2 + w]))
        copies[-1].start()
    col_out[...] = jnp.concatenate(sent, axis=0).astype(BF)
    pieces = dot(send[...], mixed_out[TOK * (NWF - 1) :, :]).astype(BF)
    row_out[...] = pieces[:ROW_PIECE]
    corner_out[...] = pieces[ROW_PIECE:]
    for copy in copies:
        copy.wait()


def fine_backward(gather, send, own, row, col, corner, x, qkv, weights_in, w_qkv_in, w_proj_in, own_out, row_out, col_out, corner_out, packed_out, dqkv, packed, totals):
    sources = jnp.concatenate([own[...], row[...], col[...], corner[...]], axis=0)
    dmix = dot(gather[...], sources).astype(BF)
    w_proj = jnp.concatenate([w_proj_in[...], jnp.zeros((64, 192), BF)], axis=0)
    datt = dot_nt(dmix, w_proj).astype(BF)
    ones = jnp.ones((TOK, 128), BF)
    for w in range(NWF):
        rows = pl.ds(w * TOK, TOK)
        for group, heads in ((0, 4), (1, 2)):
            lanes = slice(128 * group, 128 * group + 128)
            queries = qkv[rows, 128 * group : 128 * group + 128]
            keys = qkv[rows, 256 + 128 * group : 256 + 128 * group + 128]
            values = qkv[rows, 512 + 128 * group : 512 + 128 * group + 128]
            grad = datt[w * TOK : (w + 1) * TOK, lanes]
            queries = head_stack(queries.astype(F32), heads)
            grad = head_stack(grad.astype(F32), heads)
            weights = weights_in[w, 4 * TOK * group : 4 * TOK * group + heads * TOK, :]
            dscores = scores_back(weights, dot_nt(grad, values), ones)
            ds = dscores.astype(BF)
            dq = head_sum(dot(ds, keys), heads)
            dk = dot_tn(ds, queries)
            dv = dot_tn(weights, grad)
            wide = jnp.concatenate([dscores, jnp.zeros((heads * TOK, LANES - TOK), F32)], axis=1)
            for h in range(heads):
                total = jnp.zeros((24, LANES), F32)
                for m in range(6):
                    block = wide[TOK * h + 24 * m : TOK * h + 24 * m + 24]
                    total = total + rotated(block, (11 - 2 * m) * ROWS, 1)
                totals[6 * w + 4 * group + h] = total
            dqkv[rows, 128 * group : 128 * group + 128] = (dq * SCALE).astype(BF)
            dqkv[rows, 256 + 128 * group : 256 + 128 * group + 128] = (dk * SCALE).astype(BF)
            dqkv[rows, 512 + 128 * group : 512 + 128 * group + 128] = dv.astype(BF)
    pack_tables(totals, packed)
    packed_out[...] = packed[...].astype(BF)
    dnormed = dot_nt(dqkv[...], padded_lanes(w_qkv_in[...])).astype(BF).astype(F32)
    normed, rstd = normalise(x[...].astype(F32), 192)
    dx = normalise_back(dnormed, normed, rstd, 192).astype(BF).astype(F32)
    grad_rolled = dmix.astype(F32) + dx
    own_out[...] = grad_rolled.astype(BF)
    sent = [grad_rolled[TOK * w + HALF : TOK * w + TOK] for w in range(NWF)]
    col_out[...] = jnp.concatenate(sent, axis=0).astype(BF)
    pieces = dot(send[...], own_out[TOK * (NWF - 1) :, :]).astype(BF)
    row_out[...] = pieces[:ROW_PIECE]
    corner_out[...] = pieces[ROW_PIECE:]


def reordered(gather, values, out):
    out[...] = dot(gather[...], values[...]).astype(BF)


def unpack(bits, kept, kept_far, other, other_far, fine_out, coarse_out):
    even, low = bits[0] == 0, bits[1] == 0
    halves = [part[...].astype(F32) for part in (kept, kept_far, other, other_far)]
    tables = []
    for near, far in (halves[:2], halves[2:]):
        tables.append(
            jnp.concatenate([jnp.where(low, near, far), jnp.where(low, far, near)], axis=0)
        )
    coarse = jnp.where(even, tables[0], tables[1])
    fine = jnp.where(even, tables[1], tables[0])
    for packed, out, heads in ((fine, fine_out, 6), (coarse, coarse_out, 12)):
        for head in range(24):
            rest = 24 * (24 + head // 8)
            rest = rotated(packed[rest : rest + 24], -16 * (head % 8), 1)[:, : TOK - 128]
            table = jnp.concatenate([packed[24 * head : 24 * head + 24], rest], axis=1)
            out[0, head % heads, :, head // heads, :] = table[:REL]


def assemble(gather, own, row, col, corner, out):
    sources = jnp.concatenate([own[...], row[...], col[...], corner[...]], axis=0)
    out[...] = dot(gather[...], sources).astype(BF)


def merge_forward(gather, own, row, col, corner, w_merge, w_qkv, fine_out, coarse_out, queries_out, pairs_out):
    sources = jnp.concatenate([own[...], row[...], col[...], corner[...]], axis=0)
    fine = dot(gather[...], sources)
    fine_out[...] = fine.astype(BF)
    quarter = [fine[TOK * d : TOK * (d + 1)] for d in range(4)]
    mean = sum(jnp.sum(q, axis=-1, keepdims=True) for q in quarter) * (1.0 / 768)
    centred = [q - mean for q in quarter]
    spread = sum(jnp.sum(c * c, axis=-1, keepdims=True) for c in centred) * (1.0 / 768)
    rstd = lax.rsqrt(spread + EPS)
    coarse = jnp.zeros((TOK, 384), F32)
    for d in range(4):
        coarse = coarse + dot((centred[d] * rstd).astype(BF), w_merge[192 * d : 192 * d + 192, :])
    coarse = coarse.astype(BF)
    coarse_out[...] = coarse
    normed, _ = normalise(coarse.astype(F32), 384)
    projected = dot(normed.astype(BF), w_qkv[...])
    queries_out[...] = projected[:, :384].astype(BF)
    pairs_out[...] = projected[:, 384:].astype(BF)


def coarse_middle(parity, queries_in, pairs_in, far_in, coarse_in, fine, upstream, stripes, w_proj, w_split, result_out, input_back_out, own_back_out, far_back_out, totals, attended, weights_ref, dattended):
    pairs = pairs_in[...].astype(F32)
    far = far_in[...].astype(F32)
    queries32 = queries_in[...].astype(F32)
    joined = []
    first = parity[0] == 0
    ones = jnp.ones((TOK, 128), BF)
    lanes = lax.broadcasted_iota(jnp.int32, (24, 128), 1)
    for w in range(NWC):
        joined.append(
            jnp.concatenate([pairs[HALF * w : HALF * w + HALF], far[HALF * w : HALF * w + HALF]], axis=0).astype(BF)
        )
    for w in range(NWC):
        for group in range(3):
            queries = queries32[HALF * w : HALF * w + HALF, 128 * group : 128 * group + 128]
            keys = joined[w][:, 128 * group : 128 * group + 128]
            values = joined[w][:, 384 + 128 * group : 384 + 128 * group + 128]
            bias = []
            for h in range(4):
                stripe = stripes[12 * w + 4 * group + h]
                near = rotated(stripe, -84, 1)[:, :128]
                other = jnp.where(first, rotated(stripe, -84, 1), rotated(stripe, 60, 1))[:, :256]
                for m in range(3):
                    offset = 48 - 24 * m
                    left = rotated(near, -offset, 1)
                    right = rotated(other, -offset, 1)[:, :TOK]
                    left = jnp.where(lanes < HALF, left, right[:, :128])
                    bias.append(jnp.concatenate([left, right[:, 128:]], axis=1))
            bias = jnp.concatenate(bias, axis=0)
            scores = dot_nt(head_stack(queries, 4), keys) * SCALE + bias
            rounded, inverse, weights = softmax(scores, ones)
            weights_ref[w, group] = weights
            total = head_sum(dot(rounded, values) * inverse, 4)
            attended[HALF * w : HALF * w + HALF, 128 * group : 128 * group + 128] = total
    coarse32 = coarse_in[...].astype(F32)
    coarse_out = (coarse32 + dot(attended[...].astype(BF), w_proj[...])).astype(BF)
    normed, rstd = normalise(coarse_out.astype(F32), 384)
    normed_b = normed.astype(BF)
    back = jnp.zeros((TOK, 384), F32)
    for d in range(4):
        part = w_split[:, 192 * d : 192 * d + 192]
        up = upstream[TOK * d : TOK * d + TOK, :]
        widened = dot(normed_b, part)
        result_out[TOK * d : TOK * d + TOK, :] = (fine[TOK * d : TOK * d + TOK, :].astype(F32) + widened).astype(BF)
        back = back + dot_nt(up, part)
    back = back.astype(BF).astype(F32)
    input_back = normalise_back(back, normed, rstd, 384).astype(BF)
    input_back_out[...] = input_back
    dattended[...] = dot_nt(input_back, w_proj[...]).astype(BF).astype(F32)
    for w in range(NWC):
        for group in range(3):
            queries = queries32[HALF * w : HALF * w + HALF, 128 * group : 128 * group + 128]
            keys = joined[w][:, 128 * group : 128 * group + 128]
            values = joined[w][:, 384 + 128 * group : 384 + 128 * group + 128]
            grad = dattended[HALF * w : HALF * w + HALF, 128 * group : 128 * group + 128]
            queries = head_stack(queries, 4)
            grad = head_stack(grad, 4)
            weights = weights_ref[w, group]
            dscores = scores_back(weights, dot_nt(grad, values), ones)
            ds = dscores.astype(BF)
            dq = head_sum(dot(ds, keys), 4)
            dk = dot_tn(ds, queries)
            dv = dot_tn(weights, grad)
            blank = jnp.zeros((24, 256 - TOK), F32)
            for h in range(4):
                near = jnp.zeros((24, 128), F32)
                other = jnp.zeros((24, 256), F32)
                for m in range(3):
                    offset = 48 - 24 * m
                    block = dscores[HALF * h + 24 * m : HALF * h + 24 * m + 24]
                    left = jnp.where(lanes < HALF, block[:, :128], 0.0)
                    right = jnp.concatenate([block[:, :128] - left, block[:, 128:], blank], axis=1)
                    near = near + rotated(left, offset, 1)
                    other = other + rotated(right, offset - HALF, 1)
                blank_lanes = jnp.zeros((24, LANES - 128), F32)
                near = rotated(jnp.concatenate([near, blank_lanes], axis=1), 84, 1)
                other = jnp.concatenate([other[:, :128], blank_lanes], axis=1)
                other = jnp.where(first, rotated(other, 156, 1), rotated(other, 12, 1))
                totals[12 * w + 4 * group + h] = near + other
            part = slice(HALF * w, HALF * w + HALF)
            cols = slice(128 * group, 128 * group + 128)
            own_back_out[part, cols] = dq * SCALE
            own_back_out[part, 384 + 128 * group : 384 + 128 * group + 128] = dk[:HALF] * SCALE
            own_back_out[part, 768 + 128 * group : 768 + 128 * group + 128] = dv[:HALF]
            far_back_out[part, cols] = (dk[HALF:] * SCALE).astype(BF)
            far_back_out[part, 384 + 128 * group : 384 + 128 * group + 128] = dv[HALF:].astype(BF)


def merge_backward(send, own_back, returned, coarse_in, input_back, fine, upstream, w_merge, w_qkv, own_out, row_out, col_out, corner_out):
    returned32 = returned[...].astype(F32)
    dq = own_back[:, :384].astype(BF)
    dkv = (own_back[:, 384:] + returned32).astype(BF)
    dnormed = dot_nt(dq, w_qkv[:, :384]) + dot_nt(dkv, w_qkv[:, 384:])
    dnormed = dnormed.astype(BF).astype(F32)
    normed, rstd = normalise(coarse_in[...].astype(F32), 384)
    dx = normalise_back(dnormed, normed, rstd, 384).astype(BF)
    dcoarse = (input_back[...].astype(F32) + dx.astype(F32)).astype(BF)
    quarter = [fine[TOK * d : TOK * (d + 1), :].astype(F32) for d in range(4)]
    mean = sum(jnp.sum(q, axis=-1, keepdims=True) for q in quarter) * (1.0 / 768)
    centred = [q - mean for q in quarter]
    spread = sum(jnp.sum(c * c, axis=-1, keepdims=True) for c in centred) * (1.0 / 768)
    rstd = lax.rsqrt(spread + EPS)
    normed = [c * rstd for c in centred]
    dmerged = [
        dot_nt(dcoarse, w_merge[192 * d : 192 * d + 192, :]).astype(BF).astype(F32) for d in range(4)
    ]
    first = sum(jnp.sum(g, axis=-1, keepdims=True) for g in dmerged) * (1.0 / 768)
    second = sum(jnp.sum(g * n, axis=-1, keepdims=True) for g, n in zip(dmerged, normed)) * (1.0 / 768)
    for d in range(4):
        dfine = (rstd * (dmerged[d] - first - normed[d] * second)).astype(BF).astype(F32)
        up = upstream[TOK * d : TOK * (d + 1), :].astype(F32)
        own_out[TOK * d : TOK * (d + 1), :] = (up + dfine).astype(BF)
    pieces = dot(send[...], own_out[...]).astype(BF)
    row_out[...] = pieces[:ROW_PIECE]
    col_out[...] = pieces[ROW_PIECE : ROW_PIECE + COL_PIECE]
    corner_out[...] = pieces[ROW_PIECE + COL_PIECE :]


def moved(value, lat, lon):
    lats, lons = lax.axis_size("lat"), lax.axis_size("lon")
    if lat == 0:
        pairs = [(source, (source + lon) % lons) for source in range(lons)]
        return lax.ppermute(value, "lon", pairs)
    if lon == 0:
        pairs = [(source, (source + lat) % lats) for source in range(lats)]
        return lax.ppermute(value, "lat", pairs)
    pairs = [
        (a * lons + b, (a + lat) % lats * lons + (b + lon) % lons)
        for a in range(lats)
        for b in range(lons)
    ]
    return lax.ppermute(value, ("lat", "lon"), pairs)


def exchanged(pieces, step):
    row, col, corner = pieces
    return moved(row, step, 0), moved(col, 0, step), moved(corner, step, step)


class Arriving:
    def __init__(self, source, target, semaphore):
        self.copy = pltpu.make_async_copy(source, target, semaphore)
        self.target = target
        self.shape = target.shape
        self.waiting = True
        self.copy.start()

    def __getitem__(self, index):
        if self.waiting:
            self.copy.wait()
            self.waiting = False
        return self.target[index]


def call(kernel, out_shapes, *operands, scratch=(), scalars=0, late=(), hbm_out=()):
    shapes = [jax.ShapeDtypeStruct(shape, dtype) for shape, dtype in out_shapes]
    scalar, array = pl.BlockSpec(memory_space=pltpu.SMEM), pl.BlockSpec(memory_space=pltpu.VMEM)
    remote = pl.BlockSpec(memory_space=pltpu.HBM)
    count = len(operands)
    order = [i for i in range(scalars, count) if i not in late] + list(late)
    landing = [pltpu.VMEM(operands[i].shape, operands[i].dtype) for i in order]
    landing.append(pltpu.SemaphoreType.DMA((len(order),)))

    def whole(*refs):
        inputs, others = list(refs[:count]), refs[count : len(refs) - len(landing)]
        spaces = refs[len(refs) - len(landing) :]
        for k, i in enumerate(order):
            inputs[i] = Arriving(inputs[i], spaces[k], spaces[-1].at[k])
        kernel(*inputs, *others)

    return pl.pallas_call(
        whole,
        out_shape=shapes,
        in_specs=[scalar if i < scalars else remote for i in range(count)],
        out_specs=[remote if i in hbm_out else array for i in range(len(shapes))],
        scratch_shapes=list(scratch) + landing,
        compiler_params=pltpu.CompilerParams(vmem_limit_bytes=VMEM),
        name=kernel.__name__,
    )(*operands)


def swapped(value, step):
    pairs = [(source, source ^ step) for source in range(lax.axis_size("lon"))]
    return lax.ppermute(value, "lon", pairs)


def on_device(fields, upstream, bias_f, bias_c, w_qkv_f, w_proj_f, w_merge, w_qkv_c, w_proj_c, w_split):
    windows, quartets = window_order(), quartet_order()
    last = (lax.axis_index("lat") == lax.axis_size("lat") - 1).astype(jnp.int32).reshape(1)
    odd = lax.axis_index("lon") % 2
    parity = odd.astype(jnp.int32).reshape(1)

    fields = fields.transpose(0, 2, 1, 3)
    upstream = upstream.transpose(0, 2, 1, 3).reshape(576, 192)
    natural = natural_order()
    place = {cell: index for index, cell in enumerate(natural)}
    pieces = call(cut, [((2, 6, 3, 192), BF), ((2, 6, LAT, 192), BF), ((2, 6, 3, 192), BF)], fields)
    row, col, corner = exchanged(pieces, -1)
    (up,) = call(
        reordered, [((576, 192), BF)], one_hot([place[cell] for cell in quartets], 576), upstream
    )
    row, col, corner, up = lax.optimization_barrier((row, col, corner, up))
    piece_shapes = [((size, 192), BF) for size in (ROW_PIECE, COL_PIECE, CORNER)]
    x, qkv, weights, mixed, *pieces = call(
        fine_forward,
        [((576, 192), BF), ((576, 768), BF), ((NWF, 6 * TOK, TOK), BF), ((576, 192), BF)] + piece_shapes,
        last, window_table(), last_window_table(), fields, row, col, corner, bias_f.transpose(0, 2, 3, 1, 4), w_qkv_f, w_proj_f,
        scratch=[
            pltpu.VMEM((2, LON, LAT + 8, 192), F32),
            pltpu.VMEM((6, 24, LANES), F32),
            pltpu.VMEM((576, 192), BF),
            pltpu.VMEM((576, 768), BF),
            pltpu.VMEM((NWF, 6 * TOK, TOK), BF),
            pltpu.SemaphoreType.DMA((6,)),
        ],
        late=(8, 7, 9, 2),
        hbm_out=(0, 1, 2),
        scalars=1,
    )
    row, col, corner = exchanged(pieces, 1)
    (stripes_c,) = call(expand, [((24, 24, LANES), F32)], bias_c.transpose(0, 2, 3, 1, 4))
    row, col, corner, stripes_c = lax.optimization_barrier((row, col, corner, stripes_c))
    fine, coarse_in, queries, pairs = call(
        merge_forward,
        [((576, 192), BF), ((TOK, 384), BF), ((TOK, 384), BF), ((TOK, 768), BF)],
        gather_table(windows, back_pieces(), unrolled_from(quartets)),
        mixed, row, col, corner, w_merge, w_qkv_c,
        late=(5, 6),
    )
    far = swapped(pairs, 1)
    result_q, input_back, own_back, far_back, totals_c = call(
        coarse_middle,
        [
            ((576, 192), BF),
            ((TOK, 384), BF),
            ((TOK, 1152), F32),
            ((TOK, 768), BF),
            ((24, 24, LANES), F32),
        ],
        parity, queries, pairs, far, coarse_in, fine, up, stripes_c, w_proj_c, w_split,
        scratch=[
            pltpu.VMEM((TOK, 384), F32),
            pltpu.VMEM((NWC, 3, 4 * HALF, TOK), BF),
            pltpu.VMEM((TOK, 384), F32),
        ],
        scalars=1,
        late=(4, 8, 9, 5, 6),
    )
    returned = swapped(far_back, 1)
    fine_back, *pieces = call(
        merge_backward,
        [((576, 192), BF)] + piece_shapes,
        send_table(quartets, forward_pieces()),
        own_back, returned, coarse_in, input_back, fine, up, w_merge, w_qkv_c,
        late=(3, 4, 5, 7, 6, 0),
    )
    row, col, corner = exchanged(pieces, -1)
    (packed_c,) = call(
        pack, [((PACKED, 128), BF)], totals_c, scratch=[pltpu.VMEM((PACKED, 128), F32)]
    )
    bits = jnp.stack([odd, lax.axis_index("lon") // 2 % 2]).astype(jnp.int32)
    row, col, corner, packed_c, bits = lax.optimization_barrier((row, col, corner, packed_c, bits))
    grad_rolled, *rest = call(
        fine_backward,
        [((576, 192), BF)] + piece_shapes + [((PACKED, 128), BF)],
        gather_table(quartets, forward_pieces(), rolled_from(windows)),
        last_window_table(),
        fine_back, row, col, corner, x, qkv, weights, w_qkv_f, w_proj_f,
        scratch=[
            pltpu.VMEM((576, 768), BF),
            pltpu.VMEM((PACKED, 128), F32),
            pltpu.VMEM((24, 24, LANES), F32),
        ],
        late=(10, 7, 8, 9, 6, 1),
    )
    *pieces, packed_f = rest

    row, col, corner = exchanged(pieces, 1)
    sent = jnp.where(odd == 0, packed_f, packed_c)
    kept = jnp.where(odd == 0, packed_c, packed_f)
    kept = kept.astype(F32) + swapped(sent, 1).astype(F32)
    far = lax.axis_index("lon") // 2 % 2
    low, high = kept[: PACKED // 2], kept[PACKED // 2 :]
    sent = jnp.where(far == 0, high, low).astype(BF)
    kept = jnp.where(far == 0, low, high)
    kept = (kept + swapped(sent, 2).astype(F32)).astype(BF)
    recv = swapped(kept, 4)
    place = {cell: index for index, cell in enumerate(quartets)}
    (result,) = call(
        reordered, [((576, 192), BF)], one_hot([place[cell] for cell in natural], 576), result_q
    )
    kept, recv, result = lax.optimization_barrier((kept, recv, result))
    kept = (kept.astype(F32) + recv.astype(F32)).astype(BF)
    recv = swapped(kept, 12)
    kept, recv, row, col, corner = lax.optimization_barrier((kept, recv, row, col, corner))
    kept = (kept.astype(F32) + recv.astype(F32)).astype(BF)
    recv = swapped(kept, 16)
    (grad_fields,) = call(
        assemble,
        [((576, 192), BF)],
        gather_table(windows, back_pieces(), unrolled_from(natural)),
        grad_rolled, row, col, corner,
    )
    kept, recv, grad_fields = lax.optimization_barrier((kept, recv, grad_fields))
    kept = (kept.astype(F32) + recv.astype(F32)).astype(BF)
    kept_far = swapped(kept, 2)
    grad_bias_f, grad_bias_c = call(
        unpack,
        [((1, 6, REL, NWF, TOK), F32), ((1, 12, REL, NWC, TOK), F32)],
        bits, kept, kept_far, swapped(kept, 1), swapped(kept_far, 1),
        scalars=1,
    )
    grad_bias_f = grad_bias_f.transpose(0, 3, 1, 2, 4)
    grad_bias_c = grad_bias_c.transpose(0, 3, 1, 2, 4)
    result = result.reshape(2, LON, LAT, 192).transpose(0, 2, 1, 3)
    grad_fields = grad_fields.reshape(2, LON, LAT, 192).transpose(0, 2, 1, 3)
    return (result, grad_fields, grad_bias_f, grad_bias_c)


def solution(mesh):
    grid = P(None, "lat", "lon", None)
    table = P(None, "lat", None, None, None)
    return jax.shard_map(
        on_device,
        mesh=mesh,
        in_specs=(grid, grid, table, table, P(), P(), P(), P(), P(), P()),
        out_specs=(grid, grid, table, table),
        check_vma=False,
    )
```

```python
import math

import jax
import jax.numpy as jnp
import numpy as np
from jax import lax
from jax.experimental import pallas as pl
from jax.experimental.pallas import tpu as pltpu
from jax.sharding import PartitionSpec as P

WIN_Z = 2
WIN_LAT = 6
WIN_LON = 12
ROWS = WIN_Z * WIN_LAT
TOK = ROWS * WIN_LON
HALF = TOK // 2
REL = 2 * WIN_LON - 1
WIDE = REL * ROWS
EPS = 1e-05
MASKED = -1000000000.0
HEAD = 32
SCALE = 1.0 / math.sqrt(HEAD)
LAT = 24
LON = 12
NWF = LAT // WIN_LAT
NWC = LAT // 2 // WIN_LAT
BF = jnp.bfloat16
F32 = jnp.float32
ROW_PIECE, COL_PIECE, CORNER = 48, 288, 48
VMEM = 56 * 1024 * 1024
TABLE = 24 + 3
LANES = 384
PACKED = 24 * TABLE + 8
BATCH = 4


def natural_order():
    return [(z, i, j) for z in range(2) for j in range(LON) for i in range(LAT)]


def window_order():
    return [
        (z, WIN_LAT * w + l, n)
        for w in range(NWF)
        for n in range(LON)
        for z in range(2)
        for l in range(WIN_LAT)
    ]


def quartet_order():
    return [
        (z, 2 * (WIN_LAT * w + l) + di, 2 * n + dj)
        for di in range(2)
        for dj in range(2)
        for w in range(NWC)
        for n in range(LON // 2)
        for z in range(2)
        for l in range(WIN_LAT)
    ]


def one_hot(rows, columns):
    table = np.zeros((len(rows), columns), np.float32)
    for row, column in enumerate(rows):
        if column is not None:
            table[row, column] = 1.0
    return jnp.asarray(table, BF)


def forward_pieces():
    row = [(z, i, j) for z in range(2) for i in range(3) for j in range(6, LON)]
    col = [(z, i, j) for z in range(2) for i in range(LAT) for j in range(6)]
    corner = [(z, i, j) for z in range(2) for i in range(3) for j in range(6)]
    return row, col, corner


def back_pieces():
    row = [(z, i, j) for z in range(2) for i in range(LAT - 3, LAT) for j in range(6)]
    col = [cell for cell in window_order() if cell[2] >= 6]
    corner = [(z, i, j) for z in range(2) for i in range(LAT - 3, LAT) for j in range(6, LON)]
    return row, col, corner


def padded_pieces(pieces):
    sizes = (ROW_PIECE, COL_PIECE, CORNER)
    return [cells + [None] * (size - len(cells)) for cells, size in zip(pieces, sizes)]


def send_table(own_order, pieces):
    place = {cell: index for index, cell in enumerate(own_order)}
    cells = sum(padded_pieces(pieces), [])
    return one_hot([None if cell is None else place[cell] for cell in cells], len(own_order))


def gather_table(own_order, pieces, wanted):
    tables = [{cell: index for index, cell in enumerate(own_order)}]
    starts = [0]
    for cells in pieces:
        tables.append({cell: index for index, cell in enumerate(cells)})
    starts = [0, len(own_order), len(own_order) + ROW_PIECE, len(own_order) + ROW_PIECE + COL_PIECE]
    total = len(own_order) + ROW_PIECE + COL_PIECE + CORNER
    rows = []
    for entry in wanted:
        rows.append(None if entry is None else starts[entry[0]] + tables[entry[0]][entry[1]])
    return one_hot(rows, total)


def window_start(w):
    return (WIN_LAT * w + WIN_LAT // 2) // 8 * 8 if w < NWF - 1 else LAT - 8


def window_table():
    rows = []
    for w in range(NWF):
        offset = WIN_LAT * w + WIN_LAT // 2 - window_start(w)
        for n in range(LON):
            for z in range(2):
                for l in range(WIN_LAT):
                    rows.append(((1 - z) * LON + n) * 16 + offset + l)
    return one_hot(rows, 2 * LON * 16)


def last_window_table():
    place = {cell: index for index, cell in enumerate(window_order()[-TOK:])}
    row, _, corner = padded_pieces(back_pieces())
    return one_hot([None if cell is None else place[cell] for cell in row + corner], TOK)


def rolled_from(cells):
    wanted = []
    for z, i, j in cells:
        z, i, j = 1 - z, i + 3, j + 6
        kind = (1 if i >= LAT else 0) + (2 if j >= LON else 0)
        wanted.append((kind, (z, i % LAT, j % LON)))
    return wanted


def unrolled_from(cells):
    wanted = []
    for cell in cells:
        z, i, j = cell
        z, i, j = 1 - z, i - 3, j - 6
        kind = (1 if i < 0 else 0) + (2 if j < 0 else 0)
        wanted.append((kind, (z, i % LAT, j % LON)))
    return wanted


def dot(a, b):
    return lax.dot_general(a, b, (((1,), (0,)), ((), ())), preferred_element_type=F32)


def dot_nt(a, b):
    return lax.dot_general(a, b, (((1,), (1,)), ((), ())), preferred_element_type=F32)


def dot_tn(a, b):
    return lax.dot_general(a, b, (((0,), (0,)), ((), ())), preferred_element_type=F32)


def normalise(values, count):
    mean = jnp.sum(values, axis=-1, keepdims=True) * (1.0 / count)
    centred = values - mean
    spread = jnp.sum(centred * centred, axis=-1, keepdims=True) * (1.0 / count)
    rstd = lax.rsqrt(spread + EPS)
    return centred * rstd, rstd


def normalise_back(cotangent, normed, rstd, count):
    first = jnp.sum(cotangent, axis=-1, keepdims=True) * (1.0 / count)
    second = jnp.sum(cotangent * normed, axis=-1, keepdims=True) * (1.0 / count)
    return rstd * (cotangent - first - normed * second)


def head_stack(values, heads):
    lanes = lax.broadcasted_iota(jnp.int32, values.shape, 1) // HEAD
    return jnp.concatenate([jnp.where(lanes == h, values, 0.0) for h in range(heads)], axis=0).astype(BF)


def head_sum(stacked, heads):
    rows = stacked.shape[0] // heads
    lanes = lax.broadcasted_iota(jnp.int32, (rows, 128), 1) // HEAD
    total = stacked[:rows]
    for h in range(1, heads):
        total = jnp.where(lanes == h, stacked[h * rows : (h + 1) * rows], total)
    return jnp.where(lanes < heads, total, 0.0)


def softmax(scores, ones):
    highest = jnp.max(scores, axis=-1, keepdims=True)
    powers = jnp.exp(scores - highest)
    rounded = powers.astype(BF)
    inverse = 1.0 / dot(rounded, ones)
    weights = powers * jnp.concatenate([inverse, inverse[:, : TOK - 128]], axis=1)
    return rounded, inverse, weights.astype(BF)


def scores_back(weights, dweights, ones):
    weights32 = weights.astype(F32)
    product = weights32 * dweights
    total = dot(product.astype(BF), ones)
    return product - weights32 * jnp.concatenate([total, total[:, : TOK - 128]], axis=1)


def rotated(value, shift, axis):
    size = value.shape[axis]
    return pltpu.roll(value, shift % size, axis)


def sheared(value, index, bits, lanes):
    for bit in range(bits):
        value = jnp.where((index >> bit) & 1 == 1, rotated(value, lanes << bit, 2), value)
    return value


def strided(value):
    tiles = []
    for start in range(0, value.shape[1], 8):
        tile = pltpu.roll(value[:, start : start + 8], 0, 2, stride=ROWS, stride_axis=1)
        tiles.append(rotated(tile, ROWS * start, 2))
    return jnp.concatenate(tiles, axis=1)


def raised(value, amount, steps):
    for step in steps:
        value = jnp.where(amount & step != 0, rotated(value, step, 1), value)
    return value


def stripes_of(table, stripes_out):
    heads = table.shape[0]
    index = lax.broadcasted_iota(jnp.int32, (1, 24, LANES), 1)
    amount = (lax.broadcasted_iota(jnp.int32, (1, 8, LANES), 2) // ROWS + 10) & 31
    table = jnp.concatenate([table, jnp.zeros((heads, REL, LANES - TOK), F32)], axis=2)
    table = jnp.concatenate([table, jnp.zeros((heads, 1, LANES), F32)], axis=1)
    table = rotated(sheared(table, index, 5, -ROWS), 22 * ROWS, 2)
    tiles = [table[:, 0:8], table[:, 8:16], table[:, 16:24], jnp.zeros((heads, 8, LANES), F32)]
    tiles = [jnp.where(amount & 16 != 0, tiles[k - 2], tiles[k]) for k in range(4)]
    tiles = [jnp.where(amount & 8 != 0, tiles[k - 1], tiles[k]) for k in range(4)]
    stripes = jnp.concatenate([tiles[3], tiles[0], tiles[1]], axis=1)
    stripes = raised(stripes, amount[:, :1], (4, 2, 1))[:, 8:]
    stripes = sheared(stripes, index[:, :16], 4, -ROWS)
    stripes = jnp.where(index[:, :16] < ROWS, stripes, 0.0)
    stripes = jnp.concatenate([stripes, jnp.zeros((heads, 8, LANES), F32)], axis=1)
    stripes_out[...] = stripes + rotated(rotated(stripes, ROWS, 2), ROWS, 1)


def stripes_back(stripes):
    heads = stripes.shape[0]
    index = lax.broadcasted_iota(jnp.int32, (1, 16, LANES), 1)
    amount = (22 - lax.broadcasted_iota(jnp.int32, (1, 8, LANES), 2) // ROWS) & 31
    stripes = stripes + rotated(rotated(stripes, -ROWS, 2), ROWS, 1)
    stripes = strided(jnp.where(index < ROWS, stripes[:, :16], 0.0))
    blank = jnp.zeros((heads, 8, LANES), F32)
    stripes = raised(jnp.concatenate([stripes, blank], axis=1), amount[:, :1], (1, 2, 4))
    tiles = [stripes[:, 0:8], stripes[:, 8:16], stripes[:, 16:24], blank]
    tiles = [jnp.where(amount & 8 != 0, tiles[k - 1], tiles[k]) for k in range(4)]
    tiles = [jnp.where(amount & 16 != 0, tiles[k - 2], tiles[k]) for k in range(3)]
    return rotated(strided(jnp.concatenate(tiles, axis=1)), -22 * ROWS, 2)


def expand(table, stripes_out):
    _, heads, _, windows, _ = table.shape
    batch = BATCH if heads % BATCH == 0 else 3
    for w in range(windows):
        for start in range(0, heads, batch):
            place = stripes_out.at[heads * w + start : heads * w + start + batch]
            stripes_of(table[0, start : start + batch, :, w, :], place)


def pack(totals, packed_out, packed):
    pack_tables(totals, packed)
    packed_out[...] = packed[...].astype(BF)


def pack_tables(totals, packed):
    packed[24 * TABLE :, :] = jnp.zeros((PACKED - 24 * TABLE, 128), F32)
    rest = jnp.zeros((24, 128), F32)
    for start in range(0, 24, BATCH):
        tables = stripes_back(totals[start : start + BATCH])
        for head in range(start, start + BATCH):
            rest = pack_table(tables[head - start], head, packed, rest)


def pack_table(table, head, packed, rest):
    packed[24 * head : 24 * head + 24, :] = table[:, :128]
    rest = rest + rotated(table[:, 128:256], 16 * (head % 8), 1)
    if head % 8 == 7:
        start = 24 * (24 + head // 8)
        packed[start : start + 24, :] = rest
        rest = jnp.zeros((24, 128), F32)
    return rest


def mask_of(last_row):
    first = lax.broadcasted_iota(jnp.int32, (24, LANES), 0) % ROWS
    second = lax.broadcasted_iota(jnp.int32, (24, LANES), 1) % ROWS
    half = WIN_Z // 2
    level = (first // WIN_LAT >= WIN_Z - half) != (second // WIN_LAT >= WIN_Z - half)
    if last_row is not None:
        half = WIN_LAT // 2
        row = (first % WIN_LAT >= WIN_LAT - half) != (second % WIN_LAT >= WIN_LAT - half)
        level = level | (row & (last_row == 1))
    return jnp.where(level, MASKED, 0.0).astype(F32)


def padded_lanes(weights):
    blocks = []
    for start in range(0, weights.shape[1], 192):
        blocks += [weights[:, start : start + 192], jnp.zeros((weights.shape[0], 64), weights.dtype)]
    return jnp.concatenate(blocks, axis=1)


def cut(fields, row_out, col_out, corner_out):
    row_out[...] = fields[:, 6:, :3]
    col_out[...] = fields[:, :6]
    corner_out[...] = fields[:, :6, :3]


def fine_forward(last, gather, send, fields, row, col, corner, table, w_qkv_in, w_proj_in, x_out, qkv_out, weights_out, mixed_out, row_out, col_out, corner_out, rolled, stripes, x_s, qkv_s, weights_s, sems):
    rolled[:, :, LAT:, :] = jnp.zeros((2, LON, 8, 192), F32)
    rolled[:, :6, :LAT, :] = fields[:, 6:].astype(F32)
    rolled[:, 6:, :LAT, :] = col[...].astype(F32)
    rolled[:, :6, LAT : LAT + 3, :] = row[...].astype(F32)
    rolled[:, 6:, LAT : LAT + 3, :] = corner[...].astype(F32)
    x = []
    for w in range(NWF):
        start = window_start(w)
        sources = rolled[:, :, start : start + 16].reshape(2 * LON * 16, 192).astype(BF)
        x.append(dot(gather[TOK * w : TOK * w + TOK, :], sources))
    x = jnp.concatenate(x, axis=0)
    x_s[...] = x.astype(BF)
    copies = [pltpu.make_async_copy(x_s, x_out, sems.at[0])]
    copies[-1].start()
    normed, _ = normalise(x, 192)
    qkv_s[...] = dot(normed.astype(BF), padded_lanes(w_qkv_in[...])).astype(BF)
    copies.append(pltpu.make_async_copy(qkv_s, qkv_out, sems.at[1]))
    copies[-1].start()
    w_proj = jnp.concatenate([w_proj_in[...], jnp.zeros((64, 192), BF)], axis=0)
    ones = jnp.ones((TOK, 128), BF)
    level_mask = mask_of(None)
    last_mask = mask_of(last[0])
    sent = []
    for w in range(NWF):
        rows = pl.ds(w * TOK, TOK)
        for start in range(0, 6, 3):
            stripes_of(table[0, start : start + 3, :, w, :], stripes.at[start : start + 3])
        blended = []
        for group, heads in ((0, 4), (1, 2)):
            queries = qkv_s[rows, 128 * group : 128 * group + 128]
            keys = qkv_s[rows, 256 + 128 * group : 256 + 128 * group + 128]
            values = qkv_s[rows, 512 + 128 * group : 512 + 128 * group + 128]
            bias = []
            for h in range(heads):
                stripe = stripes[4 * group + h] + (last_mask if w == NWF - 1 else level_mask)
                bias += [rotated(stripe, -(11 - 2 * m) * ROWS, 1)[:, :TOK] for m in range(6)]
            bias = jnp.concatenate(bias, axis=0)
            queries = head_stack(queries.astype(F32), heads)
            rounded, inverse, weights = softmax(dot_nt(queries, keys) * SCALE + bias, ones)
            weights_s[w, 4 * TOK * group : 4 * TOK * group + heads * TOK, :] = weights
            blended.append(head_sum(dot(rounded, values) * inverse, heads))
        blended = jnp.concatenate(blended, axis=1).astype(BF)
        mixed = x[w * TOK : (w + 1) * TOK] + dot(blended, w_proj)
        sent.append(mixed[HALF:])
        mixed_out[rows, :] = mixed.astype(BF)
        copies.append(pltpu.make_async_copy(weights_s.at[w], weights_out.at[w], sems.at[2 + w]))
        copies[-1].start()
    col_out[...] = jnp.concatenate(sent, axis=0).astype(BF)
    pieces = dot(send[...], mixed_out[TOK * (NWF - 1) :, :]).astype(BF)
    row_out[...] = pieces[:ROW_PIECE]
    corner_out[...] = pieces[ROW_PIECE:]
    for copy in copies:
        copy.wait()


def fine_backward(bits, gather, send, own, row, col, corner, x, qkv, weights_in, w_qkv_in, w_proj_in, packed_c, own_out, row_out, col_out, corner_out, sent_out, kept_out, dqkv, packed, totals):
    sources = jnp.concatenate([own[...], row[...], col[...], corner[...]], axis=0)
    dmix = dot(gather[...], sources).astype(BF)
    w_proj = jnp.concatenate([w_proj_in[...], jnp.zeros((64, 192), BF)], axis=0)
    datt = dot_nt(dmix, w_proj).astype(BF)
    ones = jnp.ones((TOK, 128), BF)
    for w in range(NWF):
        rows = pl.ds(w * TOK, TOK)
        for group, heads in ((0, 4), (1, 2)):
            lanes = slice(128 * group, 128 * group + 128)
            queries = qkv[rows, 128 * group : 128 * group + 128]
            keys = qkv[rows, 256 + 128 * group : 256 + 128 * group + 128]
            values = qkv[rows, 512 + 128 * group : 512 + 128 * group + 128]
            grad = datt[w * TOK : (w + 1) * TOK, lanes]
            queries = head_stack(queries.astype(F32), heads)
            grad = head_stack(grad.astype(F32), heads)
            weights = weights_in[w, 4 * TOK * group : 4 * TOK * group + heads * TOK, :]
            dscores = scores_back(weights, dot_nt(grad, values), ones)
            ds = dscores.astype(BF)
            dq = head_sum(dot(ds, keys), heads)
            dk = dot_tn(ds, queries)
            dv = dot_tn(weights, grad)
            wide = jnp.concatenate([dscores, jnp.zeros((heads * TOK, LANES - TOK), F32)], axis=1)
            for h in range(heads):
                total = jnp.zeros((24, LANES), F32)
                for m in range(6):
                    block = wide[TOK * h + 24 * m : TOK * h + 24 * m + 24]
                    total = total + rotated(block, (11 - 2 * m) * ROWS, 1)
                totals[6 * w + 4 * group + h] = total
            dqkv[rows, 128 * group : 128 * group + 128] = (dq * SCALE).astype(BF)
            dqkv[rows, 256 + 128 * group : 256 + 128 * group + 128] = (dk * SCALE).astype(BF)
            dqkv[rows, 512 + 128 * group : 512 + 128 * group + 128] = dv.astype(BF)
    pack_tables(totals, packed)
    even = bits[0] == 0
    mine = packed[...].astype(BF).astype(F32)
    other = packed_c[...].astype(F32)
    sent_out[...] = jnp.where(even, mine, other).astype(BF)
    kept_out[...] = jnp.where(even, other, mine).astype(BF)
    dnormed = dot_nt(dqkv[...], padded_lanes(w_qkv_in[...])).astype(BF).astype(F32)
    normed, rstd = normalise(x[...].astype(F32), 192)
    dx = normalise_back(dnormed, normed, rstd, 192).astype(BF).astype(F32)
    grad_rolled = dmix.astype(F32) + dx
    own_out[...] = grad_rolled.astype(BF)
    sent = [grad_rolled[TOK * w + HALF : TOK * w + TOK] for w in range(NWF)]
    col_out[...] = jnp.concatenate(sent, axis=0).astype(BF)
    pieces = dot(send[...], own_out[TOK * (NWF - 1) :, :]).astype(BF)
    row_out[...] = pieces[:ROW_PIECE]
    corner_out[...] = pieces[ROW_PIECE:]


def reordered(gather, values, out):
    out[...] = dot(gather[...], values[...]).astype(BF)


def unpack(bits, kept, kept_far, other, other_far, fine_out, coarse_out):
    even, low = bits[0] == 0, bits[1] == 0
    halves = [part[...].astype(F32) for part in (kept, kept_far, other, other_far)]
    tables = []
    for near, far in (halves[:2], halves[2:]):
        tables.append(
            jnp.concatenate([jnp.where(low, near, far), jnp.where(low, far, near)], axis=0)
        )
    coarse = jnp.where(even, tables[0], tables[1])
    fine = jnp.where(even, tables[1], tables[0])
    for packed, out, heads in ((fine, fine_out, 6), (coarse, coarse_out, 12)):
        for head in range(24):
            rest = 24 * (24 + head // 8)
            rest = rotated(packed[rest : rest + 24], -16 * (head % 8), 1)[:, : TOK - 128]
            table = jnp.concatenate([packed[24 * head : 24 * head + 24], rest], axis=1)
            out[0, head % heads, :, head // heads, :] = table[:REL]


def assemble(gather, own, row, col, corner, out):
    sources = jnp.concatenate([own[...], row[...], col[...], corner[...]], axis=0)
    out[...] = dot(gather[...], sources).astype(BF)


def merge_forward(gather, own, row, col, corner, w_merge, w_qkv, fine_out, coarse_out, queries_out, pairs_out):
    sources = jnp.concatenate([own[...], row[...], col[...], corner[...]], axis=0)
    fine = dot(gather[...], sources)
    fine_out[...] = fine.astype(BF)
    quarter = [fine[TOK * d : TOK * (d + 1)] for d in range(4)]
    mean = sum(jnp.sum(q, axis=-1, keepdims=True) for q in quarter) * (1.0 / 768)
    centred = [q - mean for q in quarter]
    spread = sum(jnp.sum(c * c, axis=-1, keepdims=True) for c in centred) * (1.0 / 768)
    rstd = lax.rsqrt(spread + EPS)
    coarse = jnp.zeros((TOK, 384), F32)
    for d in range(4):
        coarse = coarse + dot((centred[d] * rstd).astype(BF), w_merge[192 * d : 192 * d + 192, :])
    coarse = coarse.astype(BF)
    coarse_out[...] = coarse
    normed, _ = normalise(coarse.astype(F32), 384)
    projected = dot(normed.astype(BF), w_qkv[...])
    queries_out[...] = projected[:, :384].astype(BF)
    pairs_out[...] = projected[:, 384:].astype(BF)


def coarse_middle(parity, queries_in, pairs_in, far_in, coarse_in, fine, upstream, stripes, w_proj, w_split, result_out, input_back_out, own_back_out, far_back_out, totals, attended, weights_ref, dattended):
    pairs = pairs_in[...].astype(F32)
    far = far_in[...].astype(F32)
    queries32 = queries_in[...].astype(F32)
    joined = []
    first = parity[0] == 0
    ones = jnp.ones((TOK, 128), BF)
    lanes = lax.broadcasted_iota(jnp.int32, (24, 128), 1)
    for w in range(NWC):
        joined.append(
            jnp.concatenate([pairs[HALF * w : HALF * w + HALF], far[HALF * w : HALF * w + HALF]], axis=0).astype(BF)
        )
    for w in range(NWC):
        for group in range(3):
            queries = queries32[HALF * w : HALF * w + HALF, 128 * group : 128 * group + 128]
            keys = joined[w][:, 128 * group : 128 * group + 128]
            values = joined[w][:, 384 + 128 * group : 384 + 128 * group + 128]
            bias = []
            for h in range(4):
                stripe = stripes[12 * w + 4 * group + h]
                near = rotated(stripe, -84, 1)[:, :128]
                other = jnp.where(first, rotated(stripe, -84, 1), rotated(stripe, 60, 1))[:, :256]
                for m in range(3):
                    offset = 48 - 24 * m
                    left = rotated(near, -offset, 1)
                    right = rotated(other, -offset, 1)[:, :TOK]
                    left = jnp.where(lanes < HALF, left, right[:, :128])
                    bias.append(jnp.concatenate([left, right[:, 128:]], axis=1))
            bias = jnp.concatenate(bias, axis=0)
            scores = dot_nt(head_stack(queries, 4), keys) * SCALE + bias
            rounded, inverse, weights = softmax(scores, ones)
            weights_ref[w, group] = weights
            total = head_sum(dot(rounded, values) * inverse, 4)
            attended[HALF * w : HALF * w + HALF, 128 * group : 128 * group + 128] = total
    coarse32 = coarse_in[...].astype(F32)
    coarse_out = (coarse32 + dot(attended[...].astype(BF), w_proj[...])).astype(BF)
    normed, rstd = normalise(coarse_out.astype(F32), 384)
    normed_b = normed.astype(BF)
    back = jnp.zeros((TOK, 384), F32)
    for d in range(4):
        part = w_split[:, 192 * d : 192 * d + 192]
        up = upstream[TOK * d : TOK * d + TOK, :]
        widened = dot(normed_b, part)
        result_out[TOK * d : TOK * d + TOK, :] = (fine[TOK * d : TOK * d + TOK, :].astype(F32) + widened).astype(BF)
        back = back + dot_nt(up, part)
    back = back.astype(BF).astype(F32)
    input_back = normalise_back(back, normed, rstd, 384).astype(BF)
    input_back_out[...] = input_back
    dattended[...] = dot_nt(input_back, w_proj[...]).astype(BF).astype(F32)
    for w in range(NWC):
        for group in range(3):
            queries = queries32[HALF * w : HALF * w + HALF, 128 * group : 128 * group + 128]
            keys = joined[w][:, 128 * group : 128 * group + 128]
            values = joined[w][:, 384 + 128 * group : 384 + 128 * group + 128]
            grad = dattended[HALF * w : HALF * w + HALF, 128 * group : 128 * group + 128]
            queries = head_stack(queries, 4)
            grad = head_stack(grad, 4)
            weights = weights_ref[w, group]
            dscores = scores_back(weights, dot_nt(grad, values), ones)
            ds = dscores.astype(BF)
            dq = head_sum(dot(ds, keys), 4)
            dk = dot_tn(ds, queries)
            dv = dot_tn(weights, grad)
            blank = jnp.zeros((24, 256 - TOK), F32)
            for h in range(4):
                near = jnp.zeros((24, 128), F32)
                other = jnp.zeros((24, 256), F32)
                for m in range(3):
                    offset = 48 - 24 * m
                    block = dscores[HALF * h + 24 * m : HALF * h + 24 * m + 24]
                    left = jnp.where(lanes < HALF, block[:, :128], 0.0)
                    right = jnp.concatenate([block[:, :128] - left, block[:, 128:], blank], axis=1)
                    near = near + rotated(left, offset, 1)
                    other = other + rotated(right, offset - HALF, 1)
                blank_lanes = jnp.zeros((24, LANES - 128), F32)
                near = rotated(jnp.concatenate([near, blank_lanes], axis=1), 84, 1)
                other = jnp.concatenate([other[:, :128], blank_lanes], axis=1)
                other = jnp.where(first, rotated(other, 156, 1), rotated(other, 12, 1))
                totals[12 * w + 4 * group + h] = near + other
            part = slice(HALF * w, HALF * w + HALF)
            cols = slice(128 * group, 128 * group + 128)
            own_back_out[part, cols] = dq * SCALE
            own_back_out[part, 384 + 128 * group : 384 + 128 * group + 128] = dk[:HALF] * SCALE
            own_back_out[part, 768 + 128 * group : 768 + 128 * group + 128] = dv[:HALF]
            far_back_out[part, cols] = (dk[HALF:] * SCALE).astype(BF)
            far_back_out[part, 384 + 128 * group : 384 + 128 * group + 128] = dv[HALF:].astype(BF)


def merge_backward(send, own_back, returned, coarse_in, input_back, fine, upstream, w_merge, w_qkv, own_out, row_out, col_out, corner_out):
    returned32 = returned[...].astype(F32)
    dq = own_back[:, :384].astype(BF)
    dkv = (own_back[:, 384:] + returned32).astype(BF)
    dnormed = dot_nt(dq, w_qkv[:, :384]) + dot_nt(dkv, w_qkv[:, 384:])
    dnormed = dnormed.astype(BF).astype(F32)
    normed, rstd = normalise(coarse_in[...].astype(F32), 384)
    dx = normalise_back(dnormed, normed, rstd, 384).astype(BF)
    dcoarse = (input_back[...].astype(F32) + dx.astype(F32)).astype(BF)
    quarter = [fine[TOK * d : TOK * (d + 1), :].astype(F32) for d in range(4)]
    mean = sum(jnp.sum(q, axis=-1, keepdims=True) for q in quarter) * (1.0 / 768)
    centred = [q - mean for q in quarter]
    spread = sum(jnp.sum(c * c, axis=-1, keepdims=True) for c in centred) * (1.0 / 768)
    rstd = lax.rsqrt(spread + EPS)
    normed = [c * rstd for c in centred]
    dmerged = [
        dot_nt(dcoarse, w_merge[192 * d : 192 * d + 192, :]).astype(BF).astype(F32) for d in range(4)
    ]
    first = sum(jnp.sum(g, axis=-1, keepdims=True) for g in dmerged) * (1.0 / 768)
    second = sum(jnp.sum(g * n, axis=-1, keepdims=True) for g, n in zip(dmerged, normed)) * (1.0 / 768)
    for d in range(4):
        dfine = (rstd * (dmerged[d] - first - normed[d] * second)).astype(BF).astype(F32)
        up = upstream[TOK * d : TOK * (d + 1), :].astype(F32)
        own_out[TOK * d : TOK * (d + 1), :] = (up + dfine).astype(BF)
    pieces = dot(send[...], own_out[...]).astype(BF)
    row_out[...] = pieces[:ROW_PIECE]
    col_out[...] = pieces[ROW_PIECE : ROW_PIECE + COL_PIECE]
    corner_out[...] = pieces[ROW_PIECE + COL_PIECE :]


def moved(value, lat, lon):
    lats, lons = lax.axis_size("lat"), lax.axis_size("lon")
    if lat == 0:
        pairs = [(source, (source + lon) % lons) for source in range(lons)]
        return lax.ppermute(value, "lon", pairs)
    if lon == 0:
        pairs = [(source, (source + lat) % lats) for source in range(lats)]
        return lax.ppermute(value, "lat", pairs)
    pairs = [
        (a * lons + b, (a + lat) % lats * lons + (b + lon) % lons)
        for a in range(lats)
        for b in range(lons)
    ]
    return lax.ppermute(value, ("lat", "lon"), pairs)


def exchanged(pieces, step):
    row, col, corner = pieces
    return moved(row, step, 0), moved(col, 0, step), moved(corner, step, step)


class Arriving:
    def __init__(self, source, target, semaphore):
        self.copy = pltpu.make_async_copy(source, target, semaphore)
        self.target = target
        self.shape = target.shape
        self.waiting = True
        self.copy.start()

    def __getitem__(self, index):
        if self.waiting:
            self.copy.wait()
            self.waiting = False
        return self.target[index]


def call(kernel, out_shapes, *operands, scratch=(), scalars=0, late=(), hbm_out=(), eager=False):
    shapes = [jax.ShapeDtypeStruct(shape, dtype) for shape, dtype in out_shapes]
    scalar, array = pl.BlockSpec(memory_space=pltpu.SMEM), pl.BlockSpec(memory_space=pltpu.VMEM)
    remote = pl.BlockSpec(memory_space=pltpu.HBM)
    count = len(operands)
    limit = VMEM // 4 if eager else VMEM
    order = [] if eager else [i for i in range(scalars, count) if i not in late] + list(late)
    landing = [pltpu.VMEM(operands[i].shape, operands[i].dtype) for i in order]
    if order:
        landing.append(pltpu.SemaphoreType.DMA((len(order),)))

    def whole(*refs):
        inputs, others = list(refs[:count]), refs[count : len(refs) - len(landing)]
        spaces = refs[len(refs) - len(landing) :]
        for k, i in enumerate(order):
            inputs[i] = Arriving(inputs[i], spaces[k], spaces[-1].at[k])
        kernel(*inputs, *others)

    return pl.pallas_call(
        whole,
        out_shape=shapes,
        in_specs=[scalar if i < scalars else remote if i in order else array for i in range(count)],
        out_specs=[remote if i in hbm_out else array for i in range(len(shapes))],
        scratch_shapes=list(scratch) + landing,
        compiler_params=pltpu.CompilerParams(vmem_limit_bytes=limit),
        name=kernel.__name__,
    )(*operands)


def swapped(value, step):
    pairs = [(source, source ^ step) for source in range(lax.axis_size("lon"))]
    return lax.ppermute(value, "lon", pairs)


def on_device(fields, upstream, bias_f, bias_c, w_qkv_f, w_proj_f, w_merge, w_qkv_c, w_proj_c, w_split):
    windows, quartets = window_order(), quartet_order()
    last = (lax.axis_index("lat") == lax.axis_size("lat") - 1).astype(jnp.int32).reshape(1)
    odd = lax.axis_index("lon") % 2
    parity = odd.astype(jnp.int32).reshape(1)

    fields = fields.transpose(0, 2, 1, 3)
    upstream = upstream.transpose(0, 2, 1, 3).reshape(576, 192)
    natural = natural_order()
    place = {cell: index for index, cell in enumerate(natural)}
    pieces = call(cut, [((2, 6, 3, 192), BF), ((2, 6, LAT, 192), BF), ((2, 6, 3, 192), BF)], fields)
    row, col, corner = exchanged(pieces, -1)
    (up,) = call(
        reordered, [((576, 192), BF)], one_hot([place[cell] for cell in quartets], 576), upstream
    )
    row, col, corner, up = lax.optimization_barrier((row, col, corner, up))
    piece_shapes = [((size, 192), BF) for size in (ROW_PIECE, COL_PIECE, CORNER)]
    x, qkv, weights, mixed, *pieces = call(
        fine_forward,
        [((576, 192), BF), ((576, 768), BF), ((NWF, 6 * TOK, TOK), BF), ((576, 192), BF)] + piece_shapes,
        last, window_table(), last_window_table(), fields, row, col, corner, bias_f.transpose(0, 2, 3, 1, 4), w_qkv_f, w_proj_f,
        scratch=[
            pltpu.VMEM((2, LON, LAT + 8, 192), F32),
            pltpu.VMEM((6, 24, LANES), F32),
            pltpu.VMEM((576, 192), BF),
            pltpu.VMEM((576, 768), BF),
            pltpu.VMEM((NWF, 6 * TOK, TOK), BF),
            pltpu.SemaphoreType.DMA((6,)),
        ],
        late=(8, 7, 9, 2),
        hbm_out=(0, 1, 2),
        scalars=1,
    )
    row, col, corner = exchanged(pieces, 1)
    (stripes_c,) = call(expand, [((24, 24, LANES), F32)], bias_c.transpose(0, 2, 3, 1, 4))
    row, col, corner, stripes_c = lax.optimization_barrier((row, col, corner, stripes_c))
    fine, coarse_in, queries, pairs = call(
        merge_forward,
        [((576, 192), BF), ((TOK, 384), BF), ((TOK, 384), BF), ((TOK, 768), BF)],
        gather_table(windows, back_pieces(), unrolled_from(quartets)),
        mixed, row, col, corner, w_merge, w_qkv_c,
        eager=True,
    )
    far = swapped(pairs, 1)
    result_q, input_back, own_back, far_back, totals_c = call(
        coarse_middle,
        [
            ((576, 192), BF),
            ((TOK, 384), BF),
            ((TOK, 1152), F32),
            ((TOK, 768), BF),
            ((24, 24, LANES), F32),
        ],
        parity, queries, pairs, far, coarse_in, fine, up, stripes_c, w_proj_c, w_split,
        scratch=[
            pltpu.VMEM((TOK, 384), F32),
            pltpu.VMEM((NWC, 3, 4 * HALF, TOK), BF),
            pltpu.VMEM((TOK, 384), F32),
        ],
        scalars=1,
        late=(4, 8, 9, 5, 6),
    )
    returned = swapped(far_back, 1)
    fine_back, *pieces = call(
        merge_backward,
        [((576, 192), BF)] + piece_shapes,
        send_table(quartets, forward_pieces()),
        own_back, returned, coarse_in, input_back, fine, up, w_merge, w_qkv_c,
        eager=True,
    )
    row, col, corner = exchanged(pieces, -1)
    (packed_c,) = call(
        pack, [((PACKED, 128), BF)], totals_c, scratch=[pltpu.VMEM((PACKED, 128), F32)]
    )
    bits = jnp.stack([odd, lax.axis_index("lon") // 2 % 2]).astype(jnp.int32)
    row, col, corner, packed_c, bits = lax.optimization_barrier((row, col, corner, packed_c, bits))
    grad_rolled, *rest = call(
        fine_backward,
        [((576, 192), BF)] + piece_shapes + [((PACKED, 128), BF)] * 2,
        bits, gather_table(quartets, forward_pieces(), rolled_from(windows)),
        last_window_table(),
        fine_back, row, col, corner, x, qkv, weights, w_qkv_f, w_proj_f, packed_c,
        scratch=[
            pltpu.VMEM((576, 768), BF),
            pltpu.VMEM((PACKED, 128), F32),
            pltpu.VMEM((24, 24, LANES), F32),
        ],
        scalars=1,
        late=(11, 8, 9, 10, 7, 2, 12),
    )
    *pieces, sent, kept = rest

    row, col, corner = exchanged(pieces, 1)
    kept = kept.astype(F32) + swapped(sent, 1).astype(F32)
    far = lax.axis_index("lon") // 2 % 2
    low, high = kept[: PACKED // 2], kept[PACKED // 2 :]
    sent = jnp.where(far == 0, high, low).astype(BF)
    kept = jnp.where(far == 0, low, high)
    kept = (kept + swapped(sent, 2).astype(F32)).astype(BF)
    recv = swapped(kept, 4)
    place = {cell: index for index, cell in enumerate(quartets)}
    (result,) = call(
        reordered, [((576, 192), BF)], one_hot([place[cell] for cell in natural], 576), result_q
    )
    kept, recv, result = lax.optimization_barrier((kept, recv, result))
    kept = (kept.astype(F32) + recv.astype(F32)).astype(BF)
    recv = swapped(kept, 12)
    kept, recv, row, col, corner = lax.optimization_barrier((kept, recv, row, col, corner))
    kept = (kept.astype(F32) + recv.astype(F32)).astype(BF)
    recv = swapped(kept, 16)
    (grad_fields,) = call(
        assemble,
        [((576, 192), BF)],
        gather_table(windows, back_pieces(), unrolled_from(natural)),
        grad_rolled, row, col, corner,
    )
    kept, recv, grad_fields = lax.optimization_barrier((kept, recv, grad_fields))
    kept = (kept.astype(F32) + recv.astype(F32)).astype(BF)
    kept_far = swapped(kept, 2)
    grad_bias_f, grad_bias_c = call(
        unpack,
        [((1, 6, REL, NWF, TOK), F32), ((1, 12, REL, NWC, TOK), F32)],
        bits, kept, kept_far, swapped(kept, 1), swapped(kept_far, 1),
        scalars=1,
    )
    grad_bias_f = grad_bias_f.transpose(0, 3, 1, 2, 4)
    grad_bias_c = grad_bias_c.transpose(0, 3, 1, 2, 4)
    result = result.reshape(2, LON, LAT, 192).transpose(0, 2, 1, 3)
    grad_fields = grad_fields.reshape(2, LON, LAT, 192).transpose(0, 2, 1, 3)
    return (result, grad_fields, grad_bias_f, grad_bias_c)


def solution(mesh):
    grid = P(None, "lat", "lon", None)
    table = P(None, "lat", None, None, None)
    return jax.shard_map(
        on_device,
        mesh=mesh,
        in_specs=(grid, grid, table, table, P(), P(), P(), P(), P(), P()),
        out_specs=(grid, grid, table, table),
        check_vma=False,
    )
```

```python
import math

import jax
import jax.numpy as jnp
import numpy as np
from jax import lax
from jax.experimental import pallas as pl
from jax.experimental.pallas import tpu as pltpu
from jax.sharding import PartitionSpec as P

WIN_Z = 2
WIN_LAT = 6
WIN_LON = 12
ROWS = WIN_Z * WIN_LAT
TOK = ROWS * WIN_LON
HALF = TOK // 2
REL = 2 * WIN_LON - 1
WIDE = REL * ROWS
EPS = 1e-05
MASKED = -1000000000.0
HEAD = 32
SCALE = 1.0 / math.sqrt(HEAD)
LAT = 24
LON = 12
NWF = LAT // WIN_LAT
NWC = LAT // 2 // WIN_LAT
BF = jnp.bfloat16
F32 = jnp.float32
ROW_PIECE, COL_PIECE, CORNER = 48, 288, 48
VMEM = 56 * 1024 * 1024
TABLE = 24 + 3
LANES = 384
PACKED = 24 * TABLE + 8
BATCH = 4


def natural_order():
    return [(z, i, j) for z in range(2) for j in range(LON) for i in range(LAT)]


def window_order():
    return [
        (z, WIN_LAT * w + l, n)
        for w in range(NWF)
        for n in range(LON)
        for z in range(2)
        for l in range(WIN_LAT)
    ]


def quartet_order():
    return [
        (z, 2 * (WIN_LAT * w + l) + di, 2 * n + dj)
        for di in range(2)
        for dj in range(2)
        for w in range(NWC)
        for n in range(LON // 2)
        for z in range(2)
        for l in range(WIN_LAT)
    ]


def one_hot(rows, columns):
    table = np.zeros((len(rows), columns), np.float32)
    for row, column in enumerate(rows):
        if column is not None:
            table[row, column] = 1.0
    return jnp.asarray(table, BF)


def forward_pieces():
    row = [(z, i, j) for z in range(2) for i in range(3) for j in range(6, LON)]
    col = [(z, i, j) for z in range(2) for i in range(LAT) for j in range(6)]
    corner = [(z, i, j) for z in range(2) for i in range(3) for j in range(6)]
    return row, col, corner


def back_pieces():
    row = [(z, i, j) for z in range(2) for i in range(LAT - 3, LAT) for j in range(6)]
    col = [cell for cell in window_order() if cell[2] >= 6]
    corner = [(z, i, j) for z in range(2) for i in range(LAT - 3, LAT) for j in range(6, LON)]
    return row, col, corner


def padded_pieces(pieces):
    sizes = (ROW_PIECE, COL_PIECE, CORNER)
    return [cells + [None] * (size - len(cells)) for cells, size in zip(pieces, sizes)]


def send_table(own_order, pieces):
    place = {cell: index for index, cell in enumerate(own_order)}
    cells = sum(padded_pieces(pieces), [])
    return one_hot([None if cell is None else place[cell] for cell in cells], len(own_order))


def gather_table(own_order, pieces, wanted):
    tables = [{cell: index for index, cell in enumerate(own_order)}]
    starts = [0]
    for cells in pieces:
        tables.append({cell: index for index, cell in enumerate(cells)})
    starts = [0, len(own_order), len(own_order) + ROW_PIECE, len(own_order) + ROW_PIECE + COL_PIECE]
    total = len(own_order) + ROW_PIECE + COL_PIECE + CORNER
    rows = []
    for entry in wanted:
        rows.append(None if entry is None else starts[entry[0]] + tables[entry[0]][entry[1]])
    return one_hot(rows, total)


def window_start(w):
    return (WIN_LAT * w + WIN_LAT // 2) // 8 * 8 if w < NWF - 1 else LAT - 8


def window_table():
    rows = []
    for w in range(NWF):
        offset = WIN_LAT * w + WIN_LAT // 2 - window_start(w)
        for n in range(LON):
            for z in range(2):
                for l in range(WIN_LAT):
                    rows.append(((1 - z) * LON + n) * 16 + offset + l)
    return one_hot(rows, 2 * LON * 16)


def last_window_table():
    place = {cell: index for index, cell in enumerate(window_order()[-TOK:])}
    row, _, corner = padded_pieces(back_pieces())
    return one_hot([None if cell is None else place[cell] for cell in row + corner], TOK)


def rolled_from(cells):
    wanted = []
    for z, i, j in cells:
        z, i, j = 1 - z, i + 3, j + 6
        kind = (1 if i >= LAT else 0) + (2 if j >= LON else 0)
        wanted.append((kind, (z, i % LAT, j % LON)))
    return wanted


def unrolled_from(cells):
    wanted = []
    for cell in cells:
        z, i, j = cell
        z, i, j = 1 - z, i - 3, j - 6
        kind = (1 if i < 0 else 0) + (2 if j < 0 else 0)
        wanted.append((kind, (z, i % LAT, j % LON)))
    return wanted


def dot(a, b):
    return lax.dot_general(a, b, (((1,), (0,)), ((), ())), preferred_element_type=F32)


def dot_nt(a, b):
    return lax.dot_general(a, b, (((1,), (1,)), ((), ())), preferred_element_type=F32)


def dot_tn(a, b):
    return lax.dot_general(a, b, (((0,), (0,)), ((), ())), preferred_element_type=F32)


def normalise(values, count):
    mean = jnp.sum(values, axis=-1, keepdims=True) * (1.0 / count)
    centred = values - mean
    spread = jnp.sum(centred * centred, axis=-1, keepdims=True) * (1.0 / count)
    rstd = lax.rsqrt(spread + EPS)
    return centred * rstd, rstd


def normalise_back(cotangent, normed, rstd, count):
    first = jnp.sum(cotangent, axis=-1, keepdims=True) * (1.0 / count)
    second = jnp.sum(cotangent * normed, axis=-1, keepdims=True) * (1.0 / count)
    return rstd * (cotangent - first - normed * second)


def head_stack(values, heads):
    lanes = lax.broadcasted_iota(jnp.int32, values.shape, 1) // HEAD
    return jnp.concatenate([jnp.where(lanes == h, values, 0.0) for h in range(heads)], axis=0).astype(BF)


def head_sum(stacked, heads):
    rows = stacked.shape[0] // heads
    lanes = lax.broadcasted_iota(jnp.int32, (rows, 128), 1) // HEAD
    total = stacked[:rows]
    for h in range(1, heads):
        total = jnp.where(lanes == h, stacked[h * rows : (h + 1) * rows], total)
    return jnp.where(lanes < heads, total, 0.0)


def softmax(scores, ones):
    highest = jnp.max(scores, axis=-1, keepdims=True)
    powers = jnp.exp(scores - highest)
    rounded = powers.astype(BF)
    inverse = 1.0 / dot(rounded, ones)
    weights = powers * jnp.concatenate([inverse, inverse[:, : TOK - 128]], axis=1)
    return rounded, inverse, weights.astype(BF)


def scores_back(weights, dweights, ones):
    weights32 = weights.astype(F32)
    product = weights32 * dweights
    total = dot(product.astype(BF), ones)
    return product - weights32 * jnp.concatenate([total, total[:, : TOK - 128]], axis=1)


def rotated(value, shift, axis):
    size = value.shape[axis]
    return pltpu.roll(value, shift % size, axis)


def sheared(value, index, bits, lanes):
    for bit in range(bits):
        value = jnp.where((index >> bit) & 1 == 1, rotated(value, lanes << bit, 2), value)
    return value


def strided(value):
    tiles = []
    for start in range(0, value.shape[1], 8):
        tile = pltpu.roll(value[:, start : start + 8], 0, 2, stride=ROWS, stride_axis=1)
        tiles.append(rotated(tile, ROWS * start, 2))
    return jnp.concatenate(tiles, axis=1)


def raised(value, amount, steps):
    for step in steps:
        value = jnp.where(amount & step != 0, rotated(value, step, 1), value)
    return value


def stripes_of(table, stripes_out):
    heads = table.shape[0]
    index = lax.broadcasted_iota(jnp.int32, (1, 24, LANES), 1)
    amount = (lax.broadcasted_iota(jnp.int32, (1, 8, LANES), 2) // ROWS + 10) & 31
    table = jnp.concatenate([table, jnp.zeros((heads, REL, LANES - TOK), F32)], axis=2)
    table = jnp.concatenate([table, jnp.zeros((heads, 1, LANES), F32)], axis=1)
    table = rotated(sheared(table, index, 5, -ROWS), 22 * ROWS, 2)
    tiles = [table[:, 0:8], table[:, 8:16], table[:, 16:24], jnp.zeros((heads, 8, LANES), F32)]
    tiles = [jnp.where(amount & 16 != 0, tiles[k - 2], tiles[k]) for k in range(4)]
    tiles = [jnp.where(amount & 8 != 0, tiles[k - 1], tiles[k]) for k in range(4)]
    stripes = jnp.concatenate([tiles[3], tiles[0], tiles[1]], axis=1)
    stripes = raised(stripes, amount[:, :1], (4, 2, 1))[:, 8:]
    stripes = sheared(stripes, index[:, :16], 4, -ROWS)
    stripes = jnp.where(index[:, :16] < ROWS, stripes, 0.0)
    stripes = jnp.concatenate([stripes, jnp.zeros((heads, 8, LANES), F32)], axis=1)
    stripes_out[...] = stripes + rotated(rotated(stripes, ROWS, 2), ROWS, 1)


def stripes_back(stripes):
    heads = stripes.shape[0]
    index = lax.broadcasted_iota(jnp.int32, (1, 16, LANES), 1)
    amount = (22 - lax.broadcasted_iota(jnp.int32, (1, 8, LANES), 2) // ROWS) & 31
    stripes = stripes + rotated(rotated(stripes, -ROWS, 2), ROWS, 1)
    stripes = strided(jnp.where(index < ROWS, stripes[:, :16], 0.0))
    blank = jnp.zeros((heads, 8, LANES), F32)
    stripes = raised(jnp.concatenate([stripes, blank], axis=1), amount[:, :1], (1, 2, 4))
    tiles = [stripes[:, 0:8], stripes[:, 8:16], stripes[:, 16:24], blank]
    tiles = [jnp.where(amount & 8 != 0, tiles[k - 1], tiles[k]) for k in range(4)]
    tiles = [jnp.where(amount & 16 != 0, tiles[k - 2], tiles[k]) for k in range(3)]
    return rotated(strided(jnp.concatenate(tiles, axis=1)), -22 * ROWS, 2)


def expand(table, stripes_out):
    _, heads, _, windows, _ = table.shape
    batch = BATCH if heads % BATCH == 0 else 3
    for w in range(windows):
        for start in range(0, heads, batch):
            place = stripes_out.at[heads * w + start : heads * w + start + batch]
            stripes_of(table[0, start : start + batch, :, w, :], place)


def pack(totals, packed_out, packed):
    pack_tables(totals, packed)
    packed_out[...] = packed[...].astype(BF)


def pack_tables(totals, packed):
    packed[24 * TABLE :, :] = jnp.zeros((PACKED - 24 * TABLE, 128), F32)
    rest = jnp.zeros((24, 128), F32)
    for start in range(0, 24, BATCH):
        tables = stripes_back(totals[start : start + BATCH])
        for head in range(start, start + BATCH):
            rest = pack_table(tables[head - start], head, packed, rest)


def pack_table(table, head, packed, rest):
    packed[24 * head : 24 * head + 24, :] = table[:, :128]
    rest = rest + rotated(table[:, 128:256], 16 * (head % 8), 1)
    if head % 8 == 7:
        start = 24 * (24 + head // 8)
        packed[start : start + 24, :] = rest
        rest = jnp.zeros((24, 128), F32)
    return rest


def mask_of(last_row):
    first = lax.broadcasted_iota(jnp.int32, (24, LANES), 0) % ROWS
    second = lax.broadcasted_iota(jnp.int32, (24, LANES), 1) % ROWS
    half = WIN_Z // 2
    level = (first // WIN_LAT >= WIN_Z - half) != (second // WIN_LAT >= WIN_Z - half)
    if last_row is not None:
        half = WIN_LAT // 2
        row = (first % WIN_LAT >= WIN_LAT - half) != (second % WIN_LAT >= WIN_LAT - half)
        level = level | (row & (last_row == 1))
    return jnp.where(level, MASKED, 0.0).astype(F32)


def padded_lanes(weights):
    blocks = []
    for start in range(0, weights.shape[1], 192):
        blocks += [weights[:, start : start + 192], jnp.zeros((weights.shape[0], 64), weights.dtype)]
    return jnp.concatenate(blocks, axis=1)


def cut(fields, row_out, col_out, corner_out):
    row_out[...] = fields[:, 6:, :3]
    col_out[...] = fields[:, :6]
    corner_out[...] = fields[:, :6, :3]


def fine_forward(last, gather, send, fields, row, col, corner, table, w_qkv_in, w_proj_in, x_out, qkv_out, weights_out, mixed_out, row_out, col_out, corner_out, rolled, stripes, x_s, qkv_s, weights_s, sems):
    rolled[:, :, LAT:, :] = jnp.zeros((2, LON, 8, 192), F32)
    rolled[:, :6, :LAT, :] = fields[:, 6:].astype(F32)
    rolled[:, 6:, :LAT, :] = col[...].astype(F32)
    rolled[:, :6, LAT : LAT + 3, :] = row[...].astype(F32)
    rolled[:, 6:, LAT : LAT + 3, :] = corner[...].astype(F32)
    x = []
    for w in range(NWF):
        start = window_start(w)
        sources = rolled[:, :, start : start + 16].reshape(2 * LON * 16, 192).astype(BF)
        x.append(dot(gather[TOK * w : TOK * w + TOK, :], sources))
    x = jnp.concatenate(x, axis=0)
    x_s[...] = x.astype(BF)
    copies = [pltpu.make_async_copy(x_s, x_out, sems.at[0])]
    copies[-1].start()
    normed, _ = normalise(x, 192)
    qkv_s[...] = dot(normed.astype(BF), padded_lanes(w_qkv_in[...])).astype(BF)
    copies.append(pltpu.make_async_copy(qkv_s, qkv_out, sems.at[1]))
    copies[-1].start()
    w_proj = jnp.concatenate([w_proj_in[...], jnp.zeros((64, 192), BF)], axis=0)
    ones = jnp.ones((TOK, 128), BF)
    level_mask = mask_of(None)
    last_mask = mask_of(last[0])
    sent = []
    for w in range(NWF):
        rows = pl.ds(w * TOK, TOK)
        for start in range(0, 6, 3):
            stripes_of(table[0, start : start + 3, :, w, :], stripes.at[start : start + 3])
        blended = []
        for group, heads in ((0, 4), (1, 2)):
            queries = qkv_s[rows, 128 * group : 128 * group + 128]
            keys = qkv_s[rows, 256 + 128 * group : 256 + 128 * group + 128]
            values = qkv_s[rows, 512 + 128 * group : 512 + 128 * group + 128]
            bias = []
            for h in range(heads):
                stripe = stripes[4 * group + h] + (last_mask if w == NWF - 1 else level_mask)
                bias += [rotated(stripe, -(11 - 2 * m) * ROWS, 1)[:, :TOK] for m in range(6)]
            bias = jnp.concatenate(bias, axis=0)
            queries = head_stack(queries.astype(F32), heads)
            rounded, inverse, weights = softmax(dot_nt(queries, keys) * SCALE + bias, ones)
            weights_s[w, 4 * TOK * group : 4 * TOK * group + heads * TOK, :] = weights
            blended.append(head_sum(dot(rounded, values) * inverse, heads))
        blended = jnp.concatenate(blended, axis=1).astype(BF)
        mixed = x[w * TOK : (w + 1) * TOK] + dot(blended, w_proj)
        sent.append(mixed[HALF:])
        mixed_out[rows, :] = mixed.astype(BF)
        copies.append(pltpu.make_async_copy(weights_s.at[w], weights_out.at[w], sems.at[2 + w]))
        copies[-1].start()
    col_out[...] = jnp.concatenate(sent, axis=0).astype(BF)
    pieces = dot(send[...], mixed_out[TOK * (NWF - 1) :, :]).astype(BF)
    row_out[...] = pieces[:ROW_PIECE]
    corner_out[...] = pieces[ROW_PIECE:]
    for copy in copies:
        copy.wait()


def fine_backward(bits, gather, send, own, row, col, corner, x, qkv, weights_in, w_qkv_in, w_proj_in, packed_c, own_out, row_out, col_out, corner_out, sent_out, kept_out, dqkv, packed, totals):
    sources = jnp.concatenate([own[...], row[...], col[...], corner[...]], axis=0)
    dmix = dot(gather[...], sources).astype(BF)
    w_proj = jnp.concatenate([w_proj_in[...], jnp.zeros((64, 192), BF)], axis=0)
    datt = dot_nt(dmix, w_proj).astype(BF)
    ones = jnp.ones((TOK, 128), BF)
    for w in range(NWF):
        rows = pl.ds(w * TOK, TOK)
        for group, heads in ((0, 4), (1, 2)):
            lanes = slice(128 * group, 128 * group + 128)
            queries = qkv[rows, 128 * group : 128 * group + 128]
            keys = qkv[rows, 256 + 128 * group : 256 + 128 * group + 128]
            values = qkv[rows, 512 + 128 * group : 512 + 128 * group + 128]
            grad = datt[w * TOK : (w + 1) * TOK, lanes]
            queries = head_stack(queries.astype(F32), heads)
            grad = head_stack(grad.astype(F32), heads)
            weights = weights_in[w, 4 * TOK * group : 4 * TOK * group + heads * TOK, :]
            dscores = scores_back(weights, dot_nt(grad, values), ones)
            ds = dscores.astype(BF)
            dq = head_sum(dot(ds, keys), heads)
            dk = dot_tn(ds, queries)
            dv = dot_tn(weights, grad)
            wide = jnp.concatenate([dscores, jnp.zeros((heads * TOK, LANES - TOK), F32)], axis=1)
            for h in range(heads):
                total = jnp.zeros((24, LANES), F32)
                for m in range(6):
                    block = wide[TOK * h + 24 * m : TOK * h + 24 * m + 24]
                    total = total + rotated(block, (11 - 2 * m) * ROWS, 1)
                totals[6 * w + 4 * group + h] = total
            dqkv[rows, 128 * group : 128 * group + 128] = (dq * SCALE).astype(BF)
            dqkv[rows, 256 + 128 * group : 256 + 128 * group + 128] = (dk * SCALE).astype(BF)
            dqkv[rows, 512 + 128 * group : 512 + 128 * group + 128] = dv.astype(BF)
    pack_tables(totals, packed)
    even = bits[0] == 0
    mine = packed[...].astype(BF).astype(F32)
    other = packed_c[...].astype(F32)
    sent_out[...] = jnp.where(even, mine, other).astype(BF)
    kept_out[...] = jnp.where(even, other, mine).astype(BF)
    dnormed = dot_nt(dqkv[...], padded_lanes(w_qkv_in[...])).astype(BF).astype(F32)
    normed, rstd = normalise(x[...].astype(F32), 192)
    dx = normalise_back(dnormed, normed, rstd, 192).astype(BF).astype(F32)
    grad_rolled = dmix.astype(F32) + dx
    own_out[...] = grad_rolled.astype(BF)
    sent = [grad_rolled[TOK * w + HALF : TOK * w + TOK] for w in range(NWF)]
    col_out[...] = jnp.concatenate(sent, axis=0).astype(BF)
    pieces = dot(send[...], own_out[TOK * (NWF - 1) :, :]).astype(BF)
    row_out[...] = pieces[:ROW_PIECE]
    corner_out[...] = pieces[ROW_PIECE:]


def reordered(gather, values, out):
    out[...] = dot(gather[...], values[...]).astype(BF)


def unpack(bits, kept, kept_far, other, other_far, fine_out, coarse_out):
    even, low = bits[0] == 0, bits[1] == 0
    halves = [part[...].astype(F32) for part in (kept, kept_far, other, other_far)]
    tables = []
    for near, far in (halves[:2], halves[2:]):
        tables.append(
            jnp.concatenate([jnp.where(low, near, far), jnp.where(low, far, near)], axis=0)
        )
    coarse = jnp.where(even, tables[0], tables[1])
    fine = jnp.where(even, tables[1], tables[0])
    for packed, out, heads in ((fine, fine_out, 6), (coarse, coarse_out, 12)):
        for head in range(24):
            rest = 24 * (24 + head // 8)
            rest = rotated(packed[rest : rest + 24], -16 * (head % 8), 1)[:, : TOK - 128]
            table = jnp.concatenate([packed[24 * head : 24 * head + 24], rest], axis=1)
            out[0, head % heads, :, head // heads, :] = table[:REL]


def assemble(gather, own, row, col, corner, out):
    sources = jnp.concatenate([own[...], row[...], col[...], corner[...]], axis=0)
    out[...] = dot(gather[...], sources).astype(BF)


def merge_forward(gather, own, row, col, corner, w_merge, w_qkv, fine_out, coarse_out, queries_out, pairs_out):
    sources = jnp.concatenate([own[...], row[...], col[...], corner[...]], axis=0)
    fine = dot(gather[...], sources)
    fine_out[...] = fine.astype(BF)
    quarter = [fine[TOK * d : TOK * (d + 1)] for d in range(4)]
    mean = sum(jnp.sum(q, axis=-1, keepdims=True) for q in quarter) * (1.0 / 768)
    centred = [q - mean for q in quarter]
    spread = sum(jnp.sum(c * c, axis=-1, keepdims=True) for c in centred) * (1.0 / 768)
    rstd = lax.rsqrt(spread + EPS)
    coarse = jnp.zeros((TOK, 384), F32)
    for d in range(4):
        coarse = coarse + dot((centred[d] * rstd).astype(BF), w_merge[192 * d : 192 * d + 192, :])
    coarse = coarse.astype(BF)
    coarse_out[...] = coarse
    normed, _ = normalise(coarse.astype(F32), 384)
    projected = dot(normed.astype(BF), w_qkv[...])
    queries_out[...] = projected[:, :384].astype(BF)
    pairs_out[...] = projected[:, 384:].astype(BF)


def coarse_middle(parity, queries_in, pairs_in, far_in, coarse_in, fine, upstream, stripes, w_proj, w_split, result_out, input_back_out, own_back_out, far_back_out, totals, attended, weights_ref, dattended):
    pairs = pairs_in[...].astype(F32)
    far = far_in[...].astype(F32)
    queries32 = queries_in[...].astype(F32)
    joined = []
    first = parity[0] == 0
    ones = jnp.ones((TOK, 128), BF)
    lanes = lax.broadcasted_iota(jnp.int32, (24, 128), 1)
    for w in range(NWC):
        joined.append(
            jnp.concatenate([pairs[HALF * w : HALF * w + HALF], far[HALF * w : HALF * w + HALF]], axis=0).astype(BF)
        )
    for w in range(NWC):
        for group in range(3):
            queries = queries32[HALF * w : HALF * w + HALF, 128 * group : 128 * group + 128]
            keys = joined[w][:, 128 * group : 128 * group + 128]
            values = joined[w][:, 384 + 128 * group : 384 + 128 * group + 128]
            bias = []
            for h in range(4):
                stripe = stripes[12 * w + 4 * group + h]
                near = rotated(stripe, -84, 1)[:, :128]
                other = jnp.where(first, rotated(stripe, -84, 1), rotated(stripe, 60, 1))[:, :256]
                for m in range(3):
                    offset = 48 - 24 * m
                    left = rotated(near, -offset, 1)
                    right = rotated(other, -offset, 1)[:, :TOK]
                    left = jnp.where(lanes < HALF, left, right[:, :128])
                    bias.append(jnp.concatenate([left, right[:, 128:]], axis=1))
            bias = jnp.concatenate(bias, axis=0)
            scores = dot_nt(head_stack(queries, 4), keys) * SCALE + bias
            rounded, inverse, weights = softmax(scores, ones)
            weights_ref[w, group] = weights
            total = head_sum(dot(rounded, values) * inverse, 4)
            attended[HALF * w : HALF * w + HALF, 128 * group : 128 * group + 128] = total
    coarse32 = coarse_in[...].astype(F32)
    coarse_out = (coarse32 + dot(attended[...].astype(BF), w_proj[...])).astype(BF)
    normed, rstd = normalise(coarse_out.astype(F32), 384)
    normed_b = normed.astype(BF)
    back = jnp.zeros((TOK, 384), F32)
    for d in range(4):
        part = w_split[:, 192 * d : 192 * d + 192]
        up = upstream[TOK * d : TOK * d + TOK, :]
        widened = dot(normed_b, part)
        result_out[TOK * d : TOK * d + TOK, :] = (fine[TOK * d : TOK * d + TOK, :].astype(F32) + widened).astype(BF)
        back = back + dot_nt(up, part)
    back = back.astype(BF).astype(F32)
    input_back = normalise_back(back, normed, rstd, 384).astype(BF)
    input_back_out[...] = input_back
    dattended[...] = dot_nt(input_back, w_proj[...]).astype(BF).astype(F32)
    for w in range(NWC):
        for group in range(3):
            queries = queries32[HALF * w : HALF * w + HALF, 128 * group : 128 * group + 128]
            keys = joined[w][:, 128 * group : 128 * group + 128]
            values = joined[w][:, 384 + 128 * group : 384 + 128 * group + 128]
            grad = dattended[HALF * w : HALF * w + HALF, 128 * group : 128 * group + 128]
            queries = head_stack(queries, 4)
            grad = head_stack(grad, 4)
            weights = weights_ref[w, group]
            dscores = scores_back(weights, dot_nt(grad, values), ones)
            ds = dscores.astype(BF)
            dq = head_sum(dot(ds, keys), 4)
            dk = dot_tn(ds, queries)
            dv = dot_tn(weights, grad)
            blank = jnp.zeros((24, 256 - TOK), F32)
            for h in range(4):
                near = jnp.zeros((24, 128), F32)
                other = jnp.zeros((24, 256), F32)
                for m in range(3):
                    offset = 48 - 24 * m
                    block = dscores[HALF * h + 24 * m : HALF * h + 24 * m + 24]
                    left = jnp.where(lanes < HALF, block[:, :128], 0.0)
                    right = jnp.concatenate([block[:, :128] - left, block[:, 128:], blank], axis=1)
                    near = near + rotated(left, offset, 1)
                    other = other + rotated(right, offset - HALF, 1)
                blank_lanes = jnp.zeros((24, LANES - 128), F32)
                near = rotated(jnp.concatenate([near, blank_lanes], axis=1), 84, 1)
                other = jnp.concatenate([other[:, :128], blank_lanes], axis=1)
                other = jnp.where(first, rotated(other, 156, 1), rotated(other, 12, 1))
                totals[12 * w + 4 * group + h] = near + other
            part = slice(HALF * w, HALF * w + HALF)
            cols = slice(128 * group, 128 * group + 128)
            own_back_out[part, cols] = dq * SCALE
            own_back_out[part, 384 + 128 * group : 384 + 128 * group + 128] = dk[:HALF] * SCALE
            own_back_out[part, 768 + 128 * group : 768 + 128 * group + 128] = dv[:HALF]
            far_back_out[part, cols] = (dk[HALF:] * SCALE).astype(BF)
            far_back_out[part, 384 + 128 * group : 384 + 128 * group + 128] = dv[HALF:].astype(BF)


def merge_backward(send, own_back, returned, coarse_in, input_back, fine, upstream, w_merge, w_qkv, own_out, row_out, col_out, corner_out):
    returned32 = returned[...].astype(F32)
    dq = own_back[:, :384].astype(BF)
    dkv = (own_back[:, 384:] + returned32).astype(BF)
    dnormed = dot_nt(dq, w_qkv[:, :384]) + dot_nt(dkv, w_qkv[:, 384:])
    dnormed = dnormed.astype(BF).astype(F32)
    normed, rstd = normalise(coarse_in[...].astype(F32), 384)
    dx = normalise_back(dnormed, normed, rstd, 384).astype(BF)
    dcoarse = (input_back[...].astype(F32) + dx.astype(F32)).astype(BF)
    quarter = [fine[TOK * d : TOK * (d + 1), :].astype(F32) for d in range(4)]
    mean = sum(jnp.sum(q, axis=-1, keepdims=True) for q in quarter) * (1.0 / 768)
    centred = [q - mean for q in quarter]
    spread = sum(jnp.sum(c * c, axis=-1, keepdims=True) for c in centred) * (1.0 / 768)
    rstd = lax.rsqrt(spread + EPS)
    normed = [c * rstd for c in centred]
    dmerged = [
        dot_nt(dcoarse, w_merge[192 * d : 192 * d + 192, :]).astype(BF).astype(F32) for d in range(4)
    ]
    first = sum(jnp.sum(g, axis=-1, keepdims=True) for g in dmerged) * (1.0 / 768)
    second = sum(jnp.sum(g * n, axis=-1, keepdims=True) for g, n in zip(dmerged, normed)) * (1.0 / 768)
    for d in range(4):
        dfine = (rstd * (dmerged[d] - first - normed[d] * second)).astype(BF).astype(F32)
        up = upstream[TOK * d : TOK * (d + 1), :].astype(F32)
        own_out[TOK * d : TOK * (d + 1), :] = (up + dfine).astype(BF)
    pieces = dot(send[...], own_out[...]).astype(BF)
    row_out[...] = pieces[:ROW_PIECE]
    col_out[...] = pieces[ROW_PIECE : ROW_PIECE + COL_PIECE]
    corner_out[...] = pieces[ROW_PIECE + COL_PIECE :]


def moved(value, lat, lon):
    lats, lons = lax.axis_size("lat"), lax.axis_size("lon")
    if lat == 0:
        pairs = [(source, (source + lon) % lons) for source in range(lons)]
        return lax.ppermute(value, "lon", pairs)
    if lon == 0:
        pairs = [(source, (source + lat) % lats) for source in range(lats)]
        return lax.ppermute(value, "lat", pairs)
    pairs = [
        (a * lons + b, (a + lat) % lats * lons + (b + lon) % lons)
        for a in range(lats)
        for b in range(lons)
    ]
    return lax.ppermute(value, ("lat", "lon"), pairs)


def exchanged(pieces, step):
    row, col, corner = pieces
    return moved(row, step, 0), moved(col, 0, step), moved(corner, step, step)


class Arriving:
    def __init__(self, source, target, semaphore):
        self.copy = pltpu.make_async_copy(source, target, semaphore)
        self.target = target
        self.shape = target.shape
        self.waiting = True
        self.copy.start()

    def __getitem__(self, index):
        if self.waiting:
            self.copy.wait()
            self.waiting = False
        return self.target[index]


def call(kernel, out_shapes, *operands, scratch=(), scalars=0, late=(), hbm_out=(), eager=False):
    shapes = [jax.ShapeDtypeStruct(shape, dtype) for shape, dtype in out_shapes]
    scalar, array = pl.BlockSpec(memory_space=pltpu.SMEM), pl.BlockSpec(memory_space=pltpu.VMEM)
    remote = pl.BlockSpec(memory_space=pltpu.HBM)
    count = len(operands)
    limit = VMEM // 4 if eager else VMEM
    order = [] if eager else [i for i in range(scalars, count) if i not in late] + list(late)
    landing = [pltpu.VMEM(operands[i].shape, operands[i].dtype) for i in order]
    if order:
        landing.append(pltpu.SemaphoreType.DMA((len(order),)))

    def whole(*refs):
        inputs, others = list(refs[:count]), refs[count : len(refs) - len(landing)]
        spaces = refs[len(refs) - len(landing) :]
        for k, i in enumerate(order):
            inputs[i] = Arriving(inputs[i], spaces[k], spaces[-1].at[k])
        kernel(*inputs, *others)

    return pl.pallas_call(
        whole,
        out_shape=shapes,
        in_specs=[scalar if i < scalars else remote if i in order else array for i in range(count)],
        out_specs=[remote if i in hbm_out else array for i in range(len(shapes))],
        scratch_shapes=list(scratch) + landing,
        compiler_params=pltpu.CompilerParams(vmem_limit_bytes=limit),
        name=kernel.__name__,
    )(*operands)


def swapped(value, step):
    pairs = [(source, source ^ step) for source in range(lax.axis_size("lon"))]
    return lax.ppermute(value, "lon", pairs)


def on_device(fields, upstream, bias_f, bias_c, w_qkv_f, w_proj_f, w_merge, w_qkv_c, w_proj_c, w_split):
    windows, quartets = window_order(), quartet_order()
    last = (lax.axis_index("lat") == lax.axis_size("lat") - 1).astype(jnp.int32).reshape(1)
    odd = lax.axis_index("lon") % 2
    parity = odd.astype(jnp.int32).reshape(1)

    fields = fields.transpose(0, 2, 1, 3)
    upstream = upstream.transpose(0, 2, 1, 3).reshape(576, 192)
    natural = natural_order()
    place = {cell: index for index, cell in enumerate(natural)}
    pieces = call(cut, [((2, 6, 3, 192), BF), ((2, 6, LAT, 192), BF), ((2, 6, 3, 192), BF)], fields)
    row, col, corner = exchanged(pieces, -1)
    (up,) = call(
        reordered, [((576, 192), BF)], one_hot([place[cell] for cell in quartets], 576), upstream
    )
    row, col, corner, up = lax.optimization_barrier((row, col, corner, up))
    piece_shapes = [((size, 192), BF) for size in (ROW_PIECE, COL_PIECE, CORNER)]
    x, qkv, weights, mixed, *pieces = call(
        fine_forward,
        [((576, 192), BF), ((576, 768), BF), ((NWF, 6 * TOK, TOK), BF), ((576, 192), BF)] + piece_shapes,
        last, window_table(), last_window_table(), fields, row, col, corner, bias_f.transpose(0, 2, 3, 1, 4), w_qkv_f, w_proj_f,
        scratch=[
            pltpu.VMEM((2, LON, LAT + 8, 192), F32),
            pltpu.VMEM((6, 24, LANES), F32),
            pltpu.VMEM((576, 192), BF),
            pltpu.VMEM((576, 768), BF),
            pltpu.VMEM((NWF, 6 * TOK, TOK), BF),
            pltpu.SemaphoreType.DMA((6,)),
        ],
        late=(8, 7, 9, 2),
        hbm_out=(0, 1, 2),
        scalars=1,
    )
    row, col, corner = exchanged(pieces, 1)
    (stripes_c,) = call(expand, [((24, 24, LANES), F32)], bias_c.transpose(0, 2, 3, 1, 4))
    row, col, corner, stripes_c = lax.optimization_barrier((row, col, corner, stripes_c))
    fine, coarse_in, queries, pairs = call(
        merge_forward,
        [((576, 192), BF), ((TOK, 384), BF), ((TOK, 384), BF), ((TOK, 768), BF)],
        gather_table(windows, back_pieces(), unrolled_from(quartets)),
        mixed, row, col, corner, w_merge, w_qkv_c,
        eager=True,
    )
    far = swapped(pairs, 1)
    result_q, input_back, own_back, far_back, totals_c = call(
        coarse_middle,
        [
            ((576, 192), BF),
            ((TOK, 384), BF),
            ((TOK, 1152), F32),
            ((TOK, 768), BF),
            ((24, 24, LANES), F32),
        ],
        parity, queries, pairs, far, coarse_in, fine, up, stripes_c, w_proj_c, w_split,
        scratch=[
            pltpu.VMEM((TOK, 384), F32),
            pltpu.VMEM((NWC, 3, 4 * HALF, TOK), BF),
            pltpu.VMEM((TOK, 384), F32),
        ],
        scalars=1,
        late=(4, 8, 9, 5, 6),
    )
    returned = swapped(far_back, 1)
    fine_back, *pieces = call(
        merge_backward,
        [((576, 192), BF)] + piece_shapes,
        send_table(quartets, forward_pieces()),
        own_back, returned, coarse_in, input_back, fine, up, w_merge, w_qkv_c,
        eager=True,
    )
    row, col, corner = exchanged(pieces, -1)
    (packed_c,) = call(
        pack, [((PACKED, 128), BF)], totals_c, scratch=[pltpu.VMEM((PACKED, 128), F32)]
    )
    bits = jnp.stack([odd, lax.axis_index("lon") // 2 % 2]).astype(jnp.int32)
    row, col, corner, packed_c, bits = lax.optimization_barrier((row, col, corner, packed_c, bits))
    grad_rolled, *rest = call(
        fine_backward,
        [((576, 192), BF)] + piece_shapes + [((PACKED, 128), BF)] * 2,
        bits, gather_table(quartets, forward_pieces(), rolled_from(windows)),
        last_window_table(),
        fine_back, row, col, corner, x, qkv, weights, w_qkv_f, w_proj_f, packed_c,
        scratch=[
            pltpu.VMEM((576, 768), BF),
            pltpu.VMEM((PACKED, 128), F32),
            pltpu.VMEM((24, 24, LANES), F32),
        ],
        scalars=1,
        late=(11, 8, 9, 10, 7, 2, 12),
    )
    *pieces, sent, kept = rest

    row, col, corner = exchanged(pieces, 1)
    kept = kept.astype(F32) + swapped(sent, 1).astype(F32)
    far = lax.axis_index("lon") // 2 % 2
    low, high = kept[: PACKED // 2], kept[PACKED // 2 :]
    sent = jnp.where(far == 0, high, low).astype(BF)
    kept = jnp.where(far == 0, low, high)
    kept = (kept + swapped(sent, 2).astype(F32)).astype(BF)
    recv = swapped(kept, 4)
    place = {cell: index for index, cell in enumerate(quartets)}
    (result,) = call(
        reordered, [((576, 192), BF)], one_hot([place[cell] for cell in natural], 576), result_q
    )
    kept, recv, result = lax.optimization_barrier((kept, recv, result))
    kept = (kept.astype(F32) + recv.astype(F32)).astype(BF)
    recv = swapped(kept, 12)
    kept, recv, row, col, corner = lax.optimization_barrier((kept, recv, row, col, corner))
    kept = (kept.astype(F32) + recv.astype(F32)).astype(BF)
    recv = swapped(kept, 16)
    (grad_fields,) = call(
        assemble,
        [((576, 192), BF)],
        gather_table(windows, back_pieces(), unrolled_from(natural)),
        grad_rolled, row, col, corner,
    )
    kept, recv, grad_fields = lax.optimization_barrier((kept, recv, grad_fields))
    kept = (kept.astype(F32) + recv.astype(F32)).astype(BF)
    kept_far = swapped(kept, 2)
    grad_bias_f, grad_bias_c = call(
        unpack,
        [((1, 6, REL, NWF, TOK), F32), ((1, 12, REL, NWC, TOK), F32)],
        bits, kept, kept_far, swapped(kept, 1), swapped(kept_far, 1),
        scalars=1,
        eager=True,
    )
    grad_bias_f = grad_bias_f.transpose(0, 3, 1, 2, 4)
    grad_bias_c = grad_bias_c.transpose(0, 3, 1, 2, 4)
    result = result.reshape(2, LON, LAT, 192).transpose(0, 2, 1, 3)
    grad_fields = grad_fields.reshape(2, LON, LAT, 192).transpose(0, 2, 1, 3)
    return (result, grad_fields, grad_bias_f, grad_bias_c)


def solution(mesh):
    grid = P(None, "lat", "lon", None)
    table = P(None, "lat", None, None, None)
    return jax.shard_map(
        on_device,
        mesh=mesh,
        in_specs=(grid, grid, table, table, P(), P(), P(), P(), P(), P()),
        out_specs=(grid, grid, table, table),
        check_vma=False,
    )
```
